32 devices in a mesh: row: 8 (over y, x, core), col: 4 (over z).
Axes of the slice: x: 2, y: 2, z: 4, core: 2. Of those that a mesh axis runs over, the one named last changes fastest.
Arguments:
- inputs: bfloat16 [512, 16384], P('col', 'row'), may hold values from -6 to 6
- gate_weight: bfloat16 [16384, 26624], P('row', 'col'), may hold values from -0.0625 to 0.0625
- up_weight: bfloat16 [16384, 26624], P('row', 'col'), may hold values from -0.0625 to 0.0625
- gate_pattern: int32 [128, 208], P('row', 'col'), may hold values 0 or 1
- up_pattern: int32 [128, 208], P('row', 'col'), may hold values 0 or 1
- cotangent: bfloat16 [512, 26624], P('row', 'col'), may hold values from -6 to 6
Outputs:
- hidden: bfloat16 [512, 26624], P('row', 'col')
- input_grad: bfloat16 [512, 16384], P('col', 'row')
The draws below stay inside these ranges and needn't reach their ends.
All inputs are finite; a program needn't handle non-finite values. No bound on the sum of `gate_pattern` or of `up_pattern` on one device may be relied on, other than what follows from the above.
Results may differ from the reference program's by a relative error of at most 0.039.
Values may be sent and summed in bfloat16 or wider, within the bound.
No kernel may reach another device: no remote copies, remote signals or barrier semaphores. Data moves between devices by JAX's collectives and lax.ppermute only.
A program may use at most 256 MiB of HBM per device.

```python
import jax
import jax.numpy as jnp
from jax import lax

D = 16384
FF = 26624
BLOCK = 128
TOKENS = 512
N_ROW = 8


def plant(drawn, key, low, top_value):
    dims = drawn.shape
    spot = [jax.random.randint(jax.random.fold_in(key, axis), (), 0, dims[axis]) for axis in range(len(dims))]
    drawn = drawn.at[tuple(spot)].set(low)
    longest = dims.index(max(dims))
    spot[longest] = (spot[longest] + 1) % dims[longest]
    return drawn.at[tuple(spot)].set(top_value)


def shard_levels(rng, extent, cuts, low, largest):
    gain = 1.0
    for dim, shards_of in cuts:
        steps = jax.random.uniform(jax.random.fold_in(jax.random.fold_in(rng, 6), dim), (shards_of,), jnp.float32, low / len(cuts), largest / len(cuts))
        gain = gain * jnp.repeat(jnp.exp(steps), extent[dim] // shards_of).reshape((-1,) + (1,) * (len(extent) - 1 - dim))
    return gain


def scatter_about(key, dims, scale, bound, pieces=(), held_as=jnp.bfloat16):
    gain = shard_levels(key, dims, pieces, -0.22, 0.18) if pieces else 1.0
    entries = jax.random.normal(key, dims, jnp.float32) * scale * gain
    return jnp.minimum(jnp.maximum(entries, -bound), bound).astype(held_as)


def setup_inputs(seed: int = 0) -> dict:
    arg_keys = jax.random.split(jax.random.key(seed), 7)
    inputs = scatter_about(arg_keys[0], (TOKENS, D), 1.0, 6.0, ((0, 4), (1, 8)))
    gate_weight = scatter_about(arg_keys[1], (D, FF), (D // 2) ** -0.5, 0.0625, ((0, 8), (1, 4)))
    up_weight = scatter_about(arg_keys[2], (D, FF), (D // 2) ** -0.5, 0.0625, ((0, 8), (1, 4)))
    gate_pattern = plant((jax.random.randint(arg_keys[3], (D // BLOCK, FF // BLOCK), 0, 2) < 1).astype(jnp.int32), jax.random.fold_in(arg_keys[3], 1), 0, 1)
    up_pattern = plant((jax.random.randint(arg_keys[4], (D // BLOCK, FF // BLOCK), 0, 2) < 1).astype(jnp.int32), jax.random.fold_in(arg_keys[4], 1), 0, 1)
    cotangent = scatter_about(arg_keys[5], (TOKENS, FF), 1.0, 6.0, ((0, 8), (1, 4)))
    return {"inputs": inputs, "gate_weight": gate_weight, "up_weight": up_weight, "gate_pattern": gate_pattern, "up_pattern": up_pattern, "cotangent": cotangent}


def expand(weight, pattern):
    height, breadth = weight.shape
    flags = pattern.astype(weight.dtype)
    tiles = weight.reshape(height // BLOCK, BLOCK, breadth // BLOCK, BLOCK) * flags[:, None, :, None]
    return tiles.reshape(height, breadth)


def reference(inputs, gate_weight, up_weight, gate_pattern, up_pattern, cotangent):
    width = D // N_ROW
    tiles = width // BLOCK

    def block_weights(block_index):
        start = (block_index * width).astype(jnp.int32)
        tile_start = (block_index * tiles).astype(jnp.int32)
        gate_block = expand(lax.dynamic_slice_in_dim(gate_weight, start, width, 0), lax.dynamic_slice_in_dim(gate_pattern, tile_start, tiles, 0))
        up_block = expand(lax.dynamic_slice_in_dim(up_weight, start, width, 0), lax.dynamic_slice_in_dim(up_pattern, tile_start, tiles, 0))
        return start, gate_block, up_block

    def forward(block_index, carry):
        gate_sum, up_sum = carry
        start, gate_block, up_block = block_weights(block_index)
        columns = lax.dynamic_slice_in_dim(inputs, start, width, 1)
        part_gate = jnp.dot(columns, gate_block, preferred_element_type=jnp.float32).astype(jnp.bfloat16)
        part_up = jnp.dot(columns, up_block, preferred_element_type=jnp.float32).astype(jnp.bfloat16)
        part_gate, part_up = lax.optimization_barrier((part_gate, part_up))
        return gate_sum + part_gate.astype(jnp.float32), up_sum + part_up.astype(jnp.float32)

    empty = jnp.zeros((TOKENS, FF), jnp.float32)
    gate_sum, up_sum = lax.fori_loop(0, N_ROW, forward, (empty, empty))
    sigmoid_gate = jax.nn.sigmoid(gate_sum)
    activated = gate_sum * sigmoid_gate
    hidden = (activated * up_sum).astype(jnp.bfloat16)
    cotangent_f = cotangent.astype(jnp.float32)
    gate_grad = (cotangent_f * up_sum * sigmoid_gate * (1.0 + gate_sum * (1.0 - sigmoid_gate))).astype(jnp.bfloat16)
    up_grad = (cotangent_f * activated).astype(jnp.bfloat16)
    contract = (((1,), (1,)), ((), ()))

    def backward(block_index, result):
        start, gate_block, up_block = block_weights(block_index)
        piece = lax.dot_general(gate_grad, gate_block, contract, preferred_element_type=jnp.float32)
        piece = piece + lax.dot_general(up_grad, up_block, contract, preferred_element_type=jnp.float32)
        return lax.dynamic_update_slice_in_dim(result, piece, start, 1)

    input_grad = lax.fori_loop(0, N_ROW, backward, jnp.zeros((TOKENS, D), jnp.float32))
    return hidden, input_grad.astype(jnp.bfloat16)
```

```python
import functools

import jax
import jax.numpy as jnp
from jax import lax
from jax.experimental import pallas as pl
from jax.experimental.pallas import tpu as pltpu
from jax.sharding import PartitionSpec as P

BLOCK = 128
TOKEN_CHUNKS = 2
HIDDEN_CHUNKS = 2
VMEM_BYTES = 48 * 1024 * 1024


def masked(w_ref, f_ref):
    return jnp.concatenate(
        [
            w_ref[k * BLOCK : (k + 1) * BLOCK, :] * f_ref[k : k + 1, :]
            for k in range(w_ref.shape[0] // BLOCK)
        ],
        axis=0,
    )


def forward_kernel(x_ref, wg_ref, wu_ref, fg_ref, fu_ref, og_ref, ou_ref):
    for w_ref, f_ref, o_ref in ((wg_ref, fg_ref, og_ref), (wu_ref, fu_ref, ou_ref)):
        o_ref[...] = jnp.dot(
            x_ref[...], masked(w_ref, f_ref), preferred_element_type=jnp.float32
        ).astype(jnp.bfloat16)


def forward(x, weights, flags, first, tiles, tile):
    rows, depth = x.shape
    blocks = flags[0].shape[0]
    w_spec = pl.BlockSpec((depth, tile), lambda i: (0, first + i))
    f_spec = pl.BlockSpec((blocks, tile), lambda i: (0, first + i))
    o_spec = pl.BlockSpec((rows, tile), lambda i: (0, i))
    out = jax.ShapeDtypeStruct((rows, tiles * tile), jnp.bfloat16)
    return pl.pallas_call(
        forward_kernel,
        grid=(tiles,),
        in_specs=[pl.BlockSpec((rows, depth), lambda i: (0, 0)), w_spec, w_spec, f_spec, f_spec],
        out_specs=[o_spec, o_spec],
        out_shape=[out, out],
        compiler_params=pltpu.CompilerParams(vmem_limit_bytes=VMEM_BYTES),
        cost_estimate=pl.CostEstimate(
            flops=4 * rows * depth * tiles * tile,
            bytes_accessed=4 * tiles * tile * (depth + rows) + 2 * rows * depth,
            transcendentals=0,
        ),
    )(x, *weights, *flags)


def backward_kernel(steps, last, a_ref, gg_ref, gu_ref, wg_ref, wu_ref, fg_ref, fu_ref, o_ref, acc):
    i = pl.program_id(0)
    contract = (((1,), (1,)), ((), ()))

    @pl.when(i == 0)
    def _():
        if a_ref is None:
            acc[...] = jnp.zeros_like(acc)
        else:
            acc[...] = a_ref[...]

    for g_ref, w_ref, f_ref in ((gg_ref, wg_ref, fg_ref), (gu_ref, wu_ref, fu_ref)):
        acc[...] += lax.dot_general(
            g_ref[...], masked(w_ref, f_ref), contract, preferred_element_type=jnp.float32
        )

    @pl.when(i == steps - 1)
    def _():
        o_ref[...] = acc[...].astype(o_ref.dtype)


def backward(carry, grads, weights, flags, first, tiles, tile, last):
    rows = grads[0].shape[0]
    blocks, _ = flags[0].shape
    depth = weights[0].shape[0]
    whole = pl.BlockSpec((rows, depth), lambda i: (0, 0))
    w_spec = pl.BlockSpec((depth, tile), lambda i: (0, first + i))
    f_spec = pl.BlockSpec((blocks, tile), lambda i: (0, first + i))
    g_spec = pl.BlockSpec((rows, tile), lambda i: (0, i))
    kernel = functools.partial(backward_kernel, tiles, last)
    if carry is None:
        kernel = functools.partial(backward_kernel, tiles, last, None)
    return pl.pallas_call(
        kernel,
        grid=(tiles,),
        in_specs=([] if carry is None else [whole])
        + [g_spec, g_spec, w_spec, w_spec, f_spec, f_spec],
        out_specs=whole,
        out_shape=jax.ShapeDtypeStruct((rows, depth), jnp.bfloat16 if last else jnp.float32),
        scratch_shapes=[pltpu.VMEM((rows, depth), jnp.float32)],
        compiler_params=pltpu.CompilerParams(vmem_limit_bytes=VMEM_BYTES),
        cost_estimate=pl.CostEstimate(
            flops=4 * rows * depth * tiles * tile,
            bytes_accessed=4 * tiles * tile * (depth + rows) + 2 * rows * depth,
            transcendentals=0,
        ),
    )(*(() if carry is None else (carry,)), *grads, *weights, *flags)


def derivatives(gate_sum, up_sum, cotangent):
    gate_sum = gate_sum.astype(jnp.float32)
    up_sum = up_sum.astype(jnp.float32)
    sigmoid_gate = jax.nn.sigmoid(gate_sum)
    activated = gate_sum * sigmoid_gate
    hidden = (activated * up_sum).astype(jnp.bfloat16)
    cotangent_f = cotangent.astype(jnp.float32)
    gate_grad = (
        cotangent_f * up_sum * sigmoid_gate * (1.0 + gate_sum * (1.0 - sigmoid_gate))
    ).astype(jnp.bfloat16)
    up_grad = (cotangent_f * activated).astype(jnp.bfloat16)
    return hidden, gate_grad, up_grad


def shards(inputs, gate_weight, up_weight, gate_pattern, up_pattern, cotangent):
    depth, local_hidden = gate_weight.shape
    share = cotangent.shape[0]
    piece = share // TOKEN_CHUNKS
    tile = 512 if local_hidden % 512 == 0 else 256
    n_tiles = local_hidden // tile
    bounds = [n_tiles * c // HIDDEN_CHUNKS for c in range(HIDDEN_CHUNKS + 1)]
    weights = (gate_weight, up_weight)
    flags = tuple(
        jnp.repeat(p.astype(jnp.bfloat16), BLOCK, axis=1) for p in (gate_pattern, up_pattern)
    )

    by_chunk = inputs.reshape(-1, TOKEN_CHUNKS, piece, depth)
    xs = [
        lax.all_gather(by_chunk[:, t].reshape(-1, depth), "col", axis=0, tiled=True)
        for t in range(TOKEN_CHUNKS)
    ]
    sums = {}
    for t in range(TOKEN_CHUNKS):
        for c in range(HIDDEN_CHUNKS):
            parts = forward(
                xs[t], weights, flags, bounds[c], bounds[c + 1] - bounds[c], tile
            )
            sums[t, c] = [
                lax.psum_scatter(p, "row", scatter_dimension=0, tiled=True) for p in parts
            ]
    hidden, input_grad = [], []
    for t in range(TOKEN_CHUNKS):
        rows = slice(t * piece, (t + 1) * piece)
        hidden_row = []
        carry = None
        for c in range(HIDDEN_CHUNKS):
            columns = slice(bounds[c] * tile, bounds[c + 1] * tile)
            h, gate_grad, up_grad = derivatives(*sums[t, c], cotangent[rows, columns])
            hidden_row.append(h)
            grads = [
                lax.all_gather(g, "row", axis=0, tiled=True) for g in (gate_grad, up_grad)
            ]
            carry = backward(
                carry,
                grads,
                weights,
                flags,
                bounds[c],
                bounds[c + 1] - bounds[c],
                tile,
                c == HIDDEN_CHUNKS - 1,
            )
        hidden.append(jnp.concatenate(hidden_row, axis=1))
        summed = lax.psum_scatter(carry, "col", scatter_dimension=0, tiled=True)
        input_grad.append(summed.reshape(-1, 1, piece, depth))
    return (
        jnp.concatenate(hidden, axis=0),
        jnp.concatenate(input_grad, axis=1).reshape(-1, depth),
    )


def solution(mesh):
    placed = (
        P("col", "row"),
        P("row", "col"),
        P("row", "col"),
        P("row", "col"),
        P("row", "col"),
        P("row", "col"),
    )
    return jax.shard_map(
        shards,
        mesh=mesh,
        in_specs=placed,
        out_specs=(P("row", "col"), P("col", "row")),
        check_vma=False,
    )
```

```python
import functools

import jax
import jax.numpy as jnp
import numpy as np
from jax import lax
from jax.experimental import pallas as pl
from jax.experimental.pallas import tpu as pltpu
from jax.sharding import PartitionSpec as P

BLOCK = 128
TOKEN_CHUNKS = 2
FORWARD_CHUNKS = 4
GROUP = 2
VMEM_BYTES = 48 * 1024 * 1024
ANY = pl.BlockSpec(memory_space=pl.ANY)


def masked(w_ref, f_ref):
    return jnp.concatenate(
        [
            w_ref[k * BLOCK : (k + 1) * BLOCK, :] * f_ref[k : k + 1, :]
            for k in range(w_ref.shape[0] // BLOCK)
        ],
        axis=0,
    )


class Cube:
    def __init__(self, size):
        self.size = size
        self.half = size // 2
        rising = [1 << b for b in range(1, size.bit_length() - 1)]
        self.dims = (rising, rising[::-1])

    def offset(self, parity, slot):
        dims = self.dims[parity]
        digits = [slot >> (len(dims) - 1 - i) & 1 for i in range(len(dims))]
        return int(np.bitwise_xor.reduce([0] + [d for d, on in zip(dims, digits) if on]))

    def owner(self, me, slot):
        if slot >= self.half:
            me, slot = me ^ 1, slot - self.half
        return me ^ self.offset(me & 1, slot)

    def step(self, array, i):
        perm = [(r, r ^ self.dims[r & 1][i]) for r in range(self.size)]
        return lax.ppermute(array, "row", perm)

    def sibling(self, array):
        return lax.ppermute(array, "row", [(r, r ^ 1) for r in range(self.size)])


def places(cube, n_col):
    ratio = cube.size // n_col
    table = np.zeros((cube.size, n_col, cube.size), np.int32)
    for me in range(cube.size):
        for z in range(n_col):
            for slot in range(cube.size):
                d = cube.owner(me, slot)
                table[me, z, slot] = ratio * ((d // ratio) ^ z) + d % ratio
    return table


def forward_kernel(n_x, slots, *refs):
    x_refs = refs[:n_x]
    wg_ref, wu_ref, fg_ref, fu_ref, keep_ref, send_ref, x_all, sem = refs[n_x:]
    half = keep_ref.shape[1]
    shares = slots.shape[0]
    share = 2 * half // shares
    ratio = shares // n_x

    @pl.when(pl.program_id(0) == 0)
    def _():
        copies = []
        for k in range(n_x):
            for c in range(ratio):
                place = k * ratio + c
                row = pl.multiple_of(slots[place] * share, share)
                copies.append(
                    pltpu.make_async_copy(
                        x_refs[k].at[pl.ds(c * share, share), :],
                        x_all.at[pl.ds(row, share), :],
                        sem.at[place],
                    )
                )
        for copy in copies:
            copy.start()
        for copy in copies:
            copy.wait()

    for n, (w_ref, f_ref) in enumerate(((wg_ref, fg_ref), (wu_ref, fu_ref))):
        out = jnp.dot(
            x_all[...], masked(w_ref, f_ref), preferred_element_type=jnp.float32
        ).astype(jnp.bfloat16)
        keep_ref[n] = out[:half]
        send_ref[n] = out[half:]


def forward(slots, xs, weights, flags, first, tiles, tile):
    depth = xs[0].shape[1]
    rows = len(xs) * xs[0].shape[0]
    blocks = flags[0].shape[0]
    w_spec = pl.BlockSpec((depth, tile), lambda i, s: (0, first + i))
    f_spec = pl.BlockSpec((blocks, tile), lambda i, s: (0, first + i))
    o_spec = pl.BlockSpec((2, rows // 2, tile), lambda i, s: (0, 0, i))
    out = jax.ShapeDtypeStruct((2, rows // 2, tiles * tile), jnp.bfloat16)
    return pl.pallas_call(
        functools.partial(forward_kernel, len(xs)),
        grid_spec=pltpu.PrefetchScalarGridSpec(
            num_scalar_prefetch=1,
            grid=(tiles,),
            in_specs=[ANY] * len(xs) + [w_spec, w_spec, f_spec, f_spec],
            out_specs=[o_spec, o_spec],
            scratch_shapes=[
                pltpu.VMEM((rows, depth), jnp.bfloat16),
                pltpu.SemaphoreType.DMA((slots.shape[0],)),
            ],
        ),
        out_shape=[out, out],
        compiler_params=pltpu.CompilerParams(vmem_limit_bytes=VMEM_BYTES),
        cost_estimate=pl.CostEstimate(
            flops=4 * rows * depth * tiles * tile,
            bytes_accessed=4 * tiles * tile * (depth + rows) + 2 * rows * depth,
            transcendentals=0,
        ),
    )(slots, *xs, *weights, *flags)


def backward_kernel(n_g, n_out, steps, chained, where, *refs):
    g_refs, refs = refs[:n_g], refs[n_g:]
    wg_ref, wu_ref, fg_ref, fu_ref = refs[:4]
    refs = refs[4:]
    if chained:
        carry_ref, refs = refs[0], refs[1:]
    o_refs = refs[:n_out]
    g_all, acc, sem = refs[n_out:]
    i = pl.program_id(0)
    tile = wg_ref.shape[1]
    share = g_refs[0].shape[1]

    @pl.when(i == 0)
    def _():
        copies = []
        for slot in range(n_g):
            row = pl.multiple_of(where[slot] * share, share)
            copies.append(
                pltpu.make_async_copy(
                    g_refs[slot], g_all.at[:, pl.ds(row, share), :], sem.at[slot]
                )
            )
        for copy in copies:
            copy.start()
        if chained:
            acc[...] = carry_ref[...]
        else:
            acc[...] = jnp.zeros_like(acc)
        for copy in copies:
            copy.wait()

    columns = pl.ds(pl.multiple_of(i * tile, tile), tile)
    for n, (w_ref, f_ref) in enumerate(((wg_ref, fg_ref), (wu_ref, fu_ref))):
        acc[...] += lax.dot_general(
            masked(w_ref, f_ref),
            g_all[n, :, columns],
            (((1,), (1,)), ((), ())),
            preferred_element_type=jnp.float32,
        )

    @pl.when(i == steps - 1)
    def _():
        if n_out == 1:
            o_refs[0][...] = acc[...]
        else:
            out = acc[...].T.astype(jnp.bfloat16)
            rows = out.shape[0] // n_out
            for k in range(n_out):
                o_refs[k][...] = out[k * rows : (k + 1) * rows]


def backward(carry, where, pieces, weights, flags, first, tiles, tile, planes):
    share = pieces[0].shape[1]
    rows = share * len(pieces)
    blocks = flags[0].shape[0]
    depth = weights[0].shape[0]
    w_spec = pl.BlockSpec((depth, tile), lambda i, s: (0, first + i))
    f_spec = pl.BlockSpec((blocks, tile), lambda i, s: (0, first + i))
    whole = pl.BlockSpec((depth, rows), lambda i, s: (0, 0))
    if planes:
        out_specs = [pl.BlockSpec((rows // planes, depth), lambda i, s: (0, 0))] * planes
        out_shape = [jax.ShapeDtypeStruct((rows // planes, depth), jnp.bfloat16)] * planes
    else:
        out_specs = [whole]
        out_shape = [jax.ShapeDtypeStruct((depth, rows), jnp.float32)]
    chained = carry is not None
    return pl.pallas_call(
        functools.partial(backward_kernel, len(pieces), len(out_shape), tiles, chained),
        grid_spec=pltpu.PrefetchScalarGridSpec(
            num_scalar_prefetch=1,
            grid=(tiles,),
            in_specs=[ANY] * len(pieces)
            + [w_spec, w_spec, f_spec, f_spec]
            + [whole] * chained,
            out_specs=out_specs,
            scratch_shapes=[
                pltpu.VMEM((2, rows, tiles * tile), jnp.bfloat16),
                pltpu.VMEM((depth, rows), jnp.float32),
                pltpu.SemaphoreType.DMA((len(pieces),)),
            ],
        ),
        out_shape=out_shape,
        compiler_params=pltpu.CompilerParams(vmem_limit_bytes=VMEM_BYTES),
        cost_estimate=pl.CostEstimate(
            flops=4 * rows * depth * tiles * tile,
            bytes_accessed=4 * tiles * tile * (depth + rows) + 2 * rows * depth,
            transcendentals=0,
        ),
    )(where, *pieces, *weights, *flags, *((carry,) if chained else ()))


def wide(array):
    return array.astype(jnp.float32)


def reduce_scatter(cube, keep, send):
    terms = [keep, cube.sibling(send)]
    rows = keep.shape[1]
    for i in range(len(cube.dims[0])):
        rows //= 2
        moved = sum(wide(t[:, rows : 2 * rows]) for t in terms).astype(jnp.bfloat16)
        terms = [t[:, :rows] for t in terms] + [cube.step(moved, i)]
    return sum(wide(t) for t in terms)


def all_gather(cube, own):
    n_dims = len(cube.dims[0])
    pieces = [own]
    for slot in range(1, cube.half):
        low = slot & -slot
        pieces.append(cube.step(pieces[slot ^ low], n_dims - low.bit_length()))
    return pieces + [cube.sibling(p) for p in pieces]


def flip(array, bit, size):
    return lax.ppermute(array, "col", [(z, z ^ bit) for z in range(size)])


def derivatives(gate_sum, up_sum, cotangent):
    sigmoid_gate = jax.nn.sigmoid(gate_sum)
    activated = gate_sum * sigmoid_gate
    hidden = (activated * up_sum).astype(jnp.bfloat16)
    cotangent_f = wide(cotangent)
    gate_grad = (
        cotangent_f * up_sum * sigmoid_gate * (1.0 + gate_sum * (1.0 - sigmoid_gate))
    ).astype(jnp.bfloat16)
    up_grad = (cotangent_f * activated).astype(jnp.bfloat16)
    return hidden, gate_grad, up_grad


def shards(cube, n_col, inputs, gate_weight, up_weight, gate_pattern, up_pattern, cotangent):
    depth, local_hidden = gate_weight.shape
    share = cotangent.shape[0]
    piece = share // TOKEN_CHUNKS
    tile = 512 if local_hidden % 512 == 0 else 256
    n_tiles = local_hidden // tile
    bounds = [n_tiles * c // FORWARD_CHUNKS for c in range(FORWARD_CHUNKS + 1)]
    weights = (gate_weight, up_weight)
    flags = tuple(
        jnp.repeat(p.astype(jnp.bfloat16), BLOCK, axis=1) for p in (gate_pattern, up_pattern)
    )
    table = places(cube, n_col)
    row, col = lax.axis_index("row"), lax.axis_index("col")
    where = jnp.asarray(table)[row, col]
    slots = jnp.asarray(np.argsort(table, axis=-1).astype(np.int32))[row, col]

    xs = [inputs]
    for k in range(1, n_col):
        low = k & -k
        xs.append(flip(xs[k ^ low], low, n_col))

    sums = []
    for c in range(FORWARD_CHUNKS):
        keep, send = forward(
            slots, xs, weights, flags, bounds[c], bounds[c + 1] - bounds[c], tile
        )
        sums.append(reduce_scatter(cube, keep, send))

    hidden, input_grad = [], []
    for t in range(TOKEN_CHUNKS):
        rows = slice(t * piece, (t + 1) * piece)
        hidden_row = []
        carry = None
        for c in range(0, FORWARD_CHUNKS, GROUP):
            last = c + GROUP == FORWARD_CHUNKS
            results = [
                derivatives(
                    sums[b][0, rows],
                    sums[b][1, rows],
                    cotangent[rows, bounds[b] * tile : bounds[b + 1] * tile],
                )
                for b in range(c, c + GROUP)
            ]
            hidden_row += [r[0] for r in results]
            own = jnp.stack(
                [jnp.concatenate([r[n] for r in results], axis=1) for n in (1, 2)]
            )
            parts = backward(
                carry,
                where,
                all_gather(cube, own),
                weights,
                flags,
                bounds[c],
                bounds[c + GROUP] - bounds[c],
                tile,
                n_col if last else 0,
            )
            carry = parts[0]
        hidden.append(jnp.concatenate(hidden_row, axis=1))
        parts = list(parts)
        for k in range(n_col - 1, 0, -1):
            low = k & -k
            moved = flip(parts[k].astype(jnp.bfloat16), low, n_col)
            parts[k ^ low] = wide(parts[k ^ low]) + wide(moved)
        input_grad.append(parts[0].astype(jnp.bfloat16).reshape(-1, 1, piece, depth))
    return (
        jnp.concatenate(hidden, axis=0),
        jnp.concatenate(input_grad, axis=1).reshape(-1, depth),
    )


def solution(mesh):
    placed = (
        P("col", "row"),
        P("row", "col"),
        P("row", "col"),
        P("row", "col"),
        P("row", "col"),
        P("row", "col"),
    )
    return jax.shard_map(
        functools.partial(shards, Cube(mesh.shape["row"]), mesh.shape["col"]),
        mesh=mesh,
        in_specs=placed,
        out_specs=(P("row", "col"), P("col", "row")),
        check_vma=False,
    )
```

```python
import functools

import jax
import jax.numpy as jnp
import numpy as np
from jax import lax
from jax.experimental import pallas as pl
from jax.experimental.pallas import tpu as pltpu
from jax.sharding import PartitionSpec as P

BLOCK = 128
PARTS = ((2, 4, 7), (6, 4, 3))
VMEM_BYTES = 48 * 1024 * 1024
ANY = pl.BlockSpec(memory_space=pl.ANY)


def masked(w_ref, f_ref):
    return jnp.concatenate(
        [
            w_ref[k * BLOCK : (k + 1) * BLOCK, :] * f_ref[k : k + 1, :]
            for k in range(w_ref.shape[0] // BLOCK)
        ],
        axis=0,
    )


class Cube:
    def __init__(self, size):
        self.size = size
        self.half = size // 2
        rising = [1 << b for b in range(1, size.bit_length() - 1)]
        self.dims = (rising, rising[::-1])

    def offset(self, parity, slot):
        dims = self.dims[parity]
        digits = [slot >> (len(dims) - 1 - i) & 1 for i in range(len(dims))]
        return int(np.bitwise_xor.reduce([0] + [d for d, on in zip(dims, digits) if on]))

    def owner(self, me, slot):
        if slot >= self.half:
            me, slot = me ^ 1, slot - self.half
        return me ^ self.offset(me & 1, slot)

    def step(self, array, i):
        perm = [(r, r ^ self.dims[r & 1][i]) for r in range(self.size)]
        return lax.ppermute(array, "row", perm)

    def sibling(self, array):
        return lax.ppermute(array, "row", [(r, r ^ 1) for r in range(self.size)])


def places(cube, n_col):
    ratio = cube.size // n_col
    table = np.zeros((cube.size, n_col, cube.size), np.int32)
    for me in range(cube.size):
        for z in range(n_col):
            for slot in range(cube.size):
                d = cube.owner(me, slot)
                table[me, z, slot] = ratio * ((d // ratio) ^ z) + d % ratio
    return table


def copy_all(copies):
    for copy in copies:
        copy.start()
    for copy in copies:
        copy.wait()


def cut_kernel(part, share, x_ref, *refs):
    out_ref, sem = refs[-2:]
    piece = share * out_ref.shape[0] // x_ref.shape[0]
    copy_all(
        [
            pltpu.make_async_copy(
                x_ref.at[pl.ds(c * share + part * piece, piece), :],
                out_ref.at[pl.ds(c * piece, piece), :],
                sem.at[c],
            )
            for c in range(x_ref.shape[0] // share)
        ]
    )


def cut(x, part, share, after):
    rows, depth = x.shape
    return pl.pallas_call(
        functools.partial(cut_kernel, part, share),
        in_specs=[ANY] * (1 + len(after)),
        out_specs=ANY,
        out_shape=jax.ShapeDtypeStruct((rows // len(PARTS), depth), x.dtype),
        scratch_shapes=[pltpu.SemaphoreType.DMA((rows // share,))],
    )(x, *after)


def forward_kernel(n_x, n_skip, masking, slots, *refs):
    x_refs, refs = refs[:n_x], refs[n_x:]
    if masking:
        wg_ref, wu_ref, fg_ref, fu_ref = refs[:4]
        refs = refs[4 + n_skip :]
        keep_ref, send_ref, mg_ref, mu_ref, x_all, sem = refs
    else:
        mg_ref, mu_ref = refs[:2]
        keep_ref, send_ref, x_all, sem = refs[2 + n_skip :]
    half = keep_ref.shape[1]
    shares = slots.shape[0]
    share = 2 * half // shares
    ratio = shares // n_x

    @pl.when(pl.program_id(0) == 0)
    def _():
        copies = []
        for k in range(n_x):
            for c in range(ratio):
                place = k * ratio + c
                row = pl.multiple_of(slots[place] * share, share)
                copies.append(
                    pltpu.make_async_copy(
                        x_refs[k].at[pl.ds(c * share, share), :],
                        x_all.at[pl.ds(row, share), :],
                        sem.at[place],
                    )
                )
        copy_all(copies)

    if masking:
        mg_ref[...] = masked(wg_ref, fg_ref)
        mu_ref[...] = masked(wu_ref, fu_ref)
    for n, m_ref in enumerate((mg_ref, mu_ref)):
        out = jnp.dot(x_all[...], m_ref[...], preferred_element_type=jnp.float32)
        out = out.astype(jnp.bfloat16)
        keep_ref[n] = out[:half]
        send_ref[n] = out[half:]


def forward(slots, xs, weights, flags, ready, first, tiles, tile, after):
    depth = weights[0].shape[0]
    rows = len(xs) * xs[0].shape[0]
    w_spec = pl.BlockSpec((depth, tile), lambda i, s: (0, first + i))
    o_spec = pl.BlockSpec((2, rows // 2, tile), lambda i, s: (0, 0, i))
    out = jax.ShapeDtypeStruct((2, rows // 2, tiles * tile), jnp.bfloat16)
    out_specs, out_shape = [o_spec, o_spec], [out, out]
    operands, in_specs, aliases = [slots, *xs, *weights], [ANY] * len(xs) + [w_spec] * 2, {}
    masking = flags is not None
    if masking:
        f_spec = pl.BlockSpec((flags[0].shape[0], tile), lambda i, s: (0, first + i))
        operands += flags
        in_specs += [f_spec] * 2
        out_specs += [w_spec] * 2
        out_shape += [jax.ShapeDtypeStruct(w.shape, w.dtype) for w in weights]
        if ready:
            aliases = {len(operands): 2, len(operands) + 1: 3}
    skipped = [*ready, *after]
    return pl.pallas_call(
        functools.partial(forward_kernel, len(xs), len(skipped), masking),
        grid_spec=pltpu.PrefetchScalarGridSpec(
            num_scalar_prefetch=1,
            grid=(tiles,),
            in_specs=in_specs + [ANY] * len(skipped),
            out_specs=out_specs,
            scratch_shapes=[
                pltpu.VMEM((rows, depth), jnp.bfloat16),
                pltpu.SemaphoreType.DMA((slots.shape[0],)),
            ],
        ),
        out_shape=out_shape,
        input_output_aliases=aliases,
        compiler_params=pltpu.CompilerParams(vmem_limit_bytes=VMEM_BYTES),
        cost_estimate=pl.CostEstimate(
            flops=4 * rows * depth * tiles * tile,
            bytes_accessed=4 * tiles * tile * (depth * (1 + masking) + rows) + 2 * rows * depth,
            transcendentals=0,
        ),
    )(*operands, *skipped)


def derivatives_kernel(part, first, n_terms, *refs):
    terms = refs[:n_terms]
    cot_ref = refs[n_terms]
    h_ref, g_ref = refs[-5 - n_terms : -3 - n_terms]
    held = refs[-3 - n_terms : -3]
    cot, sem, _ = refs[-3:]
    piece, columns = h_ref.shape
    copies = [
        pltpu.make_async_copy(t.at[:, pl.ds(0, piece), :], v, sem.at[n])
        for n, (t, v) in enumerate(zip(terms, held))
    ]
    copies.append(
        pltpu.make_async_copy(
            cot_ref.at[pl.ds(part * piece, piece), pl.ds(first, columns)],
            cot,
            sem.at[n_terms],
        )
    )
    copy_all(copies)
    step = 256
    for c in range(0, columns, step):
        at = slice(c, c + step)
        gate_sum = sum(wide(v[0, :, at]) for v in held)
        up_sum = sum(wide(v[1, :, at]) for v in held)
        cotangent = wide(cot[:, at])
        sigmoid_gate = jax.nn.sigmoid(gate_sum)
        activated = gate_sum * sigmoid_gate
        h_ref[:, at] = (activated * up_sum).astype(jnp.bfloat16)
        g_ref[0, :, at] = (
            cotangent * up_sum * sigmoid_gate * (1.0 + gate_sum * (1.0 - sigmoid_gate))
        ).astype(jnp.bfloat16)
        g_ref[1, :, at] = (cotangent * activated).astype(jnp.bfloat16)


def derivatives(terms, cotangent, part, piece, first, columns, after):
    held = pltpu.VMEM((2, piece, columns), jnp.bfloat16)
    return pl.pallas_call(
        functools.partial(derivatives_kernel, part, first, len(terms)),
        in_specs=[ANY] * (len(terms) + 1 + len(after)),
        out_specs=[pl.BlockSpec(memory_space=pltpu.VMEM)] * 2,
        out_shape=[
            jax.ShapeDtypeStruct((piece, columns), jnp.bfloat16),
            jax.ShapeDtypeStruct((2, piece, columns), jnp.bfloat16),
        ],
        scratch_shapes=[held] * len(terms)
        + [
            pltpu.VMEM((piece, columns), jnp.bfloat16),
            pltpu.SemaphoreType.DMA((len(terms) + 1,)),
            pltpu.SemaphoreType.REGULAR,
        ],
        compiler_params=pltpu.CompilerParams(vmem_limit_bytes=VMEM_BYTES),
        cost_estimate=pl.CostEstimate(
            flops=20 * piece * columns,
            bytes_accessed=4 * piece * columns * (len(terms) + 2),
            transcendentals=piece * columns,
        ),
    )(*terms, cotangent, *after)


def backward_kernel(widths, n_out, steps, chained, n_after, where, *refs):
    n_slots = where.shape[0]
    n_g = n_slots * len(widths)
    g_refs, (mg_ref, mu_ref), refs = refs[:n_g], refs[n_g : n_g + 2], refs[n_g + 2 :]
    if chained:
        carry_ref, refs = refs[0], refs[1:]
    refs = refs[n_after:]
    o_refs = refs[:n_out]
    g_all, acc, sem = refs[n_out:]
    i = pl.program_id(0)
    tile = mg_ref.shape[1]
    share = g_refs[0].shape[1]

    @pl.when(i == 0)
    def _():
        copies = []
        start = 0
        for n, width in enumerate(widths):
            for slot in range(n_slots):
                row = pl.multiple_of(where[slot] * share, share)
                copies.append(
                    pltpu.make_async_copy(
                        g_refs[n * n_slots + slot],
                        g_all.at[:, pl.ds(row, share), pl.ds(start, width)],
                        sem.at[n * n_slots + slot],
                    )
                )
            start += width
        for copy in copies:
            copy.start()
        if chained:
            acc[...] = carry_ref[...]
        else:
            acc[...] = jnp.zeros_like(acc)
        for copy in copies:
            copy.wait()

    columns = pl.ds(pl.multiple_of(i * tile, tile), tile)
    for n, m_ref in enumerate((mg_ref, mu_ref)):
        acc[...] += lax.dot_general(
            m_ref[...],
            g_all[n, :, columns],
            (((1,), (1,)), ((), ())),
            preferred_element_type=jnp.float32,
        )

    @pl.when(i == steps - 1)
    def _():
        if n_out == 1:
            o_refs[0][...] = acc[...]
        else:
            out = acc[...].T.astype(jnp.bfloat16)
            rows = out.shape[0] // n_out
            for k in range(n_out):
                o_refs[k][...] = out[k * rows : (k + 1) * rows]


def backward(carry, where, gathered, weights, first, tile, planes, after):
    n_slots = where.shape[0]
    widths = [pieces[0].shape[2] for pieces in gathered]
    tiles = sum(widths) // tile
    rows = gathered[0][0].shape[1] * n_slots
    depth = weights[0].shape[0]
    w_spec = pl.BlockSpec((depth, tile), lambda i, s: (0, first + i))
    whole = pl.BlockSpec((depth, rows), lambda i, s: (0, 0))
    if planes:
        out_specs = [pl.BlockSpec((rows // planes, depth), lambda i, s: (0, 0))] * planes
        out_shape = [jax.ShapeDtypeStruct((rows // planes, depth), jnp.bfloat16)] * planes
    else:
        out_specs = [whole]
        out_shape = [jax.ShapeDtypeStruct((depth, rows), jnp.float32)]
    chained = carry is not None
    return pl.pallas_call(
        functools.partial(
            backward_kernel, widths, len(out_shape), tiles, chained, len(after)
        ),
        grid_spec=pltpu.PrefetchScalarGridSpec(
            num_scalar_prefetch=1,
            grid=(tiles,),
            in_specs=[ANY] * (n_slots * len(widths))
            + [w_spec, w_spec]
            + [whole] * chained
            + [ANY] * len(after),
            out_specs=out_specs,
            scratch_shapes=[
                pltpu.VMEM((2, rows, tiles * tile), jnp.bfloat16),
                pltpu.VMEM((depth, rows), jnp.float32),
                pltpu.SemaphoreType.DMA((n_slots * len(widths),)),
            ],
        ),
        out_shape=out_shape,
        compiler_params=pltpu.CompilerParams(vmem_limit_bytes=VMEM_BYTES),
        cost_estimate=pl.CostEstimate(
            flops=4 * rows * depth * tiles * tile,
            bytes_accessed=4 * tiles * tile * (depth + rows) + 2 * rows * depth,
            transcendentals=0,
        ),
    )(where, *sum(gathered, []), *weights, *((carry,) if chained else ()), *after)


def wide(array):
    return array.astype(jnp.float32)


class ReduceScatter:
    def __init__(self, cube, keep, send):
        self.cube = cube
        self.terms = [keep, cube.sibling(send)]
        self.rows = keep.shape[1]

    def exchange(self, i):
        self.rows //= 2
        rows = self.rows
        moved = sum(wide(t[:, rows : 2 * rows]) for t in self.terms).astype(jnp.bfloat16)
        self.terms.append(self.cube.step(moved, i))
        return moved


def all_gather(cube, own):
    n_dims = len(cube.dims[0])
    pieces = [own]
    for slot in range(1, cube.half):
        low = slot & -slot
        pieces.append(cube.step(pieces[slot ^ low], n_dims - low.bit_length()))
    return pieces + [cube.sibling(p) for p in pieces]


def flip(array, bit, size):
    return lax.ppermute(array, "col", [(z, z ^ bit) for z in range(size)])


def gather_planes(x, n_col):
    xs = [x]
    for k in range(1, n_col):
        low = k & -k
        xs.append(flip(xs[k ^ low], low, n_col))
    return xs


def sum_planes(parts, n_col):
    parts = list(parts)
    for k in range(n_col - 1, 0, -1):
        low = k & -k
        moved = flip(parts[k].astype(jnp.bfloat16), low, n_col)
        parts[k ^ low] = wide(parts[k ^ low]) + wide(moved)
    return parts[0].astype(jnp.bfloat16)


def shards(cube, n_col, inputs, gate_weight, up_weight, gate_pattern, up_pattern, cotangent):
    depth, local_hidden = gate_weight.shape
    share = cotangent.shape[0]
    piece = share // len(PARTS)
    tile = local_hidden // sum(PARTS[0])
    weights = (gate_weight, up_weight)
    flags = [
        jnp.repeat(p.astype(jnp.bfloat16), BLOCK, axis=1) for p in (gate_pattern, up_pattern)
    ]
    table = places(cube, n_col)
    row, col = lax.axis_index("row"), lax.axis_index("col")
    where = jnp.asarray(table)[row, col]
    slots = jnp.asarray(np.argsort(table, axis=-1).astype(np.int32))[row, col]

    xs = []
    for t in range(len(PARTS)):
        own = cut(inputs, t, share, [xs[-1][n_col // 2]] if xs else [])
        xs.append(gather_planes(own, n_col))

    units = []
    for t, widths in enumerate(PARTS):
        starts = np.cumsum((0,) + widths)
        units += [(t, int(s), w) for s, w in zip(starts, widths)]
    n_dims = len(cube.dims[0])
    masked_weights = ()
    sums, after = [], {}
    for n, (t, first, tiles) in enumerate(units):
        keep, send, *out = forward(
            slots,
            xs[t],
            weights if t == 0 else masked_weights,
            flags if t == 0 else None,
            masked_weights if t == 0 else (),
            first,
            tiles,
            tile,
            after.pop(n, []),
        )
        masked_weights = tuple(out) if t == 0 else masked_weights
        sums.append(ReduceScatter(cube, keep, send))
        for i in range(n_dims):
            after.setdefault(n + 2 + i, []).append(sums[n].exchange(i))

    hidden, input_grad = [], []
    gathered = []
    for t, first, tiles in units:
        h, own = derivatives(
            sums[len(hidden)].terms, cotangent, t, piece, first * tile, tiles * tile, []
        )
        hidden.append(h)
        gathered.append(all_gather(cube, own))
    for t, widths in enumerate(PARTS):
        mine, gathered = gathered[: len(widths)], gathered[len(widths) :]
        calls = [len(widths)] if t < len(PARTS) - 1 else [len(widths) - 1, 1]
        carry, first = None, 0
        for n, count in enumerate(calls):
            last = n == len(calls) - 1
            used, mine = mine[:count], mine[count:]
            parts = backward(
                carry, where, used, masked_weights, first, tile, n_col if last else 0, []
            )
            carry = parts[0]
            first += sum(p[0].shape[2] for p in used) // tile
        input_grad.append(sum_planes(parts, n_col).reshape(-1, 1, piece, depth))
    n = len(PARTS[0])
    return (
        jnp.concatenate(
            [jnp.concatenate(hidden[:n], axis=1), jnp.concatenate(hidden[n:], axis=1)], axis=0
        ),
        jnp.concatenate(input_grad, axis=1).reshape(-1, depth),
    )


def solution(mesh):
    placed = (
        P("col", "row"),
        P("row", "col"),
        P("row", "col"),
        P("row", "col"),
        P("row", "col"),
        P("row", "col"),
    )
    return jax.shard_map(
        functools.partial(shards, Cube(mesh.shape["row"]), mesh.shape["col"]),
        mesh=mesh,
        in_specs=placed,
        out_specs=(P("row", "col"), P("col", "row")),
        check_vma=False,
    )
```

```python
import functools

import jax
import jax.numpy as jnp
import numpy as np
from jax import lax
from jax.experimental import pallas as pl
from jax.experimental.pallas import tpu as pltpu
from jax.sharding import PartitionSpec as P

BLOCK = 128
FORWARD = ((3, 5, 5), (5, 5, 3))
BACKWARD = (5, 5, 3)
VMEM_BYTES = 48 * 1024 * 1024
ANY = pl.BlockSpec(memory_space=pl.ANY)
COST = pl.CostEstimate(flops=1, bytes_accessed=1, transcendentals=0)


def masked(w_ref, f_ref):
    return jnp.concatenate(
        [
            w_ref[k * BLOCK : (k + 1) * BLOCK, :] * f_ref[k : k + 1, :]
            for k in range(w_ref.shape[0] // BLOCK)
        ],
        axis=0,
    )


class Cube:
    def __init__(self, size):
        self.size = size
        self.half = size // 2
        rising = [1 << b for b in range(1, size.bit_length() - 1)]
        self.dims = (rising, rising[::-1])

    def offset(self, parity, slot):
        dims = self.dims[parity]
        digits = [slot >> (len(dims) - 1 - i) & 1 for i in range(len(dims))]
        return int(np.bitwise_xor.reduce([0] + [d for d, on in zip(dims, digits) if on]))

    def owner(self, me, slot):
        if slot >= self.half:
            me, slot = me ^ 1, slot - self.half
        return me ^ self.offset(me & 1, slot)

    def step(self, array, i):
        perm = [(r, r ^ self.dims[r & 1][i]) for r in range(self.size)]
        return lax.ppermute(array, "row", perm)

    def sibling(self, array):
        return lax.ppermute(array, "row", [(r, r ^ 1) for r in range(self.size)])


def places(cube, n_col):
    ratio = cube.size // n_col
    table = np.zeros((cube.size, n_col, cube.size), np.int32)
    for me in range(cube.size):
        for z in range(n_col):
            for slot in range(cube.size):
                d = cube.owner(me, slot)
                table[me, z, slot] = ratio * ((d // ratio) ^ z) + d % ratio
    return table


def copy_all(copies):
    for copy in copies:
        copy.start()
    for copy in copies:
        copy.wait()


def cut_kernel(part, share, n_after, x_ref, *refs):
    out_ref = refs[n_after]
    piece = share * out_ref.shape[0] // x_ref.shape[0]
    for c in range(x_ref.shape[0] // share):
        start = c * share + part * piece
        out_ref[c * piece : (c + 1) * piece] = x_ref[start : start + piece]


def cut(x, part, share, after):
    rows, depth = x.shape
    in_vmem = pl.BlockSpec(memory_space=pltpu.VMEM)
    return pl.pallas_call(
        functools.partial(cut_kernel, part, share, len(after)),
        in_specs=[in_vmem] + [ANY] * len(after),
        out_specs=in_vmem,
        out_shape=jax.ShapeDtypeStruct((rows // len(FORWARD), depth), x.dtype),
        compiler_params=pltpu.CompilerParams(vmem_limit_bytes=VMEM_BYTES),
        cost_estimate=COST,
    )(x, *after)


def forward_kernel(n_x, n_after, slots, *refs):
    x_refs, refs = refs[:n_x], refs[n_x:]
    wg_ref, wu_ref, fg_ref, fu_ref = refs[:4]
    keep_ref, send_ref, x_all, sem = refs[4 + n_after :]
    half = keep_ref.shape[1]
    shares = slots.shape[0]
    share = 2 * half // shares
    ratio = shares // n_x

    @pl.when(pl.program_id(0) == 0)
    def _():
        copies = []
        for k in range(n_x):
            for c in range(ratio):
                place = k * ratio + c
                row = pl.multiple_of(slots[place] * share, share)
                copies.append(
                    pltpu.make_async_copy(
                        x_refs[k].at[pl.ds(c * share, share), :],
                        x_all.at[pl.ds(row, share), :],
                        sem.at[place],
                    )
                )
        copy_all(copies)

    for n, (w_ref, f_ref) in enumerate(((wg_ref, fg_ref), (wu_ref, fu_ref))):
        out = jnp.dot(x_all[...], masked(w_ref, f_ref), preferred_element_type=jnp.float32)
        out = out.astype(jnp.bfloat16)
        keep_ref[n] = out[:half]
        send_ref[n] = out[half:]


def forward(slots, xs, weights, flags, first, tiles, tile, after):
    depth = weights[0].shape[0]
    rows = len(xs) * xs[0].shape[0]
    w_spec = pl.BlockSpec((depth, tile), lambda i, s: (0, first + i))
    f_spec = pl.BlockSpec((flags[0].shape[0], tile), lambda i, s: (0, first + i))
    o_spec = pl.BlockSpec((2, rows // 2, tile), lambda i, s: (0, 0, i))
    out = jax.ShapeDtypeStruct((2, rows // 2, tiles * tile), jnp.bfloat16)
    return pl.pallas_call(
        functools.partial(forward_kernel, len(xs), len(after)),
        grid_spec=pltpu.PrefetchScalarGridSpec(
            num_scalar_prefetch=1,
            grid=(tiles,),
            in_specs=[ANY] * len(xs) + [w_spec] * 2 + [f_spec] * 2 + [ANY] * len(after),
            out_specs=[o_spec, o_spec],
            scratch_shapes=[
                pltpu.VMEM((rows, depth), jnp.bfloat16),
                pltpu.SemaphoreType.DMA((slots.shape[0],)),
            ],
        ),
        out_shape=[out, out],
        compiler_params=pltpu.CompilerParams(vmem_limit_bytes=VMEM_BYTES),
        cost_estimate=pl.CostEstimate(
            flops=8 * rows * depth * tiles * tile,
            bytes_accessed=4 * depth * tiles * tile,
            transcendentals=0,
        ),
    )(slots, *xs, *weights, *flags, *after)


def derivatives_kernel(first, layout, n_terms, *refs):
    sources, cot_ref = refs[: len(layout) * n_terms], refs[len(layout) * n_terms]
    h_ref, g_ref = refs[-4 - n_terms : -2 - n_terms]
    held = refs[-2 - n_terms : -2]
    cot, sem = refs[-2:]
    share, columns = h_ref.shape
    piece = share // len(FORWARD)
    copies = []
    for m, (part, source, place, width) in enumerate(layout):
        for n in range(n_terms):
            copies.append(
                pltpu.make_async_copy(
                    sources[m * n_terms + n].at[:, pl.ds(0, piece), pl.ds(source, width)],
                    held[n].at[:, pl.ds(part * piece, piece), pl.ds(place, width)],
                    sem.at[m * n_terms + n],
                )
            )
    copies.append(
        pltpu.make_async_copy(
            cot_ref.at[:, pl.ds(first, columns)], cot, sem.at[len(layout) * n_terms]
        )
    )
    copy_all(copies)
    step = 256
    for c in range(0, columns, step):
        at = slice(c, c + step)
        gate_sum = sum(wide(v[0, :, at]) for v in held)
        up_sum = sum(wide(v[1, :, at]) for v in held)
        cotangent = wide(cot[:, at])
        sigmoid_gate = jax.nn.sigmoid(gate_sum)
        activated = gate_sum * sigmoid_gate
        h_ref[:, at] = (activated * up_sum).astype(jnp.bfloat16)
        g_ref[0, :, at] = (
            cotangent * up_sum * sigmoid_gate * (1.0 + gate_sum * (1.0 - sigmoid_gate))
        ).astype(jnp.bfloat16)
        g_ref[1, :, at] = (cotangent * activated).astype(jnp.bfloat16)


def derivatives(layout, terms, cotangent, first, columns, after):
    share = cotangent.shape[0]
    n_terms = len(terms[0])
    return pl.pallas_call(
        functools.partial(derivatives_kernel, first, layout, n_terms),
        in_specs=[ANY] * (len(layout) * n_terms + 1 + len(after)),
        out_specs=[pl.BlockSpec(memory_space=pltpu.VMEM)] * 2,
        out_shape=[
            jax.ShapeDtypeStruct((share, columns), jnp.bfloat16),
            jax.ShapeDtypeStruct((2, share, columns), jnp.bfloat16),
        ],
        scratch_shapes=[pltpu.VMEM((2, share, columns), jnp.bfloat16)] * n_terms
        + [
            pltpu.VMEM((share, columns), jnp.bfloat16),
            pltpu.SemaphoreType.DMA((len(layout) * n_terms + 1,)),
        ],
        compiler_params=pltpu.CompilerParams(vmem_limit_bytes=VMEM_BYTES),
        cost_estimate=COST,
    )(*sum(terms, []), cotangent, *after)


def backward_kernel(n_out, steps, chained, where, *refs):
    n_slots = where.shape[0]
    g_refs, refs = refs[:n_slots], refs[n_slots:]
    (wg_ref, wu_ref, fg_ref, fu_ref), refs = refs[:4], refs[4:]
    if chained:
        carry_ref, refs = refs[0], refs[1:]
    o_refs = refs[:n_out]
    g_all, acc, sem = refs[n_out:]
    i = pl.program_id(0)
    tile = wg_ref.shape[1]
    share = g_refs[0].shape[1]

    @pl.when(i == 0)
    def _():
        copies = []
        for slot in range(n_slots):
            row = pl.multiple_of(where[slot] * share, share)
            copies.append(
                pltpu.make_async_copy(
                    g_refs[slot], g_all.at[:, pl.ds(row, share), :], sem.at[slot]
                )
            )
        if chained:
            copies.append(pltpu.make_async_copy(carry_ref, acc, sem.at[n_slots]))
        else:
            acc[...] = jnp.zeros_like(acc)
        copy_all(copies)

    columns = pl.ds(pl.multiple_of(i * tile, tile), tile)
    for n, (w_ref, f_ref) in enumerate(((wg_ref, fg_ref), (wu_ref, fu_ref))):
        acc[...] += lax.dot_general(
            masked(w_ref, f_ref),
            g_all[n, :, columns],
            (((1,), (1,)), ((), ())),
            preferred_element_type=jnp.float32,
        )

    @pl.when(i == steps - 1)
    def _():
        if n_out == 1:
            copy_all([pltpu.make_async_copy(acc, o_refs[0], sem.at[0])])
        else:
            for k in range(n_out):
                o_refs[k][...] = acc[:, k * share : (k + 1) * share].T.astype(jnp.bfloat16)


def backward(carry, where, pieces, weights, flags, first, tile, last):
    n_slots = where.shape[0]
    share = pieces[0].shape[1]
    width = pieces[0].shape[2]
    rows = share * n_slots
    depth = weights[0].shape[0]
    tiles = width // tile
    w_spec = pl.BlockSpec((depth, tile), lambda i, s: (0, first + i))
    f_spec = pl.BlockSpec((flags[0].shape[0], tile), lambda i, s: (0, first + i))
    if last:
        out_specs = [pl.BlockSpec((share, depth), lambda i, s: (0, 0))] * n_slots
        out_shape = [jax.ShapeDtypeStruct((share, depth), jnp.bfloat16)] * n_slots
    else:
        out_specs = [ANY]
        out_shape = [jax.ShapeDtypeStruct((depth, rows), jnp.float32)]
    chained = carry is not None
    return pl.pallas_call(
        functools.partial(backward_kernel, len(out_shape), tiles, chained),
        grid_spec=pltpu.PrefetchScalarGridSpec(
            num_scalar_prefetch=1,
            grid=(tiles,),
            in_specs=[ANY] * n_slots + [w_spec] * 2 + [f_spec] * 2 + [ANY] * chained,
            out_specs=out_specs,
            scratch_shapes=[
                pltpu.VMEM((2, rows, width), jnp.bfloat16),
                pltpu.VMEM((depth, rows), jnp.float32),
                pltpu.SemaphoreType.DMA((n_slots + 1,)),
            ],
        ),
        out_shape=out_shape,
        compiler_params=pltpu.CompilerParams(vmem_limit_bytes=VMEM_BYTES),
        cost_estimate=pl.CostEstimate(
            flops=6 * rows * depth * width,
            bytes_accessed=4 * depth * width,
            transcendentals=0,
        ),
    )(where, *pieces, *weights, *flags, *((carry,) if chained else ()))


def wide(array):
    return array.astype(jnp.float32)


class ReduceScatter:
    def __init__(self, cube, keep, send):
        self.cube = cube
        self.terms = [keep, cube.sibling(send)]
        self.rows = keep.shape[1]

    def exchange(self, i):
        self.rows //= 2
        rows = self.rows
        moved = sum(wide(t[:, rows : 2 * rows]) for t in self.terms).astype(jnp.bfloat16)
        self.terms.append(self.cube.step(moved, i))
        return moved


def all_gather(cube, own):
    n_dims = len(cube.dims[0])
    pieces = [own]
    for slot in range(1, cube.half):
        low = slot & -slot
        pieces.append(cube.step(pieces[slot ^ low], n_dims - low.bit_length()))
    return pieces + [cube.sibling(p) for p in pieces]


def flip(array, bit, size):
    return lax.ppermute(array, "col", [(z, z ^ bit) for z in range(size)])


def gather_planes(x, n_col):
    xs = [x]
    for k in range(1, n_col):
        low = k & -k
        xs.append(flip(xs[k ^ low], low, n_col))
    return xs


def sum_planes(parts, n_col):
    parts = list(parts)
    for k in range(n_col - 1, 0, -1):
        low = k & -k
        moved = flip(parts[k].astype(jnp.bfloat16), low, n_col)
        parts[k ^ low] = wide(parts[k ^ low]) + wide(moved)
    return parts[0].astype(jnp.bfloat16)


def shards(cube, n_col, inputs, gate_weight, up_weight, gate_pattern, up_pattern, cotangent):
    depth, local_hidden = gate_weight.shape
    share = cotangent.shape[0]
    tile = local_hidden // sum(BACKWARD)
    weights = (gate_weight, up_weight)
    flags = [
        jnp.repeat(p.astype(jnp.bfloat16), BLOCK, axis=1) for p in (gate_pattern, up_pattern)
    ]
    table = places(cube, n_col)
    row, col = lax.axis_index("row"), lax.axis_index("col")
    where = jnp.asarray(table)[row, col]
    slots = jnp.asarray(np.argsort(table, axis=-1).astype(np.int32))[row, col]

    xs = []
    for t in range(len(FORWARD)):
        own = cut(inputs, t, share, [xs[-1][n_col // 2]] if xs else [])
        xs.append(gather_planes(own, n_col))

    units = []
    for t, widths in enumerate(FORWARD):
        starts = np.cumsum((0,) + widths)
        units += [(t, int(s), w) for s, w in zip(starts, widths)]
    sums = []
    after = {0: [x[0] for x in xs[1:]], 1: [x[n_col // 2] for x in xs[1:]]}
    after[2] = [x[-1] for x in xs[1:]]
    for n, (t, first, tiles) in enumerate(units):
        keep, send = forward(
            slots, xs[t], weights, flags, first, tiles, tile, after.pop(n, [])
        )
        sums.append(ReduceScatter(cube, keep, send))
        after.setdefault(n + 1, []).append(keep)
        for i in range(len(cube.dims[0])):
            after.setdefault(n + 2 + i, []).append(sums[n].exchange(i))

    hidden, gathered = [], []
    starts = [sum(BACKWARD[:n]) for n in range(len(BACKWARD))]
    carry, parts = None, []

    def differentiate(n):
        first, tiles = starts[n], BACKWARD[n]
        layout, terms = [], []
        for (t, start, width), unit in zip(units, sums):
            low, high = max(first, start), min(first + tiles, start + width)
            if low < high:
                layout.append(
                    (t, (low - start) * tile, (low - first) * tile, (high - low) * tile)
                )
                terms.append(unit.terms)
        h, own = derivatives(layout, terms, cotangent, first * tile, tiles * tile, parts[:1])
        hidden.append(h)
        gathered.append(all_gather(cube, own))

    ahead = 2
    for n in range(ahead):
        differentiate(n)
    for n, first in enumerate(starts):
        last = n == len(starts) - 1
        parts = backward(carry, where, gathered[n], weights, flags, first, tile, last)
        carry = parts[0]
        if n + ahead < len(starts):
            differentiate(n + ahead)
    ratio = cube.size // n_col
    input_grad = [sum_planes(parts[c::ratio], n_col) for c in range(ratio)]
    return jnp.concatenate(hidden, axis=1), jnp.concatenate(input_grad, axis=0)


def solution(mesh):
    placed = (
        P("col", "row"),
        P("row", "col"),
        P("row", "col"),
        P("row", "col"),
        P("row", "col"),
        P("row", "col"),
    )
    return jax.shard_map(
        functools.partial(shards, Cube(mesh.shape["row"]), mesh.shape["col"]),
        mesh=mesh,
        in_specs=placed,
        out_specs=(P("row", "col"), P("col", "row")),
        check_vma=False,
    )
```

```python
import functools

import jax
import jax.numpy as jnp
import numpy as np
from jax import lax
from jax.experimental import pallas as pl
from jax.experimental.pallas import tpu as pltpu
from jax.sharding import PartitionSpec as P

BLOCK = 128
ROWS = 16
FORWARD = ((2, 3, 4, 4),)
BACKWARD = (5, 4, 4)
VMEM_BYTES = 48 * 1024 * 1024
ANY = pl.BlockSpec(memory_space=pl.ANY)
COST = pl.CostEstimate(flops=1, bytes_accessed=1, transcendentals=0)


def masked(w_ref, f_ref):
    rows, columns = w_ref.shape
    packed = (rows // BLOCK, BLOCK // ROWS, ROWS, columns)
    flags = f_ref[...].reshape(rows // BLOCK, 1, ROWS, columns)
    return (w_ref[...].reshape(packed) * flags).reshape(rows, columns)


class Cube:
    def __init__(self, size):
        self.size = size
        self.half = size // 2
        rising = [1 << b for b in range(1, size.bit_length() - 1)]
        self.dims = (rising, rising[::-1])

    def offset(self, parity, slot):
        dims = self.dims[parity]
        digits = [slot >> (len(dims) - 1 - i) & 1 for i in range(len(dims))]
        return int(np.bitwise_xor.reduce([0] + [d for d, on in zip(dims, digits) if on]))

    def owner(self, me, slot):
        if slot >= self.half:
            me, slot = me ^ 1, slot - self.half
        return me ^ self.offset(me & 1, slot)

    def step(self, array, i):
        perm = [(r, r ^ self.dims[r & 1][i]) for r in range(self.size)]
        return lax.ppermute(array, "row", perm)

    def sibling(self, array):
        return lax.ppermute(array, "row", [(r, r ^ 1) for r in range(self.size)])


def places(cube, n_col):
    ratio = cube.size // n_col
    table = np.zeros((cube.size, n_col, cube.size), np.int32)
    for me in range(cube.size):
        for z in range(n_col):
            for slot in range(cube.size):
                d = cube.owner(me, slot)
                table[me, z, slot] = ratio * ((d // ratio) ^ z) + d % ratio
    return table


def copy_all(copies):
    for copy in copies:
        copy.start()
    for copy in copies:
        copy.wait()


def cut_kernel(part, share, n_after, x_ref, *refs):
    out_ref = refs[n_after]
    piece = share * out_ref.shape[0] // x_ref.shape[0]
    for c in range(x_ref.shape[0] // share):
        start = c * share + part * piece
        out_ref[c * piece : (c + 1) * piece] = x_ref[start : start + piece]


def cut(x, part, share, after):
    rows, depth = x.shape
    in_vmem = pl.BlockSpec(memory_space=pltpu.VMEM)
    return pl.pallas_call(
        functools.partial(cut_kernel, part, share, len(after)),
        in_specs=[in_vmem] + [ANY] * len(after),
        out_specs=in_vmem,
        out_shape=jax.ShapeDtypeStruct((rows // len(FORWARD), depth), x.dtype),
        compiler_params=pltpu.CompilerParams(vmem_limit_bytes=VMEM_BYTES),
        cost_estimate=COST,
    )(x, *after)


def forward_kernel(n_x, n_after, slots, *refs):
    x_refs, refs = refs[:n_x], refs[n_x:]
    wg_ref, wu_ref, fg_ref, fu_ref = refs[:4]
    keep_ref, send_ref, x_all, sem = refs[4 + n_after :]
    half = keep_ref.shape[1]
    shares = slots.shape[0]
    share = 2 * half // shares
    ratio = shares // n_x

    @pl.when(pl.program_id(0) == 0)
    def _():
        copies = []
        for k in range(n_x):
            for c in range(ratio):
                place = k * ratio + c
                row = pl.multiple_of(slots[place] * share, share)
                copies.append(
                    pltpu.make_async_copy(
                        x_refs[k].at[pl.ds(c * share, share), :],
                        x_all.at[pl.ds(row, share), :],
                        sem.at[place],
                    )
                )
        copy_all(copies)

    for n, (w_ref, f_ref) in enumerate(((wg_ref, fg_ref), (wu_ref, fu_ref))):
        out = jnp.dot(x_all[...], masked(w_ref, f_ref), preferred_element_type=jnp.float32)
        out = out.astype(jnp.bfloat16)
        keep_ref[n] = out[:half]
        send_ref[n] = out[half:]


def forward(slots, xs, weights, flags, first, tiles, tile, after):
    depth = weights[0].shape[0]
    rows = len(xs) * xs[0].shape[0]
    w_spec = pl.BlockSpec((depth, tile), lambda i, s: (0, first + i))
    f_spec = pl.BlockSpec((flags[0].shape[0], tile), lambda i, s: (0, first + i))
    o_spec = pl.BlockSpec((2, rows // 2, tile), lambda i, s: (0, 0, i))
    out = jax.ShapeDtypeStruct((2, rows // 2, tiles * tile), jnp.bfloat16)
    return pl.pallas_call(
        functools.partial(forward_kernel, len(xs), len(after)),
        grid_spec=pltpu.PrefetchScalarGridSpec(
            num_scalar_prefetch=1,
            grid=(tiles,),
            in_specs=[ANY] * len(xs) + [w_spec] * 2 + [f_spec] * 2 + [ANY] * len(after),
            out_specs=[o_spec, o_spec],
            scratch_shapes=[
                pltpu.VMEM((rows, depth), jnp.bfloat16),
                pltpu.SemaphoreType.DMA((slots.shape[0],)),
            ],
        ),
        out_shape=[out, out],
        compiler_params=pltpu.CompilerParams(vmem_limit_bytes=VMEM_BYTES),
        cost_estimate=pl.CostEstimate(
            flops=8 * rows * depth * tiles * tile,
            bytes_accessed=4 * depth * tiles * tile,
            transcendentals=0,
        ),
    )(slots, *xs, *weights, *flags, *after)


def derivatives_kernel(first, layout, n_terms, *refs):
    sources, cot_ref = refs[: len(layout) * n_terms], refs[len(layout) * n_terms]
    h_ref, g_ref = refs[-4 - n_terms : -2 - n_terms]
    held = refs[-2 - n_terms : -2]
    cot, sem = refs[-2:]
    share, columns = h_ref.shape
    piece = share // len(FORWARD)
    copies = []
    for m, (part, source, place, width) in enumerate(layout):
        for n in range(n_terms):
            copies.append(
                pltpu.make_async_copy(
                    sources[m * n_terms + n].at[:, pl.ds(0, piece), pl.ds(source, width)],
                    held[n].at[:, pl.ds(part * piece, piece), pl.ds(place, width)],
                    sem.at[m * n_terms + n],
                )
            )
    copies.append(
        pltpu.make_async_copy(
            cot_ref.at[:, pl.ds(first, columns)], cot, sem.at[len(layout) * n_terms]
        )
    )
    copy_all(copies)
    step = 256
    for c in range(0, columns, step):
        at = slice(c, c + step)
        gate_sum = sum(wide(v[0, :, at]) for v in held)
        up_sum = sum(wide(v[1, :, at]) for v in held)
        cotangent = wide(cot[:, at])
        sigmoid_gate = jax.nn.sigmoid(gate_sum)
        activated = gate_sum * sigmoid_gate
        h_ref[:, at] = (activated * up_sum).astype(jnp.bfloat16)
        g_ref[0, :, at] = (
            cotangent * up_sum * sigmoid_gate * (1.0 + gate_sum * (1.0 - sigmoid_gate))
        ).astype(jnp.bfloat16)
        g_ref[1, :, at] = (cotangent * activated).astype(jnp.bfloat16)


def derivatives(layout, terms, cotangent, first, columns, after):
    share = cotangent.shape[0]
    n_terms = len(terms[0])
    return pl.pallas_call(
        functools.partial(derivatives_kernel, first, layout, n_terms),
        in_specs=[ANY] * (len(layout) * n_terms + 1 + len(after)),
        out_specs=[pl.BlockSpec(memory_space=pltpu.VMEM)] * 2,
        out_shape=[
            jax.ShapeDtypeStruct((share, columns), jnp.bfloat16),
            jax.ShapeDtypeStruct((2, share, columns), jnp.bfloat16),
        ],
        scratch_shapes=[pltpu.VMEM((2, share, columns), jnp.bfloat16)] * n_terms
        + [
            pltpu.VMEM((share, columns), jnp.bfloat16),
            pltpu.SemaphoreType.DMA((len(layout) * n_terms + 1,)),
        ],
        compiler_params=pltpu.CompilerParams(vmem_limit_bytes=VMEM_BYTES),
        cost_estimate=COST,
    )(*sum(terms, []), cotangent, *after)


def backward_kernel(n_out, steps, chained, where, *refs):
    n_slots = where.shape[0]
    g_refs, refs = refs[:n_slots], refs[n_slots:]
    (wg_ref, wu_ref, fg_ref, fu_ref), refs = refs[:4], refs[4:]
    if chained:
        carry_ref, refs = refs[0], refs[1:]
    o_refs = refs[:n_out]
    g_all, acc, both, sem = refs[n_out:]
    i = pl.program_id(0)
    tile = wg_ref.shape[1]
    share = g_refs[0].shape[1]

    @pl.when(i == 0)
    def _():
        copies = []
        for slot in range(n_slots):
            row = pl.multiple_of(where[slot] * share, share)
            copies.append(
                pltpu.make_async_copy(
                    g_refs[slot], g_all.at[:, pl.ds(row, share), :], sem.at[slot]
                )
            )
        if chained:
            copies.append(pltpu.make_async_copy(carry_ref, acc, sem.at[n_slots]))
        else:
            acc[...] = jnp.zeros_like(acc)
        copy_all(copies)

    columns = pl.ds(pl.multiple_of(i * tile, tile), tile)
    both[:, :tile] = masked(wg_ref, fg_ref)
    both[:, tile:] = masked(wu_ref, fu_ref)
    acc[...] += lax.dot_general(
        both[...],
        jnp.concatenate([g_all[0, :, columns], g_all[1, :, columns]], axis=1),
        (((1,), (1,)), ((), ())),
        preferred_element_type=jnp.float32,
    )

    @pl.when(i == steps - 1)
    def _():
        if n_out == 1:
            copy_all([pltpu.make_async_copy(acc, o_refs[0], sem.at[0])])
        else:
            for k in range(n_out):
                o_refs[k][...] = acc[:, k * share : (k + 1) * share].T.astype(jnp.bfloat16)


def backward(carry, where, pieces, weights, flags, first, tile, last):
    n_slots = where.shape[0]
    share = pieces[0].shape[1]
    width = pieces[0].shape[2]
    rows = share * n_slots
    depth = weights[0].shape[0]
    tiles = width // tile
    w_spec = pl.BlockSpec((depth, tile), lambda i, s: (0, first + i))
    f_spec = pl.BlockSpec((flags[0].shape[0], tile), lambda i, s: (0, first + i))
    if last:
        out_specs = [pl.BlockSpec((share, depth), lambda i, s: (0, 0))] * n_slots
        out_shape = [jax.ShapeDtypeStruct((share, depth), jnp.bfloat16)] * n_slots
    else:
        out_specs = [ANY]
        out_shape = [jax.ShapeDtypeStruct((depth, rows), jnp.float32)]
    chained = carry is not None
    return pl.pallas_call(
        functools.partial(backward_kernel, len(out_shape), tiles, chained),
        grid_spec=pltpu.PrefetchScalarGridSpec(
            num_scalar_prefetch=1,
            grid=(tiles,),
            in_specs=[ANY] * n_slots + [w_spec] * 2 + [f_spec] * 2 + [ANY] * chained,
            out_specs=out_specs,
            scratch_shapes=[
                pltpu.VMEM((2, rows, width), jnp.bfloat16),
                pltpu.VMEM((depth, rows), jnp.float32),
                pltpu.VMEM((depth, 2 * tile), jnp.bfloat16),
                pltpu.SemaphoreType.DMA((n_slots + 1,)),
            ],
        ),
        out_shape=out_shape,
        compiler_params=pltpu.CompilerParams(vmem_limit_bytes=VMEM_BYTES),
        cost_estimate=pl.CostEstimate(
            flops=6 * rows * depth * width,
            bytes_accessed=4 * depth * width,
            transcendentals=0,
        ),
    )(where, *pieces, *weights, *flags, *((carry,) if chained else ()))


def wide(array):
    return array.astype(jnp.float32)


class ReduceScatter:
    def __init__(self, cube, keep, send):
        self.cube = cube
        self.terms = [keep, cube.sibling(send)]
        self.rows = keep.shape[1]

    def exchange(self, i):
        self.rows //= 2
        rows = self.rows
        moved = sum(wide(t[:, rows : 2 * rows]) for t in self.terms).astype(jnp.bfloat16)
        self.terms.append(self.cube.step(moved, i))
        return moved


def all_gather(cube, own):
    n_dims = len(cube.dims[0])
    pieces = [own]
    for slot in range(1, cube.half):
        low = slot & -slot
        pieces.append(cube.step(pieces[slot ^ low], n_dims - low.bit_length()))
    return pieces + [cube.sibling(p) for p in pieces]


def flip(array, bit, size):
    return lax.ppermute(array, "col", [(z, z ^ bit) for z in range(size)])


def gather_planes(x, n_col):
    xs = [x]
    for k in range(1, n_col):
        low = k & -k
        xs.append(flip(xs[k ^ low], low, n_col))
    return xs


def sum_planes(parts, n_col):
    parts = list(parts)
    for k in range(n_col - 1, 0, -1):
        low = k & -k
        moved = flip(parts[k].astype(jnp.bfloat16), low, n_col)
        parts[k ^ low] = wide(parts[k ^ low]) + wide(moved)
    return parts[0].astype(jnp.bfloat16)


def shards(cube, n_col, inputs, gate_weight, up_weight, gate_pattern, up_pattern, cotangent):
    depth, local_hidden = gate_weight.shape
    share = cotangent.shape[0]
    tile = local_hidden // sum(BACKWARD)
    weights = (gate_weight, up_weight)
    flags = [
        jnp.repeat(jnp.repeat(p.astype(jnp.bfloat16), BLOCK, axis=1), ROWS, axis=0)
        for p in (gate_pattern, up_pattern)
    ]
    table = places(cube, n_col)
    row, col = lax.axis_index("row"), lax.axis_index("col")
    where = jnp.asarray(table)[row, col]
    slots = jnp.asarray(np.argsort(table, axis=-1).astype(np.int32))[row, col]

    xs = []
    for t in range(len(FORWARD)):
        own = inputs
        if len(FORWARD) > 1:
            own = cut(inputs, t, share, [xs[-1][n_col // 2]] if xs else [])
        xs.append(gather_planes(own, n_col))

    units = []
    for t, widths in enumerate(FORWARD):
        starts = np.cumsum((0,) + widths)
        units += [(t, int(s), w) for s, w in zip(starts, widths)]
    sums = []
    after = {0: [x[0] for x in xs[1:]], 1: [x[n_col // 2] for x in xs[1:]]}
    after[2] = [x[-1] for x in xs[1:]]
    for n, (t, first, tiles) in enumerate(units):
        keep, send = forward(
            slots, xs[t], weights, flags, first, tiles, tile, after.pop(n, [])
        )
        sums.append(ReduceScatter(cube, keep, send))
        after.setdefault(n + 1, []).append(keep)
        for i in range(len(cube.dims[0])):
            after.setdefault(n + 2 + i, []).append(sums[n].exchange(i))

    hidden, gathered = [], []
    starts = [sum(BACKWARD[:n]) for n in range(len(BACKWARD))]
    carry, parts = None, []

    def differentiate(n):
        first, tiles = starts[n], BACKWARD[n]
        layout, terms = [], []
        for (t, start, width), unit in zip(units, sums):
            low, high = max(first, start), min(first + tiles, start + width)
            if low < high:
                layout.append(
                    (t, (low - start) * tile, (low - first) * tile, (high - low) * tile)
                )
                terms.append(unit.terms)
        h, own = derivatives(layout, terms, cotangent, first * tile, tiles * tile, parts[:1])
        hidden.append(h)
        gathered.append(all_gather(cube, own))

    ahead = 2
    for n in range(ahead):
        differentiate(n)
    for n, first in enumerate(starts):
        last = n == len(starts) - 1
        parts = backward(carry, where, gathered[n], weights, flags, first, tile, last)
        carry = parts[0]
        if n + ahead < len(starts):
            differentiate(n + ahead)
    ratio = cube.size // n_col
    input_grad = [sum_planes(parts[c::ratio], n_col) for c in range(ratio)]
    return jnp.concatenate(hidden, axis=1), jnp.concatenate(input_grad, axis=0)


def solution(mesh):
    placed = (
        P("col", "row"),
        P("row", "col"),
        P("row", "col"),
        P("row", "col"),
        P("row", "col"),
        P("row", "col"),
    )
    return jax.shard_map(
        functools.partial(shards, Cube(mesh.shape["row"]), mesh.shape["col"]),
        mesh=mesh,
        in_specs=placed,
        out_specs=(P("row", "col"), P("col", "row")),
        check_vma=False,
    )
```

```python
import functools

import jax
import jax.numpy as jnp
import numpy as np
from jax import lax
from jax.experimental import pallas as pl
from jax.experimental.pallas import tpu as pltpu
from jax.sharding import PartitionSpec as P

BLOCK = 128
FORWARD = (2, 3, 3, 3, 2)
BACKWARD = (5, 4, 4)
TOKEN_PARTS = 2
VMEM_BYTES = 48 * 1024 * 1024
ANY = pl.BlockSpec(memory_space=pl.ANY)
COST = pl.CostEstimate(flops=1, bytes_accessed=1, transcendentals=0)


def masked(w_ref, f_ref):
    rows, columns = w_ref.shape
    flags = f_ref[...].reshape(rows // BLOCK, 1, columns)
    return (w_ref[...].reshape(rows // BLOCK, BLOCK, columns) * flags).reshape(rows, columns)


class Cube:
    def __init__(self, size):
        self.size = size
        self.half = size // 2
        rising = [1 << b for b in range(1, size.bit_length() - 1)]
        self.dims = (rising, rising[::-1])

    def offset(self, parity, slot):
        dims = self.dims[parity]
        digits = [slot >> (len(dims) - 1 - i) & 1 for i in range(len(dims))]
        return int(np.bitwise_xor.reduce([0] + [d for d, on in zip(dims, digits) if on]))

    def owner(self, me, slot):
        if slot >= self.half:
            me, slot = me ^ 1, slot - self.half
        return me ^ self.offset(me & 1, slot)

    def step(self, array, i):
        perm = [(r, r ^ self.dims[r & 1][i]) for r in range(self.size)]
        return lax.ppermute(array, "row", perm)

    def sibling(self, array):
        return lax.ppermute(array, "row", [(r, r ^ 1) for r in range(self.size)])


def places(cube, n_col):
    ratio = cube.size // n_col
    table = np.zeros((cube.size, n_col, cube.size), np.int32)
    for me in range(cube.size):
        for z in range(n_col):
            for slot in range(cube.size):
                d = cube.owner(me, slot)
                table[me, z, slot] = ratio * ((d // ratio) ^ z) + d % ratio
    return table


def copy_all(copies):
    for copy in copies:
        copy.start()
    for copy in copies:
        copy.wait()


def forward_kernel(n_x, n_after, slots, *refs):
    x_refs, refs = refs[:n_x], refs[n_x:]
    wg_ref, wu_ref, fg_ref, fu_ref = refs[:4]
    keep_ref, send_ref, x_all, sem = refs[4 + n_after :]
    half = keep_ref.shape[1]
    shares = slots.shape[0]
    share = 2 * half // shares
    ratio = shares // n_x

    @pl.when(pl.program_id(0) == 0)
    def _():
        copies = []
        for k in range(n_x):
            for c in range(ratio):
                place = k * ratio + c
                row = pl.multiple_of(slots[place] * share, share)
                copies.append(
                    pltpu.make_async_copy(
                        x_refs[k].at[pl.ds(c * share, share), :],
                        x_all.at[pl.ds(row, share), :],
                        sem.at[place],
                    )
                )
        copy_all(copies)

    for n, (w_ref, f_ref) in enumerate(((wg_ref, fg_ref), (wu_ref, fu_ref))):
        out = jnp.dot(x_all[...], masked(w_ref, f_ref), preferred_element_type=jnp.float32)
        out = out.astype(jnp.bfloat16)
        keep_ref[n] = out[:half]
        send_ref[n] = out[half:]


def forward(slots, xs, weights, flags, first, tiles, tile, after):
    depth = weights[0].shape[0]
    rows = len(xs) * xs[0].shape[0]
    w_spec = pl.BlockSpec((depth, tile), lambda i, s: (0, first + i))
    f_spec = pl.BlockSpec((flags[0].shape[0], tile), lambda i, s: (0, first + i))
    o_spec = pl.BlockSpec((2, rows // 2, tile), lambda i, s: (0, 0, i))
    out = jax.ShapeDtypeStruct((2, rows // 2, tiles * tile), jnp.bfloat16)
    return pl.pallas_call(
        functools.partial(forward_kernel, len(xs), len(after)),
        grid_spec=pltpu.PrefetchScalarGridSpec(
            num_scalar_prefetch=1,
            grid=(tiles,),
            in_specs=[ANY] * len(xs) + [w_spec] * 2 + [f_spec] * 2 + [ANY] * len(after),
            out_specs=[o_spec, o_spec],
            scratch_shapes=[
                pltpu.VMEM((rows, depth), jnp.bfloat16),
                pltpu.SemaphoreType.DMA((slots.shape[0],)),
            ],
        ),
        out_shape=[out, out],
        compiler_params=pltpu.CompilerParams(vmem_limit_bytes=VMEM_BYTES),
        cost_estimate=pl.CostEstimate(
            flops=8 * rows * depth * tiles * tile,
            bytes_accessed=4 * depth * tiles * tile,
            transcendentals=0,
        ),
    )(slots, *xs, *weights, *flags, *after)


def derivatives_kernel(first, layout, n_terms, split, *refs):
    sources, cot_ref = refs[: len(layout) * n_terms], refs[len(layout) * n_terms]
    h_ref, *g_refs = refs[-3 - split - n_terms : -2 - n_terms]
    held = refs[-2 - n_terms : -2]
    cot, sem = refs[-2:]
    share, columns = h_ref.shape
    piece = share // split
    copies = []
    for m, (source, place, width) in enumerate(layout):
        for n in range(n_terms):
            copies.append(
                pltpu.make_async_copy(
                    sources[m * n_terms + n].at[:, pl.ds(0, share), pl.ds(source, width)],
                    held[n].at[:, :, pl.ds(place, width)],
                    sem.at[m * n_terms + n],
                )
            )
    copies.append(
        pltpu.make_async_copy(
            cot_ref.at[:, pl.ds(first, columns)], cot, sem.at[len(layout) * n_terms]
        )
    )
    copy_all(copies)
    step = 256
    for c in range(0, columns, step):
        at = slice(c, c + step)
        gate_sum = sum(wide(v[0, :, at]) for v in held)
        up_sum = sum(wide(v[1, :, at]) for v in held)
        cotangent = wide(cot[:, at])
        sigmoid_gate = jax.nn.sigmoid(gate_sum)
        activated = gate_sum * sigmoid_gate
        h_ref[:, at] = (activated * up_sum).astype(jnp.bfloat16)
        gate_grad = (
            cotangent * up_sum * sigmoid_gate * (1.0 + gate_sum * (1.0 - sigmoid_gate))
        ).astype(jnp.bfloat16)
        up_grad = (cotangent * activated).astype(jnp.bfloat16)
        for k, g_ref in enumerate(g_refs):
            g_ref[0, :, at] = gate_grad[k * piece : (k + 1) * piece]
            g_ref[1, :, at] = up_grad[k * piece : (k + 1) * piece]


def derivatives(layout, terms, cotangent, first, columns, split, after):
    share = cotangent.shape[0]
    n_terms = len(terms[0])
    return pl.pallas_call(
        functools.partial(derivatives_kernel, first, layout, n_terms, split),
        in_specs=[ANY] * (len(layout) * n_terms + 1 + len(after)),
        out_specs=[pl.BlockSpec(memory_space=pltpu.VMEM)] * (1 + split),
        out_shape=[
            jax.ShapeDtypeStruct((share, columns), jnp.bfloat16),
            *[jax.ShapeDtypeStruct((2, share // split, columns), jnp.bfloat16)] * split,
        ],
        scratch_shapes=[pltpu.VMEM((2, share, columns), jnp.bfloat16)] * n_terms
        + [
            pltpu.VMEM((share, columns), jnp.bfloat16),
            pltpu.SemaphoreType.DMA((len(layout) * n_terms + 1,)),
        ],
        compiler_params=pltpu.CompilerParams(vmem_limit_bytes=VMEM_BYTES),
        cost_estimate=COST,
    )(*sum(terms, []), cotangent, *after)


def backward_kernel(n_out, steps, chained, part, piece, where, *refs):
    n_slots = where.shape[0]
    g_refs, refs = refs[:n_slots], refs[n_slots:]
    (wg_ref, wu_ref, fg_ref, fu_ref), refs = refs[:4], refs[4:]
    if chained:
        carry_ref, refs = refs[0], refs[1:]
    o_refs = refs[:n_out]
    g_all, acc, both, sem = refs[n_out:]
    i = pl.program_id(0)
    tile = wg_ref.shape[1]
    rows = acc.shape[1]
    n_parts = rows // (n_slots * piece)

    @pl.when(i == 0)
    def _():
        copies = []
        for slot in range(n_slots):
            for p in range(n_parts):
                row = pl.multiple_of((p * n_slots + where[slot]) * piece, piece)
                copies.append(
                    pltpu.make_async_copy(
                        g_refs[slot].at[:, pl.ds(p * piece, piece), :],
                        g_all.at[:, pl.ds(row, piece), :],
                        sem.at[slot * n_parts + p],
                    )
                )
        if chained:
            copies.append(
                pltpu.make_async_copy(
                    carry_ref.at[:, pl.ds(part * rows, rows)], acc, sem.at[n_slots * n_parts]
                )
            )
        else:
            acc[...] = jnp.zeros_like(acc)
        copy_all(copies)

    columns = pl.ds(pl.multiple_of(i * tile, tile), tile)
    both[:, :tile] = masked(wg_ref, fg_ref)
    both[:, tile:] = masked(wu_ref, fu_ref)
    acc[...] += lax.dot_general(
        both[...],
        jnp.concatenate([g_all[0, :, columns], g_all[1, :, columns]], axis=1),
        (((1,), (1,)), ((), ())),
        preferred_element_type=jnp.float32,
    )

    @pl.when(i == steps - 1)
    def _():
        if n_out == 1:
            copy_all([pltpu.make_async_copy(acc, o_refs[0], sem.at[0])])
        else:
            for k in range(n_out):
                size = rows // n_out
                o_refs[k][...] = acc[:, k * size : (k + 1) * size].T.astype(jnp.bfloat16)


def backward(carry, where, pieces, weights, flags, first, tile, part, piece, planes):
    n_slots = where.shape[0]
    width = pieces[0].shape[2]
    rows = pieces[0].shape[1] * n_slots
    depth = weights[0].shape[0]
    tiles = width // tile
    w_spec = pl.BlockSpec((depth, tile), lambda i, s: (0, first + i))
    f_spec = pl.BlockSpec((flags[0].shape[0], tile), lambda i, s: (0, first + i))
    if planes:
        out_specs = [pl.BlockSpec((rows // planes, depth), lambda i, s: (0, 0))] * planes
        out_shape = [jax.ShapeDtypeStruct((rows // planes, depth), jnp.bfloat16)] * planes
    else:
        out_specs = [ANY]
        out_shape = [jax.ShapeDtypeStruct((depth, rows), jnp.float32)]
    chained = carry is not None
    return pl.pallas_call(
        functools.partial(backward_kernel, len(out_shape), tiles, chained, part, piece),
        grid_spec=pltpu.PrefetchScalarGridSpec(
            num_scalar_prefetch=1,
            grid=(tiles,),
            in_specs=[ANY] * n_slots + [w_spec] * 2 + [f_spec] * 2 + [ANY] * chained,
            out_specs=out_specs,
            scratch_shapes=[
                pltpu.VMEM((2, rows, width), jnp.bfloat16),
                pltpu.VMEM((depth, rows), jnp.float32),
                pltpu.VMEM((depth, 2 * tile), jnp.bfloat16),
                pltpu.SemaphoreType.DMA((rows // piece + 1,)),
            ],
        ),
        out_shape=out_shape,
        compiler_params=pltpu.CompilerParams(vmem_limit_bytes=VMEM_BYTES),
        cost_estimate=pl.CostEstimate(
            flops=6 * rows * depth * width,
            bytes_accessed=4 * depth * width,
            transcendentals=0,
        ),
    )(where, *pieces, *weights, *flags, *((carry,) if chained else ()))


def wide(array):
    return array.astype(jnp.float32)


class ReduceScatter:
    def __init__(self, cube, keep, send):
        self.cube = cube
        self.terms = [keep, cube.sibling(send)]
        self.rows = keep.shape[1]

    def exchange(self, i):
        self.rows //= 2
        rows = self.rows
        moved = sum(wide(t[:, rows : 2 * rows]) for t in self.terms).astype(jnp.bfloat16)
        self.terms.append(self.cube.step(moved, i))
        return moved


def all_gather(cube, own):
    n_dims = len(cube.dims[0])
    pieces = [own]
    for slot in range(1, cube.half):
        low = slot & -slot
        pieces.append(cube.step(pieces[slot ^ low], n_dims - low.bit_length()))
    return pieces + [cube.sibling(p) for p in pieces]


def flip(array, bit, size):
    return lax.ppermute(array, "col", [(z, z ^ bit) for z in range(size)])


def gather_planes(x, n_col):
    xs = [x]
    for k in range(1, n_col):
        low = k & -k
        xs.append(flip(xs[k ^ low], low, n_col))
    return xs


def sum_planes(parts, n_col):
    parts = list(parts)
    for k in range(n_col - 1, 0, -1):
        low = k & -k
        moved = flip(parts[k].astype(jnp.bfloat16), low, n_col)
        parts[k ^ low] = wide(parts[k ^ low]) + wide(moved)
    return parts[0].astype(jnp.bfloat16)


def shards(cube, n_col, inputs, gate_weight, up_weight, gate_pattern, up_pattern, cotangent):
    depth, local_hidden = gate_weight.shape
    share = cotangent.shape[0]
    tile = local_hidden // sum(BACKWARD)
    weights = (gate_weight, up_weight)
    flags = [
        jnp.repeat(p.astype(jnp.bfloat16), BLOCK, axis=1) for p in (gate_pattern, up_pattern)
    ]
    table = places(cube, n_col)
    row, col = lax.axis_index("row"), lax.axis_index("col")
    where = jnp.asarray(table)[row, col]
    slots = jnp.asarray(np.argsort(table, axis=-1).astype(np.int32))[row, col]

    xs = gather_planes(inputs, n_col)
    units = list(zip(np.cumsum((0,) + FORWARD).tolist(), FORWARD))
    sums, after = [], {}
    n_dims = len(cube.dims[0])
    for n, (first, tiles) in enumerate(units):
        keep, send = forward(
            slots, xs, weights, flags, first, tiles, tile, after.pop(n, [])
        )
        sums.append(ReduceScatter(cube, keep, send))
        after.setdefault(n + 1, []).append(keep)
        for i in range(n_dims):
            after.setdefault(n + 2 + i, []).append(sums[n].exchange(i))
        after.setdefault(n + 2 + n_dims, []).append(sums[n].terms[-1])

    piece = share // TOKEN_PARTS
    hidden, gathered = [], []
    starts = [sum(BACKWARD[:n]) for n in range(len(BACKWARD))]
    carry = []

    def differentiate(n):
        first, tiles = starts[n], BACKWARD[n]
        layout, terms = [], []
        for (start, width), unit in zip(units, sums):
            low, high = max(first, start), min(first + tiles, start + width)
            if low < high:
                layout.append(((low - start) * tile, (low - first) * tile, (high - low) * tile))
                terms.append(unit.terms)
        split = TOKEN_PARTS if n == len(BACKWARD) - 1 else 1
        h, *own = derivatives(layout, terms, cotangent, first * tile, tiles * tile, split, carry)
        hidden.append(h)
        gathered.extend(all_gather(cube, o) for o in own)

    ahead = 2
    for n in range(ahead):
        differentiate(n)
    for n, first in enumerate(starts[:-1]):
        carry = backward(
            carry[0] if carry else None,
            where,
            gathered[n],
            weights,
            flags,
            first,
            tile,
            0,
            piece,
            0,
        )
        if n + ahead < len(starts):
            differentiate(n + ahead)
    input_grad = []
    for t, pieces in enumerate(gathered[len(starts) - 1 :]):
        parts = backward(
            carry[0], where, pieces, weights, flags, starts[-1], tile, t, piece, n_col
        )
        input_grad.append(sum_planes(parts, n_col).reshape(-1, 1, piece, depth))
    return (
        jnp.concatenate(hidden, axis=1),
        jnp.concatenate(input_grad, axis=1).reshape(-1, depth),
    )


def solution(mesh):
    placed = (
        P("col", "row"),
        P("row", "col"),
        P("row", "col"),
        P("row", "col"),
        P("row", "col"),
        P("row", "col"),
    )
    return jax.shard_map(
        functools.partial(shards, Cube(mesh.shape["row"]), mesh.shape["col"]),
        mesh=mesh,
        in_specs=placed,
        out_specs=(P("row", "col"), P("col", "row")),
        check_vma=False,
    )
```

```python
import functools

import jax
import jax.numpy as jnp
import numpy as np
from jax import lax
from jax.experimental import pallas as pl
from jax.experimental.pallas import tpu as pltpu
from jax.sharding import PartitionSpec as P

BLOCK = 128
MASKING = (7, 6)
FORWARD = (2, 3, 4, 4)
BACKWARD = (5, 4, 4)
WHOLE_GATHERS = (0,)
VMEM_BYTES = 48 * 1024 * 1024
ANY = pl.BlockSpec(memory_space=pl.ANY)
COST = pl.CostEstimate(flops=1, bytes_accessed=1, transcendentals=0)


def masked(w_ref, f_ref):
    rows, columns = w_ref.shape
    flags = f_ref[...].reshape(rows // BLOCK, 1, columns)
    return (w_ref[...].reshape(rows // BLOCK, BLOCK, columns) * flags).reshape(rows, columns)


class Cube:
    def __init__(self, size):
        self.size = size
        self.half = size // 2
        rising = [1 << b for b in range(1, size.bit_length() - 1)]
        self.dims = (rising, rising[::-1])

    def offset(self, parity, slot):
        dims = self.dims[parity]
        digits = [slot >> (len(dims) - 1 - i) & 1 for i in range(len(dims))]
        return int(np.bitwise_xor.reduce([0] + [d for d, on in zip(dims, digits) if on]))

    def owner(self, me, slot):
        if slot >= self.half:
            me, slot = me ^ 1, slot - self.half
        return me ^ self.offset(me & 1, slot)

    def step(self, array, i):
        perm = [(r, r ^ self.dims[r & 1][i]) for r in range(self.size)]
        return lax.ppermute(array, "row", perm)

    def sibling(self, array):
        return lax.ppermute(array, "row", [(r, r ^ 1) for r in range(self.size)])


def places(cube, n_col):
    ratio = cube.size // n_col
    table = np.zeros((cube.size, n_col, cube.size), np.int32)
    for me in range(cube.size):
        for z in range(n_col):
            for slot in range(cube.size):
                d = cube.owner(me, slot)
                table[me, z, slot] = ratio * ((d // ratio) ^ z) + d % ratio
    return table


def copy_all(copies):
    for copy in copies:
        copy.start()
    for copy in copies:
        copy.wait()


def mask_kernel(wg_ref, wu_ref, fg_ref, fu_ref, *refs):
    o_ref = refs[-1]
    tile = wg_ref.shape[1]
    o_ref[:, :tile] = masked(wg_ref, fg_ref)
    o_ref[:, tile:] = masked(wu_ref, fu_ref)


def mask(weights, flags, so_far, first, tiles, tile, after):
    depth, hidden = weights[0].shape
    w_spec = pl.BlockSpec((depth, tile), lambda i: (0, first + i))
    f_spec = pl.BlockSpec((flags[0].shape[0], tile), lambda i: (0, first + i))
    return pl.pallas_call(
        mask_kernel,
        grid=(tiles,),
        in_specs=[w_spec, w_spec, f_spec, f_spec] + [ANY] * (len(so_far) + len(after)),
        out_specs=pl.BlockSpec((depth, 2 * tile), lambda i: (0, first + i)),
        out_shape=jax.ShapeDtypeStruct((depth, 2 * hidden), weights[0].dtype),
        input_output_aliases={4: 0} if so_far else {},
        compiler_params=pltpu.CompilerParams(vmem_limit_bytes=VMEM_BYTES),
        cost_estimate=pl.CostEstimate(
            flops=0, bytes_accessed=8 * depth * tiles * tile, transcendentals=0
        ),
    )(*weights, *flags, *so_far, *after)


def forward_kernel(n_x, n_after, slots, *refs):
    x_refs = refs[:n_x]
    w_ref = refs[n_x]
    keep_ref, send_ref, x_all, sem = refs[n_x + 1 + n_after :]
    half = keep_ref.shape[0]
    shares = slots.shape[0]
    share = 2 * half // shares
    ratio = shares // n_x

    @pl.when(pl.program_id(0) == 0)
    def _():
        copies = []
        for k in range(n_x):
            for c in range(ratio):
                place = k * ratio + c
                row = pl.multiple_of(slots[place] * share, share)
                copies.append(
                    pltpu.make_async_copy(
                        x_refs[k].at[pl.ds(c * share, share), :],
                        x_all.at[pl.ds(row, share), :],
                        sem.at[place],
                    )
                )
        copy_all(copies)

    out = jnp.dot(x_all[...], w_ref[...], preferred_element_type=jnp.float32)
    out = out.astype(jnp.bfloat16)
    keep_ref[...] = out[:half]
    send_ref[...] = out[half:]


def forward(slots, xs, weights, first, tiles, tile, after):
    depth = weights.shape[0]
    rows = len(xs) * xs[0].shape[0]
    o_spec = pl.BlockSpec((rows // 2, 2 * tile), lambda i, s: (0, i))
    out = jax.ShapeDtypeStruct((rows // 2, 2 * tiles * tile), jnp.bfloat16)
    return pl.pallas_call(
        functools.partial(forward_kernel, len(xs), len(after)),
        grid_spec=pltpu.PrefetchScalarGridSpec(
            num_scalar_prefetch=1,
            grid=(tiles,),
            in_specs=[ANY] * len(xs)
            + [pl.BlockSpec((depth, 2 * tile), lambda i, s: (0, first + i))]
            + [ANY] * len(after),
            out_specs=[o_spec, o_spec],
            scratch_shapes=[
                pltpu.VMEM((rows, depth), jnp.bfloat16),
                pltpu.SemaphoreType.DMA((slots.shape[0],)),
            ],
        ),
        out_shape=[out, out],
        compiler_params=pltpu.CompilerParams(vmem_limit_bytes=VMEM_BYTES),
        cost_estimate=pl.CostEstimate(
            flops=8 * rows * depth * tiles * tile,
            bytes_accessed=4 * depth * tiles * tile,
            transcendentals=0,
        ),
    )(slots, *xs, weights, *after)


def derivatives_kernel(first, tile, layout, n_terms, *refs):
    sources, cot_ref = refs[: len(layout) * n_terms], refs[len(layout) * n_terms]
    h_ref, g_ref = refs[-4 - n_terms : -2 - n_terms]
    held = refs[-2 - n_terms : -2]
    cot, sem = refs[-2:]
    share, columns = h_ref.shape
    copies = []
    for m, (source, place, width) in enumerate(layout):
        for n in range(n_terms):
            copies.append(
                pltpu.make_async_copy(
                    sources[m * n_terms + n].at[pl.ds(0, share), pl.ds(2 * source, 2 * width)],
                    held[n].at[:, pl.ds(2 * place, 2 * width)],
                    sem.at[m * n_terms + n],
                )
            )
    copies.append(
        pltpu.make_async_copy(
            cot_ref.at[:, pl.ds(first, columns)], cot, sem.at[len(layout) * n_terms]
        )
    )
    copy_all(copies)
    step = tile // 2
    for c in range(0, columns, step):
        start = c // tile * 2 * tile + c % tile
        gate_at, up_at = slice(start, start + step), slice(start + tile, start + tile + step)
        gate_sum = sum(wide(v[:, gate_at]) for v in held)
        up_sum = sum(wide(v[:, up_at]) for v in held)
        cotangent = wide(cot[:, c : c + step])
        sigmoid_gate = jax.nn.sigmoid(gate_sum)
        activated = gate_sum * sigmoid_gate
        h_ref[:, c : c + step] = (activated * up_sum).astype(jnp.bfloat16)
        g_ref[:, gate_at] = (
            cotangent * up_sum * sigmoid_gate * (1.0 + gate_sum * (1.0 - sigmoid_gate))
        ).astype(jnp.bfloat16)
        g_ref[:, up_at] = (cotangent * activated).astype(jnp.bfloat16)


def derivatives(layout, terms, cotangent, first, columns, tile, after):
    share = cotangent.shape[0]
    n_terms = len(terms[0])
    return pl.pallas_call(
        functools.partial(derivatives_kernel, first, tile, layout, n_terms),
        in_specs=[ANY] * (len(layout) * n_terms + 1 + len(after)),
        out_specs=[pl.BlockSpec(memory_space=pltpu.VMEM)] * 2,
        out_shape=[
            jax.ShapeDtypeStruct((share, columns), jnp.bfloat16),
            jax.ShapeDtypeStruct((share, 2 * columns), jnp.bfloat16),
        ],
        scratch_shapes=[pltpu.VMEM((share, 2 * columns), jnp.bfloat16)] * n_terms
        + [
            pltpu.VMEM((share, columns), jnp.bfloat16),
            pltpu.SemaphoreType.DMA((len(layout) * n_terms + 1,)),
        ],
        compiler_params=pltpu.CompilerParams(vmem_limit_bytes=VMEM_BYTES),
        cost_estimate=COST,
    )(*sum(terms, []), cotangent, *after)


def backward_kernel(n_g, n_out, steps, chained, where, *refs):
    g_refs, w_ref, refs = refs[:n_g], refs[n_g], refs[n_g + 1 :]
    if chained:
        carry_ref, refs = refs[0], refs[1:]
    o_refs = refs[:n_out]
    g_all, acc, sem = refs[n_out:]
    i = pl.program_id(0)
    shares = where.shape[0]
    share = acc.shape[1] // shares

    @pl.when(i == 0)
    def _():
        copies = []
        for n in range(shares):
            row = pl.multiple_of(where[n] * share, share)
            source = g_refs[n] if n_g > 1 else g_refs[0].at[pl.ds(n * share, share), :]
            copies.append(
                pltpu.make_async_copy(source, g_all.at[pl.ds(row, share), :], sem.at[n])
            )
        if chained:
            copies.append(pltpu.make_async_copy(carry_ref, acc, sem.at[shares]))
        else:
            acc[...] = jnp.zeros_like(acc)
        copy_all(copies)

    width = w_ref.shape[1]
    acc[...] += lax.dot_general(
        w_ref[...],
        g_all[:, pl.ds(pl.multiple_of(i * width, width), width)],
        (((1,), (1,)), ((), ())),
        preferred_element_type=jnp.float32,
    )

    @pl.when(i == steps - 1)
    def _():
        if n_out == 1:
            copy_all([pltpu.make_async_copy(acc, o_refs[0], sem.at[0])])
        else:
            for k in range(n_out):
                o_refs[k][...] = acc[:, k * share : (k + 1) * share].T.astype(jnp.bfloat16)


def backward(carry, where, pieces, weights, first, tile, last):
    shares = where.shape[0]
    rows = sum(p.shape[0] for p in pieces)
    share = rows // shares
    depth = weights.shape[0]
    width = pieces[0].shape[1]
    tiles = width // (2 * tile)
    if last:
        out_specs = [pl.BlockSpec((share, depth), lambda i, s: (0, 0))] * shares
        out_shape = [jax.ShapeDtypeStruct((share, depth), jnp.bfloat16)] * shares
    else:
        out_specs = [ANY]
        out_shape = [jax.ShapeDtypeStruct((depth, rows), jnp.float32)]
    return pl.pallas_call(
        functools.partial(
            backward_kernel, len(pieces), len(out_shape), tiles, len(carry) > 0
        ),
        grid_spec=pltpu.PrefetchScalarGridSpec(
            num_scalar_prefetch=1,
            grid=(tiles,),
            in_specs=[ANY] * len(pieces)
            + [pl.BlockSpec((depth, 2 * tile), lambda i, s: (0, first + i))]
            + [ANY] * len(carry),
            out_specs=out_specs,
            scratch_shapes=[
                pltpu.VMEM((rows, width), jnp.bfloat16),
                pltpu.VMEM((depth, rows), jnp.float32),
                pltpu.SemaphoreType.DMA((shares + 1,)),
            ],
        ),
        out_shape=out_shape,
        compiler_params=pltpu.CompilerParams(vmem_limit_bytes=VMEM_BYTES),
        cost_estimate=pl.CostEstimate(
            flops=6 * rows * depth * width,
            bytes_accessed=2 * depth * width,
            transcendentals=0,
        ),
    )(where, *pieces, weights, *carry)


def wide(array):
    return array.astype(jnp.float32)


class ReduceScatter:
    def __init__(self, cube, keep, send):
        self.cube = cube
        self.terms = [keep, cube.sibling(send)]
        self.rows = keep.shape[0]

    def exchange(self, i):
        self.rows //= 2
        rows = self.rows
        moved = sum(wide(t[rows : 2 * rows]) for t in self.terms).astype(jnp.bfloat16)
        self.terms.append(self.cube.step(moved, i))
        return moved


def all_gather(cube, own):
    n_dims = len(cube.dims[0])
    pieces = [own]
    for slot in range(1, cube.half):
        low = slot & -slot
        pieces.append(cube.step(pieces[slot ^ low], n_dims - low.bit_length()))
    return pieces + [cube.sibling(p) for p in pieces]


def flip(array, bit, size):
    return lax.ppermute(array, "col", [(z, z ^ bit) for z in range(size)])


def gather_planes(x, n_col):
    xs = [x]
    for k in range(1, n_col):
        low = k & -k
        xs.append(flip(xs[k ^ low], low, n_col))
    return xs


def sum_planes(parts, n_col):
    parts = list(parts)
    for k in range(n_col - 1, 0, -1):
        low = k & -k
        moved = flip(parts[k].astype(jnp.bfloat16), low, n_col)
        parts[k ^ low] = wide(parts[k ^ low]) + wide(moved)
    return parts[0].astype(jnp.bfloat16)


def shards(cube, n_col, inputs, gate_weight, up_weight, gate_pattern, up_pattern, cotangent):
    depth, local_hidden = gate_weight.shape
    share = cotangent.shape[0]
    tile = local_hidden // sum(BACKWARD)
    flags = [
        jnp.repeat(p.astype(jnp.bfloat16), BLOCK, axis=1) for p in (gate_pattern, up_pattern)
    ]
    by_slot = places(cube, n_col)
    ratio = cube.size // n_col
    by_device = np.array(
        [
            [ratio * ((d // ratio) ^ z) + d % ratio for d in range(cube.size)]
            for z in range(n_col)
        ],
        np.int32,
    )
    row, col = lax.axis_index("row"), lax.axis_index("col")
    where_slot = jnp.asarray(by_slot)[row, col]
    where_device = jnp.asarray(by_device)[col]
    slots = jnp.asarray(np.argsort(by_slot, axis=-1).astype(np.int32))[row, col]

    xs = gather_planes(inputs, n_col)
    weights, first = [], 0
    for tiles in MASKING:
        weights = [
            mask(
                (gate_weight, up_weight),
                flags,
                weights,
                first,
                tiles,
                tile,
                [xs[n_col // 2]] if weights else [],
            )
        ]
        first += tiles
    weights = weights[0]

    units = list(zip(np.cumsum((0,) + FORWARD).tolist(), FORWARD))
    sums, after = [], {}
    for n, (first, tiles) in enumerate(units):
        keep, send = forward(slots, xs, weights, first, tiles, tile, after.pop(n, []))
        sums.append(ReduceScatter(cube, keep, send))
        after.setdefault(n + 1, []).append(keep)
        for i in range(len(cube.dims[0])):
            after.setdefault(n + 2 + i, []).append(sums[n].exchange(i))

    hidden, gathered = [], []
    starts = [sum(BACKWARD[:n]) for n in range(len(BACKWARD))]
    carry = []

    def differentiate(n):
        first, tiles = starts[n], BACKWARD[n]
        layout, terms = [], []
        for (start, width), unit in zip(units, sums):
            low, high = max(first, start), min(first + tiles, start + width)
            if low < high:
                layout.append(((low - start) * tile, (low - first) * tile, (high - low) * tile))
                terms.append(unit.terms)
        h, own = derivatives(layout, terms, cotangent, first * tile, tiles * tile, tile, carry)
        hidden.append(h)
        if n in WHOLE_GATHERS:
            gathered.append([lax.all_gather(own, "row", axis=0, tiled=True)])
        else:
            gathered.append(all_gather(cube, own))

    ahead = 2
    for n in range(ahead):
        differentiate(n)
    for n, first in enumerate(starts):
        last = n == len(starts) - 1
        where = where_device if n in WHOLE_GATHERS else where_slot
        carry = backward(carry, where, gathered[n], weights, first, tile, last)
        if n + ahead < len(starts):
            differentiate(n + ahead)
    input_grad = [sum_planes(carry[c::ratio], n_col) for c in range(ratio)]
    return jnp.concatenate(hidden, axis=1), jnp.concatenate(input_grad, axis=0)


def solution(mesh):
    placed = (
        P("col", "row"),
        P("row", "col"),
        P("row", "col"),
        P("row", "col"),
        P("row", "col"),
        P("row", "col"),
    )
    return jax.shard_map(
        functools.partial(shards, Cube(mesh.shape["row"]), mesh.shape["col"]),
        mesh=mesh,
        in_specs=placed,
        out_specs=(P("row", "col"), P("col", "row")),
        check_vma=False,
    )
```

```python
import functools

import jax
import jax.numpy as jnp
import numpy as np
from jax import lax
from jax.experimental import pallas as pl
from jax.experimental.pallas import tpu as pltpu
from jax.sharding import PartitionSpec as P

BLOCK = 128
FORWARD = (2, 3, 4, 4)
BACKWARD = (5, 5, 3)
VMEM_BYTES = 48 * 1024 * 1024
ANY = pl.BlockSpec(memory_space=pl.ANY)
COST = pl.CostEstimate(flops=1, bytes_accessed=1, transcendentals=0)


def masked(w_ref, f_ref):
    rows, columns = w_ref.shape
    flags = f_ref[...].reshape(rows // BLOCK, 1, columns)
    return (w_ref[...].reshape(rows // BLOCK, BLOCK, columns) * flags).reshape(rows, columns)


def then(array, *others):
    return lax.optimization_barrier((array, *others))[0]


class Cube:
    def __init__(self, size):
        self.size = size
        self.half = size // 2
        rising = [1 << b for b in range(1, size.bit_length() - 1)]
        self.dims = (rising, rising[::-1])

    def offset(self, parity, slot):
        dims = self.dims[parity]
        digits = [slot >> (len(dims) - 1 - i) & 1 for i in range(len(dims))]
        return int(np.bitwise_xor.reduce([0] + [d for d, on in zip(dims, digits) if on]))

    def owner(self, me, slot):
        if slot >= self.half:
            me, slot = me ^ 1, slot - self.half
        return me ^ self.offset(me & 1, slot)

    def step(self, array, i):
        perm = [(r, r ^ self.dims[r & 1][i]) for r in range(self.size)]
        return lax.ppermute(array, "row", perm)

    def sibling(self, array):
        return lax.ppermute(array, "row", [(r, r ^ 1) for r in range(self.size)])


def places(cube, n_col):
    ratio = cube.size // n_col
    table = np.zeros((cube.size, n_col, cube.size), np.int32)
    for me in range(cube.size):
        for z in range(n_col):
            for slot in range(cube.size):
                d = cube.owner(me, slot)
                table[me, z, slot] = ratio * ((d // ratio) ^ z) + d % ratio
    return table


def copy_all(copies):
    for copy in copies:
        copy.start()
    for copy in copies:
        copy.wait()


def gather_shares(x_refs, x_all, slots, sem):
    shares = slots.shape[0]
    share = x_all.shape[0] // shares
    ratio = shares // len(x_refs)
    copies = []
    for k, x_ref in enumerate(x_refs):
        for c in range(ratio):
            place = k * ratio + c
            row = pl.multiple_of(slots[place] * share, share)
            copies.append(
                pltpu.make_async_copy(
                    x_ref.at[pl.ds(c * share, share), :],
                    x_all.at[pl.ds(row, share), :],
                    sem.at[place],
                )
            )
    copy_all(copies)


def first_half_kernel(n_x, slots, *refs):
    wg_ref, wu_ref, fg_ref, fu_ref, pg_ref, pu_ref, x_all, sem = refs[n_x:]

    @pl.when(pl.program_id(0) == 0)
    def _():
        gather_shares(refs[:n_x], x_all, slots, sem)

    for w_ref, f_ref, p_ref in ((wg_ref, fg_ref, pg_ref), (wu_ref, fu_ref, pu_ref)):
        p_ref[...] = jnp.dot(
            x_all[...], masked(w_ref, f_ref.at[0]), preferred_element_type=jnp.float32
        )


def first_half(slots, xs, weights, flags, tile):
    depth, hidden = weights[0].shape
    half = depth // 2
    rows = len(xs) * xs[0].shape[0]
    w_spec = pl.BlockSpec((half, tile), lambda i, s: (0, i))
    f_spec = pl.BlockSpec((1, flags[0].shape[1], tile), lambda i, s: (0, 0, i))
    p_spec = pl.BlockSpec((rows, tile), lambda i, s: (0, i))
    return pl.pallas_call(
        functools.partial(first_half_kernel, len(xs)),
        grid_spec=pltpu.PrefetchScalarGridSpec(
            num_scalar_prefetch=1,
            grid=(hidden // tile,),
            in_specs=[ANY] * len(xs) + [w_spec] * 2 + [f_spec] * 2,
            out_specs=[p_spec] * 2,
            scratch_shapes=[
                pltpu.VMEM((rows, half), jnp.bfloat16),
                pltpu.SemaphoreType.DMA((slots.shape[0],)),
            ],
        ),
        out_shape=[jax.ShapeDtypeStruct((rows, hidden), jnp.float32)] * 2,
        compiler_params=pltpu.CompilerParams(vmem_limit_bytes=VMEM_BYTES),
        cost_estimate=pl.CostEstimate(
            flops=4 * rows * depth * hidden,
            bytes_accessed=4 * half * hidden,
            transcendentals=0,
        ),
    )(slots, *xs, *weights, *flags)


def forward_kernel(n_x, n_after, slots, *refs):
    wg_ref, wu_ref, fg_ref, fu_ref, pg_ref, pu_ref = refs[n_x : n_x + 6]
    keep_ref, send_ref, x_all, sem = refs[n_x + 6 + n_after :]
    half = keep_ref.shape[1]

    @pl.when(pl.program_id(0) == 0)
    def _():
        gather_shares(refs[:n_x], x_all, slots, sem)

    for n, (w_ref, f_ref, p_ref) in enumerate(
        ((wg_ref, fg_ref, pg_ref), (wu_ref, fu_ref, pu_ref))
    ):
        out = jnp.dot(
            x_all[...], masked(w_ref, f_ref.at[0]), preferred_element_type=jnp.float32
        )
        out = (out + p_ref[...]).astype(jnp.bfloat16)
        keep_ref[n] = out[:half]
        send_ref[n] = out[half:]


def forward(slots, xs, weights, flags, partial, first, tiles, tile, after):
    half = weights[0].shape[0] // 2
    rows = len(xs) * xs[0].shape[0]
    w_spec = pl.BlockSpec((half, tile), lambda i, s: (1, first + i))
    f_spec = pl.BlockSpec((1, flags[0].shape[1], tile), lambda i, s: (1, 0, first + i))
    p_spec = pl.BlockSpec((rows, tile), lambda i, s: (0, first + i))
    o_spec = pl.BlockSpec((2, rows // 2, tile), lambda i, s: (0, 0, i))
    out = jax.ShapeDtypeStruct((2, rows // 2, tiles * tile), jnp.bfloat16)
    return pl.pallas_call(
        functools.partial(forward_kernel, len(xs), len(after)),
        grid_spec=pltpu.PrefetchScalarGridSpec(
            num_scalar_prefetch=1,
            grid=(tiles,),
            in_specs=[ANY] * len(xs)
            + [w_spec] * 2
            + [f_spec] * 2
            + [p_spec] * 2
            + [ANY] * len(after),
            out_specs=[o_spec, o_spec],
            scratch_shapes=[
                pltpu.VMEM((rows, half), jnp.bfloat16),
                pltpu.SemaphoreType.DMA((slots.shape[0],)),
            ],
        ),
        out_shape=[out, out],
        compiler_params=pltpu.CompilerParams(vmem_limit_bytes=VMEM_BYTES),
        cost_estimate=pl.CostEstimate(
            flops=8 * rows * half * tiles * tile,
            bytes_accessed=4 * half * tiles * tile,
            transcendentals=0,
        ),
    )(slots, *xs, *weights, *flags, *partial, *after)


def derivatives_kernel(first, layout, n_terms, *refs):
    sources, cot_ref = refs[: len(layout) * n_terms], refs[len(layout) * n_terms]
    h_ref, g_ref = refs[-4 - n_terms : -2 - n_terms]
    held = refs[-2 - n_terms : -2]
    cot, sem = refs[-2:]
    share, columns = h_ref.shape
    copies = []
    for m, (source, place, width) in enumerate(layout):
        for n in range(n_terms):
            copies.append(
                pltpu.make_async_copy(
                    sources[m * n_terms + n].at[:, pl.ds(0, share), pl.ds(source, width)],
                    held[n].at[:, :, pl.ds(place, width)],
                    sem.at[m * n_terms + n],
                )
            )
    copies.append(
        pltpu.make_async_copy(
            cot_ref.at[:, pl.ds(first, columns)], cot, sem.at[len(layout) * n_terms]
        )
    )
    copy_all(copies)
    step = 256
    for c in range(0, columns, step):
        at = slice(c, c + step)
        gate_sum = sum(wide(v[0, :, at]) for v in held)
        up_sum = sum(wide(v[1, :, at]) for v in held)
        cotangent = wide(cot[:, at])
        sigmoid_gate = jax.nn.sigmoid(gate_sum)
        activated = gate_sum * sigmoid_gate
        h_ref[:, at] = (activated * up_sum).astype(jnp.bfloat16)
        g_ref[0, :, at] = (
            cotangent * up_sum * sigmoid_gate * (1.0 + gate_sum * (1.0 - sigmoid_gate))
        ).astype(jnp.bfloat16)
        g_ref[1, :, at] = (cotangent * activated).astype(jnp.bfloat16)


def derivatives(layout, terms, cotangent, first, columns, after):
    share = cotangent.shape[0]
    n_terms = len(terms[0])
    return pl.pallas_call(
        functools.partial(derivatives_kernel, first, layout, n_terms),
        in_specs=[ANY] * (len(layout) * n_terms + 1 + len(after)),
        out_specs=[pl.BlockSpec(memory_space=pltpu.VMEM)] * 2,
        out_shape=[
            jax.ShapeDtypeStruct((share, columns), jnp.bfloat16),
            jax.ShapeDtypeStruct((2, share, columns), jnp.bfloat16),
        ],
        scratch_shapes=[pltpu.VMEM((2, share, columns), jnp.bfloat16)] * n_terms
        + [
            pltpu.VMEM((share, columns), jnp.bfloat16),
            pltpu.SemaphoreType.DMA((len(layout) * n_terms + 1,)),
        ],
        compiler_params=pltpu.CompilerParams(vmem_limit_bytes=VMEM_BYTES),
        cost_estimate=COST,
    )(*sum(terms, []), cotangent, *after)


def backward_kernel(n_out, steps, chained, n_after, where, *refs):
    n_slots = where.shape[0]
    g_refs, refs = refs[:n_slots], refs[n_slots:]
    (wg_ref, wu_ref, fg_ref, fu_ref), refs = refs[:4], refs[4:]
    if chained:
        carry_ref, refs = refs[0], refs[1:]
    refs = refs[n_after:]
    o_refs = refs[:n_out]
    g_all, acc, both, sem = refs[n_out:]
    i = pl.program_id(0)
    tile = wg_ref.shape[1]
    share = g_refs[0].shape[1]

    @pl.when(i == 0)
    def _():
        copies = []
        for slot in range(n_slots):
            row = pl.multiple_of(where[slot] * share, share)
            copies.append(
                pltpu.make_async_copy(
                    g_refs[slot], g_all.at[:, pl.ds(row, share), :], sem.at[slot]
                )
            )
        if chained:
            copies.append(pltpu.make_async_copy(carry_ref, acc, sem.at[n_slots]))
        else:
            acc[...] = jnp.zeros_like(acc)
        copy_all(copies)

    columns = pl.ds(pl.multiple_of(i * tile, tile), tile)
    both[:, :tile] = masked(wg_ref, fg_ref)
    both[:, tile:] = masked(wu_ref, fu_ref)
    acc[...] += lax.dot_general(
        both[...],
        jnp.concatenate([g_all[0, :, columns], g_all[1, :, columns]], axis=1),
        (((1,), (1,)), ((), ())),
        preferred_element_type=jnp.float32,
    )

    @pl.when(i == steps - 1)
    def _():
        if n_out == 1:
            copy_all([pltpu.make_async_copy(acc, o_refs[0], sem.at[0])])
        else:
            for k in range(n_out):
                o_refs[k][...] = acc[:, k * share : (k + 1) * share].T.astype(jnp.bfloat16)


def backward(carry, where, pieces, weights, flags, first, tile, last, after):
    n_slots = where.shape[0]
    share = pieces[0].shape[1]
    width = pieces[0].shape[2]
    rows = share * n_slots
    depth = weights[0].shape[0]
    tiles = width // tile
    w_spec = pl.BlockSpec((depth, tile), lambda i, s: (0, first + i))
    f_spec = pl.BlockSpec((*flags[0].shape[:2], tile), lambda i, s: (0, 0, first + i))
    if last:
        out_specs = [pl.BlockSpec((share, depth), lambda i, s: (0, 0))] * n_slots
        out_shape = [jax.ShapeDtypeStruct((share, depth), jnp.bfloat16)] * n_slots
    else:
        out_specs = [ANY]
        out_shape = [jax.ShapeDtypeStruct((depth, rows), jnp.float32)]
    chained = carry is not None
    return pl.pallas_call(
        functools.partial(
            backward_kernel, len(out_shape), tiles, chained, len(after)
        ),
        grid_spec=pltpu.PrefetchScalarGridSpec(
            num_scalar_prefetch=1,
            grid=(tiles,),
            in_specs=[ANY] * n_slots + [w_spec] * 2 + [f_spec] * 2 + [ANY] * (chained + len(after)),
            out_specs=out_specs,
            scratch_shapes=[
                pltpu.VMEM((2, rows, width), jnp.bfloat16),
                pltpu.VMEM((depth, rows), jnp.float32),
                pltpu.VMEM((depth, 2 * tile), jnp.bfloat16),
                pltpu.SemaphoreType.DMA((n_slots + 1,)),
            ],
        ),
        out_shape=out_shape,
        compiler_params=pltpu.CompilerParams(vmem_limit_bytes=VMEM_BYTES),
        cost_estimate=pl.CostEstimate(
            flops=6 * rows * depth * width,
            bytes_accessed=4 * depth * width,
            transcendentals=0,
        ),
    )(where, *pieces, *weights, *flags, *((carry,) if chained else ()), *after)


def wide(array):
    return array.astype(jnp.float32)


class ReduceScatter:
    def __init__(self, cube, keep, send):
        self.cube = cube
        self.terms = [keep, cube.sibling(send)]
        self.rows = keep.shape[1]

    def exchange(self, i):
        self.rows //= 2
        rows = self.rows
        moved = sum(wide(t[:, rows : 2 * rows]) for t in self.terms).astype(jnp.bfloat16)
        self.terms.append(self.cube.step(moved, i))
        return moved


class AllGather:
    def __init__(self, cube, own):
        self.cube = cube
        n_dims = len(cube.dims[0])
        self.pieces = [own] + [cube.step(own, n_dims - 1 - i) for i in range(n_dims)]

    def finish(self, *after):
        cube = self.cube
        n_dims = len(cube.dims[0])
        pieces = {0: self.pieces[0]}
        for i in range(n_dims):
            pieces[1 << i] = self.pieces[1 + i]
        pieces = {slot: then(p, *after) for slot, p in pieces.items()}
        for slot in range(1, cube.half):
            if slot not in pieces:
                low = slot & -slot
                pieces[slot] = cube.step(pieces[slot ^ low], n_dims - low.bit_length())
        pieces = [pieces[slot] for slot in range(cube.half)]
        return pieces + [cube.sibling(p) for p in pieces]


def flip(array, bit, size):
    return lax.ppermute(array, "col", [(z, z ^ bit) for z in range(size)])


def gather_planes(x, n_col):
    xs = [x]
    for k in range(1, n_col):
        low = k & -k
        xs.append(flip(xs[k ^ low], low, n_col))
    return xs


def sum_planes(groups, n_col):
    groups = [list(parts) for parts in groups]
    far = [k for k in range(n_col - 1, 0, -1) if k & (k - 1)]
    near = [k for k in range(n_col - 1, 0, -1) if not k & (k - 1)]
    for k in far + near:
        low = k & -k
        if k in near:
            groups = [
                [then(p, *arrived) if m == k else p for m, p in enumerate(parts)]
                for parts in groups
            ]
        moved = [flip(parts[k].astype(jnp.bfloat16), low, n_col) for parts in groups]
        if k in far:
            arrived = moved
        for parts, m in zip(groups, moved):
            parts[k ^ low] = wide(parts[k ^ low]) + wide(m)
    return [parts[0].astype(jnp.bfloat16) for parts in groups]


def shards(cube, n_col, inputs, gate_weight, up_weight, gate_pattern, up_pattern, cotangent):
    depth, local_hidden = gate_weight.shape
    share = cotangent.shape[0]
    tile = local_hidden // sum(BACKWARD)
    weights = (gate_weight, up_weight)
    flags = [
        jnp.repeat(p.astype(jnp.bfloat16), BLOCK, axis=1).reshape(2, -1, local_hidden)
        for p in (gate_pattern, up_pattern)
    ]
    table = places(cube, n_col)
    row, col = lax.axis_index("row"), lax.axis_index("col")
    where = jnp.asarray(table)[row, col]
    slots = jnp.asarray(np.argsort(table, axis=-1).astype(np.int32))[row, col]

    first_xs = gather_planes(inputs[:, : depth // 2], n_col)
    own = then(inputs[:, depth // 2 :], *first_xs[1:])
    second_xs = [own] + [flip(own, k, n_col) for k in range(1, n_col)]
    partial = first_half(slots, first_xs, weights, flags, tile)

    units = list(zip(np.cumsum((0,) + FORWARD).tolist(), FORWARD))
    sums, after = [], {}
    for n, (first, tiles) in enumerate(units):
        keep, send = forward(
            slots, second_xs, weights, flags, partial, first, tiles, tile, after.pop(n, [])
        )
        sums.append(ReduceScatter(cube, keep, send))
        after.setdefault(n + 1, []).append(keep)
        for i in range(len(cube.dims[0])):
            after.setdefault(n + 2 + i, []).append(sums[n].exchange(i))

    hidden, gathers, owns = [], [], []
    starts = [sum(BACKWARD[:n]) for n in range(len(BACKWARD))]
    for first, tiles in zip(starts, BACKWARD):
        layout, terms = [], []
        for (start, width), unit in zip(units, sums):
            low, high = max(first, start), min(first + tiles, start + width)
            if low < high:
                layout.append(((low - start) * tile, (low - first) * tile, (high - low) * tile))
                terms.append(unit.terms)
        h, own = derivatives(layout, terms, cotangent, first * tile, tiles * tile, owns[-1:])
        hidden.append(h)
        owns.append(own)
        gathers.append(AllGather(cube, own))
    carry, parts = None, []
    for n, first in enumerate(starts):
        last = n == len(starts) - 1
        pieces = gathers[n].finish(*parts[:1]) if n == 1 else gathers[n].finish()
        ready = [p for g in gathers[n + 1 :] for p in (g.pieces[:1])]
        parts = backward(carry, where, pieces, weights, flags, first, tile, last, ready)
        carry = parts[0]
    ratio = cube.size // n_col
    input_grad = sum_planes([parts[c::ratio] for c in range(ratio)], n_col)
    return jnp.concatenate(hidden, axis=1), jnp.concatenate(input_grad, axis=0)


def solution(mesh):
    placed = (
        P("col", "row"),
        P("row", "col"),
        P("row", "col"),
        P("row", "col"),
        P("row", "col"),
        P("row", "col"),
    )
    return jax.shard_map(
        functools.partial(shards, Cube(mesh.shape["row"]), mesh.shape["col"]),
        mesh=mesh,
        in_specs=placed,
        out_specs=(P("row", "col"), P("col", "row")),
        check_vma=False,
    )
```

```python
import functools

import jax
import jax.numpy as jnp
import numpy as np
from jax import lax
from jax.experimental import pallas as pl
from jax.experimental.pallas import tpu as pltpu
from jax.sharding import PartitionSpec as P

BLOCK = 128
FORWARD = (2, 3, 4, 4)
BACKWARD = (5, 8)
TOKEN_PARTS = 2
VMEM_BYTES = 48 * 1024 * 1024
ANY = pl.BlockSpec(memory_space=pl.ANY)
COST = pl.CostEstimate(flops=1, bytes_accessed=1, transcendentals=0)


def masked(w_ref, f_ref):
    rows, columns = w_ref.shape
    flags = f_ref[...].reshape(rows // BLOCK, 1, columns)
    return (w_ref[...].reshape(rows // BLOCK, BLOCK, columns) * flags).reshape(rows, columns)


def then(array, *others):
    return lax.optimization_barrier((array, *others))[0]


class Cube:
    def __init__(self, size):
        self.size = size
        self.half = size // 2
        rising = [1 << b for b in range(1, size.bit_length() - 1)]
        self.dims = (rising, rising[::-1])

    def offset(self, parity, slot):
        dims = self.dims[parity]
        digits = [slot >> (len(dims) - 1 - i) & 1 for i in range(len(dims))]
        return int(np.bitwise_xor.reduce([0] + [d for d, on in zip(dims, digits) if on]))

    def owner(self, me, slot):
        if slot >= self.half:
            me, slot = me ^ 1, slot - self.half
        return me ^ self.offset(me & 1, slot)

    def step(self, array, i):
        perm = [(r, r ^ self.dims[r & 1][i]) for r in range(self.size)]
        return lax.ppermute(array, "row", perm)

    def sibling(self, array):
        return lax.ppermute(array, "row", [(r, r ^ 1) for r in range(self.size)])


def places(cube, n_col):
    ratio = cube.size // n_col
    table = np.zeros((cube.size, n_col, cube.size), np.int32)
    for me in range(cube.size):
        for z in range(n_col):
            for slot in range(cube.size):
                d = cube.owner(me, slot)
                table[me, z, slot] = ratio * ((d // ratio) ^ z) + d % ratio
    return table


def copy_all(copies):
    for copy in copies:
        copy.start()
    for copy in copies:
        copy.wait()


def forward_kernel(n_x, n_after, slots, *refs):
    x_refs, refs = refs[:n_x], refs[n_x:]
    wg_ref, wu_ref, fg_ref, fu_ref = refs[:4]
    keep_ref, send_ref, x_all, sem = refs[4 + n_after :]
    half = keep_ref.shape[1]
    shares = slots.shape[0]
    share = 2 * half // shares
    ratio = shares // n_x

    @pl.when(pl.program_id(0) == 0)
    def _():
        copies = []
        for k in range(n_x):
            for c in range(ratio):
                place = k * ratio + c
                row = pl.multiple_of(slots[place] * share, share)
                copies.append(
                    pltpu.make_async_copy(
                        x_refs[k].at[pl.ds(c * share, share), :],
                        x_all.at[pl.ds(row, share), :],
                        sem.at[place],
                    )
                )
        copy_all(copies)

    for n, (w_ref, f_ref) in enumerate(((wg_ref, fg_ref), (wu_ref, fu_ref))):
        out = jnp.dot(x_all[...], masked(w_ref, f_ref), preferred_element_type=jnp.float32)
        out = out.astype(jnp.bfloat16)
        keep_ref[n] = out[:half]
        send_ref[n] = out[half:]


def forward(slots, xs, weights, flags, first, tiles, tile, after):
    depth = weights[0].shape[0]
    rows = len(xs) * xs[0].shape[0]
    w_spec = pl.BlockSpec((depth, tile), lambda i, s: (0, first + i))
    f_spec = pl.BlockSpec((flags[0].shape[0], tile), lambda i, s: (0, first + i))
    o_spec = pl.BlockSpec((2, rows // 2, tile), lambda i, s: (0, 0, i))
    out = jax.ShapeDtypeStruct((2, rows // 2, tiles * tile), jnp.bfloat16)
    return pl.pallas_call(
        functools.partial(forward_kernel, len(xs), len(after)),
        grid_spec=pltpu.PrefetchScalarGridSpec(
            num_scalar_prefetch=1,
            grid=(tiles,),
            in_specs=[ANY] * len(xs) + [w_spec] * 2 + [f_spec] * 2 + [ANY] * len(after),
            out_specs=[o_spec, o_spec],
            scratch_shapes=[
                pltpu.VMEM((rows, depth), jnp.bfloat16),
                pltpu.SemaphoreType.DMA((slots.shape[0],)),
            ],
        ),
        out_shape=[out, out],
        compiler_params=pltpu.CompilerParams(vmem_limit_bytes=VMEM_BYTES),
        cost_estimate=pl.CostEstimate(
            flops=8 * rows * depth * tiles * tile,
            bytes_accessed=4 * depth * tiles * tile,
            transcendentals=0,
        ),
    )(slots, *xs, *weights, *flags, *after)


def derivatives_kernel(first, layout, n_terms, *refs):
    sources, cot_ref = refs[: len(layout) * n_terms], refs[len(layout) * n_terms]
    h_ref, g_ref = refs[-4 - n_terms : -2 - n_terms]
    held = refs[-2 - n_terms : -2]
    cot, sem = refs[-2:]
    share, columns = h_ref.shape
    copies = []
    for m, (source, place, width) in enumerate(layout):
        for n in range(n_terms):
            copies.append(
                pltpu.make_async_copy(
                    sources[m * n_terms + n].at[:, pl.ds(0, share), pl.ds(source, width)],
                    held[n].at[:, :, pl.ds(place, width)],
                    sem.at[m * n_terms + n],
                )
            )
    copies.append(
        pltpu.make_async_copy(
            cot_ref.at[:, pl.ds(first, columns)], cot, sem.at[len(layout) * n_terms]
        )
    )
    copy_all(copies)
    step = 256
    for c in range(0, columns, step):
        at = slice(c, c + step)
        gate_sum = sum(wide(v[0, :, at]) for v in held)
        up_sum = sum(wide(v[1, :, at]) for v in held)
        cotangent = wide(cot[:, at])
        sigmoid_gate = jax.nn.sigmoid(gate_sum)
        activated = gate_sum * sigmoid_gate
        h_ref[:, at] = (activated * up_sum).astype(jnp.bfloat16)
        g_ref[0, :, at] = (
            cotangent * up_sum * sigmoid_gate * (1.0 + gate_sum * (1.0 - sigmoid_gate))
        ).astype(jnp.bfloat16)
        g_ref[1, :, at] = (cotangent * activated).astype(jnp.bfloat16)


def derivatives(layout, terms, cotangent, first, columns, after):
    share = cotangent.shape[0]
    n_terms = len(terms[0])
    return pl.pallas_call(
        functools.partial(derivatives_kernel, first, layout, n_terms),
        in_specs=[ANY] * (len(layout) * n_terms + 1 + len(after)),
        out_specs=[pl.BlockSpec(memory_space=pltpu.VMEM)] * 2,
        out_shape=[
            jax.ShapeDtypeStruct((share, columns), jnp.bfloat16),
            jax.ShapeDtypeStruct((2, share, columns), jnp.bfloat16),
        ],
        scratch_shapes=[pltpu.VMEM((2, share, columns), jnp.bfloat16)] * n_terms
        + [
            pltpu.VMEM((share, columns), jnp.bfloat16),
            pltpu.SemaphoreType.DMA((len(layout) * n_terms + 1,)),
        ],
        compiler_params=pltpu.CompilerParams(vmem_limit_bytes=VMEM_BYTES),
        cost_estimate=COST,
    )(*sum(terms, []), cotangent, *after)


def backward_kernel(n_out, steps, chained, n_after, parts, piece, where, *refs):
    n_slots = where.shape[0]
    g_refs, refs = refs[:n_slots], refs[n_slots:]
    (wg_ref, wu_ref, fg_ref, fu_ref), refs = refs[:4], refs[4:]
    if chained:
        carry_ref, refs = refs[0], refs[1:]
    refs = refs[n_after:]
    o_refs = refs[:n_out]
    g_all, acc, both, sem = refs[n_out:]
    i = pl.program_id(0)
    tile = wg_ref.shape[1]
    rows = acc.shape[1]
    n_parts = len(parts)

    @pl.when(i == 0)
    def _():
        copies = []
        for slot in range(n_slots):
            for n, part in enumerate(parts):
                row = pl.multiple_of((n * n_slots + where[slot]) * piece, piece)
                copies.append(
                    pltpu.make_async_copy(
                        g_refs[slot].at[:, pl.ds(part * piece, piece), :],
                        g_all.at[:, pl.ds(row, piece), :],
                        sem.at[slot * n_parts + n],
                    )
                )
        if chained:
            copies.append(
                pltpu.make_async_copy(
                    carry_ref.at[:, pl.ds(parts[0] * n_slots * piece, rows)],
                    acc,
                    sem.at[n_slots * n_parts],
                )
            )
        else:
            acc[...] = jnp.zeros_like(acc)
        copy_all(copies)

    columns = pl.ds(pl.multiple_of(i * tile, tile), tile)
    both[:, :tile] = masked(wg_ref, fg_ref)
    both[:, tile:] = masked(wu_ref, fu_ref)
    acc[...] += lax.dot_general(
        both[...],
        jnp.concatenate([g_all[0, :, columns], g_all[1, :, columns]], axis=1),
        (((1,), (1,)), ((), ())),
        preferred_element_type=jnp.float32,
    )

    @pl.when(i == steps - 1)
    def _():
        if n_out == 1:
            copy_all([pltpu.make_async_copy(acc, o_refs[0], sem.at[0])])
        else:
            for k in range(n_out):
                size = rows // n_out
                o_refs[k][...] = acc[:, k * size : (k + 1) * size].T.astype(jnp.bfloat16)


def backward(carry, where, pieces, weights, flags, first, tile, parts, planes, after):
    n_slots = where.shape[0]
    width = pieces[0].shape[2]
    piece = pieces[0].shape[1] // TOKEN_PARTS
    rows = piece * len(parts) * n_slots
    depth = weights[0].shape[0]
    tiles = width // tile
    w_spec = pl.BlockSpec((depth, tile), lambda i, s: (0, first + i))
    f_spec = pl.BlockSpec((flags[0].shape[0], tile), lambda i, s: (0, first + i))
    if planes:
        out_specs = [pl.BlockSpec((rows // planes, depth), lambda i, s: (0, 0))] * planes
        out_shape = [jax.ShapeDtypeStruct((rows // planes, depth), jnp.bfloat16)] * planes
    else:
        out_specs = [ANY]
        out_shape = [jax.ShapeDtypeStruct((depth, rows), jnp.float32)]
    chained = carry is not None
    return pl.pallas_call(
        functools.partial(
            backward_kernel, len(out_shape), tiles, chained, len(after), parts, piece
        ),
        grid_spec=pltpu.PrefetchScalarGridSpec(
            num_scalar_prefetch=1,
            grid=(tiles,),
            in_specs=[ANY] * n_slots + [w_spec] * 2 + [f_spec] * 2 + [ANY] * (chained + len(after)),
            out_specs=out_specs,
            scratch_shapes=[
                pltpu.VMEM((2, rows, width), jnp.bfloat16),
                pltpu.VMEM((depth, rows), jnp.float32),
                pltpu.VMEM((depth, 2 * tile), jnp.bfloat16),
                pltpu.SemaphoreType.DMA((rows // piece + 1,)),
            ],
        ),
        out_shape=out_shape,
        compiler_params=pltpu.CompilerParams(vmem_limit_bytes=VMEM_BYTES),
        cost_estimate=pl.CostEstimate(
            flops=6 * rows * depth * width,
            bytes_accessed=4 * depth * width,
            transcendentals=0,
        ),
    )(where, *pieces, *weights, *flags, *((carry,) if chained else ()), *after)


def wide(array):
    return array.astype(jnp.float32)


class ReduceScatter:
    def __init__(self, cube, keep, send):
        self.cube = cube
        self.terms = [keep, cube.sibling(send)]
        self.rows = keep.shape[1]

    def exchange(self, i, after):
        self.rows //= 2
        self.terms[0] = then(self.terms[0], *after)
        rows = self.rows
        moved = sum(wide(t[:, rows : 2 * rows]) for t in self.terms).astype(jnp.bfloat16)
        self.terms.append(self.cube.step(moved, i))
        return moved


class AllGather:
    def __init__(self, cube, own):
        self.cube = cube
        n_dims = len(cube.dims[0])
        self.pieces = [own] + [cube.step(own, n_dims - 1 - i) for i in range(n_dims)]

    def finish(self, *after):
        cube = self.cube
        n_dims = len(cube.dims[0])
        pieces = {0: self.pieces[0]}
        for i in range(n_dims):
            pieces[1 << i] = self.pieces[1 + i]
        pieces = {slot: then(p, *after) for slot, p in pieces.items()}
        for slot in range(1, cube.half):
            if slot not in pieces:
                low = slot & -slot
                pieces[slot] = cube.step(pieces[slot ^ low], n_dims - low.bit_length())
        pieces = [pieces[slot] for slot in range(cube.half)]
        return pieces + [cube.sibling(p) for p in pieces]


def flip(array, bit, size):
    return lax.ppermute(array, "col", [(z, z ^ bit) for z in range(size)])


def gather_planes(x, n_col):
    xs = [x]
    for k in range(1, n_col):
        low = k & -k
        xs.append(flip(xs[k ^ low], low, n_col))
    return xs


def sum_planes(parts, n_col, direct, after):
    terms = [wide(p) for p in parts]
    arrived = list(after)
    for k in range(n_col - 1, 0, -1):
        low = k if direct else k & -k
        sent = terms[k].astype(jnp.bfloat16)
        if not direct:
            sent = then(sent, *arrived)
        moved = flip(sent, low, n_col)
        if direct or low != k:
            arrived.append(moved)
        terms[k ^ low] = terms[k ^ low] + wide(moved)
    return terms[0].astype(jnp.bfloat16), arrived


def shards(cube, n_col, inputs, gate_weight, up_weight, gate_pattern, up_pattern, cotangent):
    depth, local_hidden = gate_weight.shape
    share = cotangent.shape[0]
    tile = local_hidden // sum(BACKWARD)
    weights = (gate_weight, up_weight)
    flags = [
        jnp.repeat(p.astype(jnp.bfloat16), BLOCK, axis=1) for p in (gate_pattern, up_pattern)
    ]
    table = places(cube, n_col)
    row, col = lax.axis_index("row"), lax.axis_index("col")
    where = jnp.asarray(table)[row, col]
    slots = jnp.asarray(np.argsort(table, axis=-1).astype(np.int32))[row, col]

    xs = gather_planes(inputs, n_col)
    units = list(zip(np.cumsum((0,) + FORWARD).tolist(), FORWARD))
    sums, after, moved = [], {}, []
    for n, (first, tiles) in enumerate(units):
        keep, send = forward(
            slots, xs, weights, flags, first, tiles, tile, after.pop(n, [])
        )
        sums.append(ReduceScatter(cube, keep, send))
        after.setdefault(n + 1, []).append(keep)
        moved.append([])
        for i in range(len(cube.dims[0])):
            before = sums[n - 2].terms[-1:] if i == 0 and n > 2 else []
            moved[n].append(sums[n].exchange(i, before))
            after.setdefault(n + 2 + i, []).append(moved[n][-1])
    first_moved = [m[0] for m in moved]

    hidden, gathers, owns = [], [], []
    starts = [sum(BACKWARD[:n]) for n in range(len(BACKWARD))]
    for first, tiles in zip(starts, BACKWARD):
        layout, terms = [], []
        for (start, width), unit in zip(units, sums):
            low, high = max(first, start), min(first + tiles, start + width)
            if low < high:
                layout.append(((low - start) * tile, (low - first) * tile, (high - low) * tile))
                terms.append(unit.terms)
        h, own = derivatives(
            layout, terms, cotangent, first * tile, tiles * tile, owns[-1:] or first_moved
        )
        hidden.append(h)
        owns.append(own)
        gathers.append(AllGather(cube, own))
    everything = tuple(range(TOKEN_PARTS))
    carry = backward(
        None, where, gathers[0].finish(), weights, flags, 0, tile, everything, 0, owns[1:]
    )
    pieces = gathers[1].finish(*carry)
    input_grad, arrived = [], []
    for t in everything:
        last = t == TOKEN_PARTS - 1
        parts = backward(
            carry[0],
            where,
            pieces,
            weights,
            flags,
            starts[1],
            tile,
            (t,),
            n_col,
            parts[:1] if t else [],
        )
        total, arrived = sum_planes(parts, n_col, not last, arrived)
        input_grad.append(total.reshape(-1, 1, share // TOKEN_PARTS, depth))
    return (
        jnp.concatenate(hidden, axis=1),
        jnp.concatenate(input_grad, axis=1).reshape(-1, depth),
    )


def solution(mesh):
    placed = (
        P("col", "row"),
        P("row", "col"),
        P("row", "col"),
        P("row", "col"),
        P("row", "col"),
        P("row", "col"),
    )
    return jax.shard_map(
        functools.partial(shards, Cube(mesh.shape["row"]), mesh.shape["col"]),
        mesh=mesh,
        in_specs=placed,
        out_specs=(P("row", "col"), P("col", "row")),
        check_vma=False,
    )
```

```python
import functools

import jax
import jax.numpy as jnp
import numpy as np
from jax import lax
from jax.experimental import pallas as pl
from jax.experimental.pallas import tpu as pltpu
from jax.sharding import PartitionSpec as P

BLOCK = 128
FORWARD = (2, 3, 4, 4)
BACKWARD = (5, 8)
FEATURE_PARTS = 2
VMEM_BYTES = 48 * 1024 * 1024
ANY = pl.BlockSpec(memory_space=pl.ANY)
COST = pl.CostEstimate(flops=1, bytes_accessed=1, transcendentals=0)


def masked(w_ref, f_ref):
    rows, columns = w_ref.shape
    flags = f_ref[...].reshape(rows // BLOCK, 1, columns)
    return (w_ref[...].reshape(rows // BLOCK, BLOCK, columns) * flags).reshape(rows, columns)


def then(array, *others):
    return lax.optimization_barrier((array, *others))[0]


class Cube:
    def __init__(self, size):
        self.size = size
        self.half = size // 2
        rising = [1 << b for b in range(1, size.bit_length() - 1)]
        self.dims = (rising, rising[::-1])

    def offset(self, parity, slot):
        dims = self.dims[parity]
        digits = [slot >> (len(dims) - 1 - i) & 1 for i in range(len(dims))]
        return int(np.bitwise_xor.reduce([0] + [d for d, on in zip(dims, digits) if on]))

    def owner(self, me, slot):
        if slot >= self.half:
            me, slot = me ^ 1, slot - self.half
        return me ^ self.offset(me & 1, slot)

    def step(self, array, i):
        perm = [(r, r ^ self.dims[r & 1][i]) for r in range(self.size)]
        return lax.ppermute(array, "row", perm)

    def sibling(self, array):
        return lax.ppermute(array, "row", [(r, r ^ 1) for r in range(self.size)])


def places(cube, n_col):
    ratio = cube.size // n_col
    table = np.zeros((cube.size, n_col, cube.size), np.int32)
    for me in range(cube.size):
        for z in range(n_col):
            for slot in range(cube.size):
                d = cube.owner(me, slot)
                table[me, z, slot] = ratio * ((d // ratio) ^ z) + d % ratio
    return table


def copy_all(copies):
    for copy in copies:
        copy.start()
    for copy in copies:
        copy.wait()


def forward_kernel(n_x, n_after, slots, *refs):
    x_refs, refs = refs[:n_x], refs[n_x:]
    wg_ref, wu_ref, fg_ref, fu_ref = refs[:4]
    keep_ref, send_ref, x_all, sem = refs[4 + n_after :]
    half = keep_ref.shape[1]
    shares = slots.shape[0]
    share = 2 * half // shares
    ratio = shares // n_x

    @pl.when(pl.program_id(0) == 0)
    def _():
        copies = []
        for k in range(n_x):
            for c in range(ratio):
                place = k * ratio + c
                row = pl.multiple_of(slots[place] * share, share)
                copies.append(
                    pltpu.make_async_copy(
                        x_refs[k].at[pl.ds(c * share, share), :],
                        x_all.at[pl.ds(row, share), :],
                        sem.at[place],
                    )
                )
        copy_all(copies)

    for n, (w_ref, f_ref) in enumerate(((wg_ref, fg_ref), (wu_ref, fu_ref))):
        out = jnp.dot(x_all[...], masked(w_ref, f_ref), preferred_element_type=jnp.float32)
        out = out.astype(jnp.bfloat16)
        keep_ref[n] = out[:half]
        send_ref[n] = out[half:]


def forward(slots, xs, weights, flags, first, tiles, tile, after):
    depth = weights[0].shape[0]
    rows = len(xs) * xs[0].shape[0]
    w_spec = pl.BlockSpec((depth, tile), lambda i, s: (0, first + i))
    f_spec = pl.BlockSpec((*flags[0].shape[:2], tile), lambda i, s: (0, 0, first + i))
    o_spec = pl.BlockSpec((2, rows // 2, tile), lambda i, s: (0, 0, i))
    out = jax.ShapeDtypeStruct((2, rows // 2, tiles * tile), jnp.bfloat16)
    return pl.pallas_call(
        functools.partial(forward_kernel, len(xs), len(after)),
        grid_spec=pltpu.PrefetchScalarGridSpec(
            num_scalar_prefetch=1,
            grid=(tiles,),
            in_specs=[ANY] * len(xs) + [w_spec] * 2 + [f_spec] * 2 + [ANY] * len(after),
            out_specs=[o_spec, o_spec],
            scratch_shapes=[
                pltpu.VMEM((rows, depth), jnp.bfloat16),
                pltpu.SemaphoreType.DMA((slots.shape[0],)),
            ],
        ),
        out_shape=[out, out],
        compiler_params=pltpu.CompilerParams(vmem_limit_bytes=VMEM_BYTES),
        cost_estimate=pl.CostEstimate(
            flops=8 * rows * depth * tiles * tile,
            bytes_accessed=4 * depth * tiles * tile,
            transcendentals=0,
        ),
    )(slots, *xs, *weights, *flags, *after)


def derivatives_kernel(first, layout, n_terms, *refs):
    sources, cot_ref = refs[: len(layout) * n_terms], refs[len(layout) * n_terms]
    h_ref, g_ref = refs[-4 - n_terms : -2 - n_terms]
    held = refs[-2 - n_terms : -2]
    cot, sem = refs[-2:]
    share, columns = h_ref.shape
    copies = []
    for m, (source, place, width) in enumerate(layout):
        for n in range(n_terms):
            copies.append(
                pltpu.make_async_copy(
                    sources[m * n_terms + n].at[:, pl.ds(0, share), pl.ds(source, width)],
                    held[n].at[:, :, pl.ds(place, width)],
                    sem.at[m * n_terms + n],
                )
            )
    copies.append(
        pltpu.make_async_copy(
            cot_ref.at[:, pl.ds(first, columns)], cot, sem.at[len(layout) * n_terms]
        )
    )
    copy_all(copies)
    step = 256
    for c in range(0, columns, step):
        at = slice(c, c + step)
        gate_sum = sum(wide(v[0, :, at]) for v in held)
        up_sum = sum(wide(v[1, :, at]) for v in held)
        cotangent = wide(cot[:, at])
        sigmoid_gate = jax.nn.sigmoid(gate_sum)
        activated = gate_sum * sigmoid_gate
        h_ref[:, at] = (activated * up_sum).astype(jnp.bfloat16)
        g_ref[0, :, at] = (
            cotangent * up_sum * sigmoid_gate * (1.0 + gate_sum * (1.0 - sigmoid_gate))
        ).astype(jnp.bfloat16)
        g_ref[1, :, at] = (cotangent * activated).astype(jnp.bfloat16)


def derivatives(layout, terms, cotangent, first, columns, after):
    share = cotangent.shape[0]
    n_terms = len(terms[0])
    return pl.pallas_call(
        functools.partial(derivatives_kernel, first, layout, n_terms),
        in_specs=[ANY] * (len(layout) * n_terms + 1 + len(after)),
        out_specs=[pl.BlockSpec(memory_space=pltpu.VMEM)] * 2,
        out_shape=[
            jax.ShapeDtypeStruct((share, columns), jnp.bfloat16),
            jax.ShapeDtypeStruct((2, share, columns), jnp.bfloat16),
        ],
        scratch_shapes=[pltpu.VMEM((2, share, columns), jnp.bfloat16)] * n_terms
        + [
            pltpu.VMEM((share, columns), jnp.bfloat16),
            pltpu.SemaphoreType.DMA((len(layout) * n_terms + 1,)),
        ],
        compiler_params=pltpu.CompilerParams(vmem_limit_bytes=VMEM_BYTES),
        cost_estimate=COST,
    )(*sum(terms, []), cotangent, *after)


def backward_kernel(n_out, steps, chained, n_after, part, where, *refs):
    n_slots = where.shape[0]
    g_refs, refs = refs[:n_slots], refs[n_slots:]
    (wg_ref, wu_ref, fg_ref, fu_ref), refs = refs[:4], refs[4:]
    if chained:
        carry_ref, refs = refs[0], refs[1:]
    refs = refs[n_after:]
    o_refs = refs[:n_out]
    g_all, acc, both, sem = refs[n_out:]
    i = pl.program_id(0)
    tile = wg_ref.shape[1]
    depth, rows = acc.shape
    share = rows // n_slots

    @pl.when(i == 0)
    def _():
        copies = []
        for slot in range(n_slots):
            row = pl.multiple_of(where[slot] * share, share)
            copies.append(
                pltpu.make_async_copy(
                    g_refs[slot], g_all.at[:, pl.ds(row, share), :], sem.at[slot]
                )
            )
        if chained:
            copies.append(
                pltpu.make_async_copy(
                    carry_ref.at[pl.ds(part * depth, depth), :], acc, sem.at[n_slots]
                )
            )
        else:
            acc[...] = jnp.zeros_like(acc)
        copy_all(copies)

    columns = pl.ds(pl.multiple_of(i * tile, tile), tile)
    both[:, :tile] = masked(wg_ref, fg_ref)
    both[:, tile:] = masked(wu_ref, fu_ref)
    acc[...] += lax.dot_general(
        both[...],
        jnp.concatenate([g_all[0, :, columns], g_all[1, :, columns]], axis=1),
        (((1,), (1,)), ((), ())),
        preferred_element_type=jnp.float32,
    )

    @pl.when(i == steps - 1)
    def _():
        if n_out == 1:
            copy_all([pltpu.make_async_copy(acc, o_refs[0], sem.at[0])])
        else:
            for k in range(n_out):
                size = rows // n_out
                o_refs[k][...] = acc[:, k * size : (k + 1) * size].T.astype(jnp.bfloat16)


def backward(carry, where, pieces, weights, flags, first, tile, part, planes, after):
    n_slots = where.shape[0]
    width = pieces[0].shape[2]
    rows = pieces[0].shape[1] * n_slots
    depth = weights[0].shape[0]
    f_parts = FEATURE_PARTS
    if part is not None:
        depth, f_parts = depth // FEATURE_PARTS, 1
    row = part or 0
    tiles = width // tile
    w_spec = pl.BlockSpec((depth, tile), lambda i, s: (row, first + i))
    f_spec = pl.BlockSpec(
        (f_parts, flags[0].shape[1], tile), lambda i, s: (row, 0, first + i)
    )
    if planes:
        out_specs = [pl.BlockSpec((rows // planes, depth), lambda i, s: (0, 0))] * planes
        out_shape = [jax.ShapeDtypeStruct((rows // planes, depth), jnp.bfloat16)] * planes
    else:
        out_specs = [ANY]
        out_shape = [jax.ShapeDtypeStruct((depth, rows), jnp.float32)]
    chained = carry is not None
    return pl.pallas_call(
        functools.partial(
            backward_kernel, len(out_shape), tiles, chained, len(after), part
        ),
        grid_spec=pltpu.PrefetchScalarGridSpec(
            num_scalar_prefetch=1,
            grid=(tiles,),
            in_specs=[ANY] * n_slots + [w_spec] * 2 + [f_spec] * 2 + [ANY] * (chained + len(after)),
            out_specs=out_specs,
            scratch_shapes=[
                pltpu.VMEM((2, rows, width), jnp.bfloat16),
                pltpu.VMEM((depth, rows), jnp.float32),
                pltpu.VMEM((depth, 2 * tile), jnp.bfloat16),
                pltpu.SemaphoreType.DMA((n_slots + 1,)),
            ],
        ),
        out_shape=out_shape,
        compiler_params=pltpu.CompilerParams(vmem_limit_bytes=VMEM_BYTES),
        cost_estimate=pl.CostEstimate(
            flops=6 * rows * depth * width,
            bytes_accessed=4 * depth * width,
            transcendentals=0,
        ),
    )(where, *pieces, *weights, *flags, *((carry,) if chained else ()), *after)


def wide(array):
    return array.astype(jnp.float32)


class ReduceScatter:
    def __init__(self, cube, keep, send):
        self.cube = cube
        self.terms = [keep, cube.sibling(send)]
        self.rows = keep.shape[1]

    def exchange(self, i, after):
        self.rows //= 2
        self.terms[0] = then(self.terms[0], *after)
        rows = self.rows
        moved = sum(wide(t[:, rows : 2 * rows]) for t in self.terms).astype(jnp.bfloat16)
        self.terms.append(self.cube.step(moved, i))
        if i == 0:
            self.first = self.terms[-1]
        return moved


class AllGather:
    def __init__(self, cube, own, *after):
        self.cube = cube
        n_dims = len(cube.dims[0])
        own = then(own, *after)
        self.pieces = [own] + [cube.step(own, n_dims - 1 - i) for i in range(n_dims)]

    def finish(self, *after):
        cube = self.cube
        n_dims = len(cube.dims[0])
        pieces = {0: self.pieces[0]}
        for i in range(n_dims):
            pieces[1 << i] = self.pieces[1 + i]
        pieces = {slot: then(p, *after) for slot, p in pieces.items()}
        for slot in range(1, cube.half):
            if slot not in pieces:
                low = slot & -slot
                pieces[slot] = cube.step(pieces[slot ^ low], n_dims - low.bit_length())
        pieces = [pieces[slot] for slot in range(cube.half)]
        return pieces + [cube.sibling(p) for p in pieces]


def flip(array, bit, size):
    return lax.ppermute(array, "col", [(z, z ^ bit) for z in range(size)])


def gather_planes(x, n_col):
    xs = [x]
    for k in range(1, n_col):
        low = k & -k
        xs.append(flip(xs[k ^ low], low, n_col))
    return xs


def sum_planes(parts, n_col, direct, after):
    terms = [wide(p) for p in parts]
    arrived = list(after)
    for k in range(n_col - 1, 0, -1):
        low = k if direct else k & -k
        sent = terms[k].astype(jnp.bfloat16)
        if not direct:
            sent = then(sent, *arrived)
        moved = flip(sent, low, n_col)
        if direct or low != k:
            arrived.append(moved)
        terms[k ^ low] = terms[k ^ low] + wide(moved)
    return terms[0].astype(jnp.bfloat16), arrived


def shards(cube, n_col, inputs, gate_weight, up_weight, gate_pattern, up_pattern, cotangent):
    depth, local_hidden = gate_weight.shape
    share = cotangent.shape[0]
    tile = local_hidden // sum(BACKWARD)
    weights = (gate_weight, up_weight)
    flags = [
        jnp.repeat(p.astype(jnp.bfloat16), BLOCK, axis=1).reshape(
            FEATURE_PARTS, -1, local_hidden
        )
        for p in (gate_pattern, up_pattern)
    ]
    table = places(cube, n_col)
    row, col = lax.axis_index("row"), lax.axis_index("col")
    where = jnp.asarray(table)[row, col]
    slots = jnp.asarray(np.argsort(table, axis=-1).astype(np.int32))[row, col]

    xs = gather_planes(inputs, n_col)
    units = list(zip(np.cumsum((0,) + FORWARD).tolist(), FORWARD))
    sums, after, moved = [], {}, []
    for n, (first, tiles) in enumerate(units):
        keep, send = forward(
            slots, xs, weights, flags, first, tiles, tile, after.pop(n, [])
        )
        sums.append(ReduceScatter(cube, keep, send))
        after.setdefault(n + 1, []).append(keep)
        moved.append([])
        for i in range(len(cube.dims[0])):
            before = []
            if i == 1 and n == 1:
                before = sums[0].terms[-1:]
            elif i == 0 and n == 2:
                before = moved[1][-1:]
            elif i == 0 and n == 3:
                before = [sums[2].first, sums[0].terms[-1], sums[1].terms[-1]]
            elif i == 1 and n == 3:
                before = sums[2].terms[-1:]
            moved[n].append(sums[n].exchange(i, before))
            after.setdefault(n + 2 + i, []).append(moved[n][-1])
    first_moved = [m[0] for m in moved]

    hidden, gathers, owns = [], [], []
    starts = [sum(BACKWARD[:n]) for n in range(len(BACKWARD))]
    for first, tiles in zip(starts, BACKWARD):
        layout, terms = [], []
        for (start, width), unit in zip(units, sums):
            low, high = max(first, start), min(first + tiles, start + width)
            if low < high:
                layout.append(((low - start) * tile, (low - first) * tile, (high - low) * tile))
                terms.append(unit.terms)
        h, own = derivatives(
            layout, terms, cotangent, first * tile, tiles * tile, owns[-1:] or first_moved
        )
        hidden.append(h)
        owns.append(own)
        gathers.append(AllGather(cube, own, moved[-1][-1]))
    carry = backward(
        None, where, gathers[0].finish(*[u.terms[-1] for u in sums]), weights, flags, 0, tile, None, 0, owns[1:]
    )
    pieces = gathers[1].finish(*carry)
    input_grad, arrived, parts = [], [], []
    for part in range(FEATURE_PARTS):
        parts = backward(
            carry[0],
            where,
            pieces,
            weights,
            flags,
            starts[1],
            tile,
            part,
            n_col,
            parts[:1],
        )
        total, arrived = sum_planes(parts, n_col, part < FEATURE_PARTS - 1, arrived)
        input_grad.append(total)
    return jnp.concatenate(hidden, axis=1), jnp.concatenate(input_grad, axis=1)


def solution(mesh):
    placed = (
        P("col", "row"),
        P("row", "col"),
        P("row", "col"),
        P("row", "col"),
        P("row", "col"),
        P("row", "col"),
    )
    return jax.shard_map(
        functools.partial(shards, Cube(mesh.shape["row"]), mesh.shape["col"]),
        mesh=mesh,
        in_specs=placed,
        out_specs=(P("row", "col"), P("col", "row")),
        check_vma=False,
    )
```

```python
import functools

import jax
import jax.numpy as jnp
import numpy as np
from jax import lax
from jax.experimental import pallas as pl
from jax.experimental.pallas import tpu as pltpu
from jax.sharding import PartitionSpec as P

BLOCK = 128
FORWARD = (4, 4, 3, 2)
BACKWARD = (5, 8)
FEATURE_PARTS = 2
VMEM_BYTES = 48 * 1024 * 1024
ANY = pl.BlockSpec(memory_space=pl.ANY)
COST = pl.CostEstimate(flops=1, bytes_accessed=1, transcendentals=0)


def masked(w_ref, f_ref):
    rows, columns = w_ref.shape
    flags = f_ref[...].reshape(rows // BLOCK, 1, columns)
    return (w_ref[...].reshape(rows // BLOCK, BLOCK, columns) * flags).reshape(rows, columns)


def then(array, *others):
    return lax.optimization_barrier((array, *others))[0]


class Cube:
    def __init__(self, size):
        self.size = size
        self.half = size // 2
        rising = [1 << b for b in range(1, size.bit_length() - 1)]
        self.dims = (rising, rising[::-1])

    def offset(self, parity, slot):
        dims = self.dims[parity]
        digits = [slot >> (len(dims) - 1 - i) & 1 for i in range(len(dims))]
        return int(np.bitwise_xor.reduce([0] + [d for d, on in zip(dims, digits) if on]))

    def owner(self, me, slot):
        if slot >= self.half:
            me, slot = me ^ 1, slot - self.half
        return me ^ self.offset(me & 1, slot)

    def step(self, array, i):
        perm = [(r, r ^ self.dims[r & 1][i]) for r in range(self.size)]
        return lax.ppermute(array, "row", perm)

    def sibling(self, array):
        return lax.ppermute(array, "row", [(r, r ^ 1) for r in range(self.size)])


def places(cube, n_col):
    ratio = cube.size // n_col
    table = np.zeros((cube.size, n_col, cube.size), np.int32)
    for me in range(cube.size):
        for z in range(n_col):
            for slot in range(cube.size):
                d = cube.owner(me, slot)
                table[me, z, slot] = ratio * ((d // ratio) ^ z) + d % ratio
    return table


def copy_all(copies):
    for copy in copies:
        copy.start()
    for copy in copies:
        copy.wait()


def forward_kernel(n_x, n_after, slots, *refs):
    x_refs, refs = refs[:n_x], refs[n_x:]
    wg_ref, wu_ref, fg_ref, fu_ref = refs[:4]
    keep_ref, send_ref, x_all, sem = refs[4 + n_after :]
    half = keep_ref.shape[1]
    shares = slots.shape[0]
    share = 2 * half // shares
    ratio = shares // n_x

    @pl.when(pl.program_id(0) == 0)
    def _():
        copies = []
        for k in range(n_x):
            for c in range(ratio):
                place = k * ratio + c
                row = pl.multiple_of(slots[place] * share, share)
                copies.append(
                    pltpu.make_async_copy(
                        x_refs[k].at[pl.ds(c * share, share), :],
                        x_all.at[pl.ds(row, share), :],
                        sem.at[place],
                    )
                )
        copy_all(copies)

    for n, (w_ref, f_ref) in enumerate(((wg_ref, fg_ref), (wu_ref, fu_ref))):
        out = jnp.dot(x_all[...], masked(w_ref, f_ref), preferred_element_type=jnp.float32)
        out = out.astype(jnp.bfloat16)
        keep_ref[n] = out[:half]
        send_ref[n] = out[half:]


def forward(slots, xs, weights, flags, first, tiles, tile, after):
    depth = weights[0].shape[0]
    rows = len(xs) * xs[0].shape[0]
    w_spec = pl.BlockSpec((depth, tile), lambda i, s: (0, first + i))
    f_spec = pl.BlockSpec((*flags[0].shape[:2], tile), lambda i, s: (0, 0, first + i))
    o_spec = pl.BlockSpec((2, rows // 2, tile), lambda i, s: (0, 0, i))
    out = jax.ShapeDtypeStruct((2, rows // 2, tiles * tile), jnp.bfloat16)
    return pl.pallas_call(
        functools.partial(forward_kernel, len(xs), len(after)),
        grid_spec=pltpu.PrefetchScalarGridSpec(
            num_scalar_prefetch=1,
            grid=(tiles,),
            in_specs=[ANY] * len(xs) + [w_spec] * 2 + [f_spec] * 2 + [ANY] * len(after),
            out_specs=[o_spec, o_spec],
            scratch_shapes=[
                pltpu.VMEM((rows, depth), jnp.bfloat16),
                pltpu.SemaphoreType.DMA((slots.shape[0],)),
            ],
        ),
        out_shape=[out, out],
        compiler_params=pltpu.CompilerParams(vmem_limit_bytes=VMEM_BYTES),
        cost_estimate=pl.CostEstimate(
            flops=8 * rows * depth * tiles * tile,
            bytes_accessed=4 * depth * tiles * tile,
            transcendentals=0,
        ),
    )(slots, *xs, *weights, *flags, *after)


def derivatives_kernel(first, layout, n_terms, *refs):
    sources, cot_ref = refs[: len(layout) * n_terms], refs[len(layout) * n_terms]
    h_ref, g_ref = refs[-4 - n_terms : -2 - n_terms]
    held = refs[-2 - n_terms : -2]
    cot, sem = refs[-2:]
    share, columns = h_ref.shape
    copies = []
    for m, (source, place, width) in enumerate(layout):
        for n in range(n_terms):
            copies.append(
                pltpu.make_async_copy(
                    sources[m * n_terms + n].at[:, pl.ds(0, share), pl.ds(source, width)],
                    held[n].at[:, :, pl.ds(place, width)],
                    sem.at[m * n_terms + n],
                )
            )
    copies.append(
        pltpu.make_async_copy(
            cot_ref.at[:, pl.ds(first, columns)], cot, sem.at[len(layout) * n_terms]
        )
    )
    copy_all(copies)
    step = 256
    for c in range(0, columns, step):
        at = slice(c, c + step)
        gate_sum = sum(wide(v[0, :, at]) for v in held)
        up_sum = sum(wide(v[1, :, at]) for v in held)
        cotangent = wide(cot[:, at])
        sigmoid_gate = jax.nn.sigmoid(gate_sum)
        activated = gate_sum * sigmoid_gate
        h_ref[:, at] = (activated * up_sum).astype(jnp.bfloat16)
        g_ref[0, :, at] = (
            cotangent * up_sum * sigmoid_gate * (1.0 + gate_sum * (1.0 - sigmoid_gate))
        ).astype(jnp.bfloat16)
        g_ref[1, :, at] = (cotangent * activated).astype(jnp.bfloat16)


def derivatives(layout, terms, cotangent, first, columns, after):
    share = cotangent.shape[0]
    n_terms = len(terms[0])
    return pl.pallas_call(
        functools.partial(derivatives_kernel, first, layout, n_terms),
        in_specs=[ANY] * (len(layout) * n_terms + 1 + len(after)),
        out_specs=[pl.BlockSpec(memory_space=pltpu.VMEM)] * 2,
        out_shape=[
            jax.ShapeDtypeStruct((share, columns), jnp.bfloat16),
            jax.ShapeDtypeStruct((2, share, columns), jnp.bfloat16),
        ],
        scratch_shapes=[pltpu.VMEM((2, share, columns), jnp.bfloat16)] * n_terms
        + [
            pltpu.VMEM((share, columns), jnp.bfloat16),
            pltpu.SemaphoreType.DMA((len(layout) * n_terms + 1,)),
        ],
        compiler_params=pltpu.CompilerParams(vmem_limit_bytes=VMEM_BYTES),
        cost_estimate=COST,
    )(*sum(terms, []), cotangent, *after)


def backward_kernel(n_out, steps, chained, n_after, part, where, *refs):
    n_slots = where.shape[0]
    g_refs, refs = refs[:n_slots], refs[n_slots:]
    (wg_ref, wu_ref, fg_ref, fu_ref), refs = refs[:4], refs[4:]
    if chained:
        carry_ref, refs = refs[0], refs[1:]
    refs = refs[n_after:]
    o_refs = refs[:n_out]
    g_all, acc, both, sem = refs[n_out:]
    i = pl.program_id(0)
    tile = wg_ref.shape[1]
    depth, rows = acc.shape
    share = rows // n_slots

    @pl.when(i == 0)
    def _():
        copies = []
        for slot in range(n_slots):
            row = pl.multiple_of(where[slot] * share, share)
            copies.append(
                pltpu.make_async_copy(
                    g_refs[slot], g_all.at[:, pl.ds(row, share), :], sem.at[slot]
                )
            )
        if chained:
            copies.append(
                pltpu.make_async_copy(
                    carry_ref.at[pl.ds(part * depth, depth), :], acc, sem.at[n_slots]
                )
            )
        else:
            acc[...] = jnp.zeros_like(acc)
        copy_all(copies)

    columns = pl.ds(pl.multiple_of(i * tile, tile), tile)
    both[:, :tile] = masked(wg_ref, fg_ref)
    both[:, tile:] = masked(wu_ref, fu_ref)
    acc[...] += lax.dot_general(
        both[...],
        jnp.concatenate([g_all[0, :, columns], g_all[1, :, columns]], axis=1),
        (((1,), (1,)), ((), ())),
        preferred_element_type=jnp.float32,
    )

    @pl.when(i == steps - 1)
    def _():
        if n_out == 1:
            copy_all([pltpu.make_async_copy(acc, o_refs[0], sem.at[0])])
        else:
            for k in range(n_out):
                size = rows // n_out
                o_refs[k][...] = acc[:, k * size : (k + 1) * size].T.astype(jnp.bfloat16)


def backward(carry, where, pieces, weights, flags, first, tile, part, planes, after):
    n_slots = where.shape[0]
    width = pieces[0].shape[2]
    rows = pieces[0].shape[1] * n_slots
    depth = weights[0].shape[0]
    f_parts = FEATURE_PARTS
    if part is not None:
        depth, f_parts = depth // FEATURE_PARTS, 1
    row = part or 0
    tiles = width // tile
    w_spec = pl.BlockSpec((depth, tile), lambda i, s: (row, first + i))
    f_spec = pl.BlockSpec(
        (f_parts, flags[0].shape[1], tile), lambda i, s: (row, 0, first + i)
    )
    if planes:
        out_specs = [pl.BlockSpec((rows // planes, depth), lambda i, s: (0, 0))] * planes
        out_shape = [jax.ShapeDtypeStruct((rows // planes, depth), jnp.bfloat16)] * planes
    else:
        out_specs = [ANY]
        out_shape = [jax.ShapeDtypeStruct((depth, rows), jnp.float32)]
    chained = carry is not None
    return pl.pallas_call(
        functools.partial(
            backward_kernel, len(out_shape), tiles, chained, len(after), part
        ),
        grid_spec=pltpu.PrefetchScalarGridSpec(
            num_scalar_prefetch=1,
            grid=(tiles,),
            in_specs=[ANY] * n_slots + [w_spec] * 2 + [f_spec] * 2 + [ANY] * (chained + len(after)),
            out_specs=out_specs,
            scratch_shapes=[
                pltpu.VMEM((2, rows, width), jnp.bfloat16),
                pltpu.VMEM((depth, rows), jnp.float32),
                pltpu.VMEM((depth, 2 * tile), jnp.bfloat16),
                pltpu.SemaphoreType.DMA((n_slots + 1,)),
            ],
        ),
        out_shape=out_shape,
        compiler_params=pltpu.CompilerParams(vmem_limit_bytes=VMEM_BYTES),
        cost_estimate=pl.CostEstimate(
            flops=6 * rows * depth * width,
            bytes_accessed=4 * depth * width,
            transcendentals=0,
        ),
    )(where, *pieces, *weights, *flags, *((carry,) if chained else ()), *after)


def wide(array):
    return array.astype(jnp.float32)


class ReduceScatter:
    def __init__(self, cube, keep, send):
        self.cube = cube
        self.terms = [keep, cube.sibling(send)]
        self.rows = keep.shape[1]

    def exchange(self, i, after):
        self.rows //= 2
        self.terms[0] = then(self.terms[0], *after)
        rows = self.rows
        moved = sum(wide(t[:, rows : 2 * rows]) for t in self.terms).astype(jnp.bfloat16)
        self.terms.append(self.cube.step(moved, i))
        if i == 0:
            self.first = self.terms[-1]
        return moved


class AllGather:
    def __init__(self, cube, own, *after):
        self.cube = cube
        n_dims = len(cube.dims[0])
        own = then(own, *after)
        self.pieces = [own] + [cube.step(own, n_dims - 1 - i) for i in range(n_dims)]

    def finish(self, *after):
        cube = self.cube
        n_dims = len(cube.dims[0])
        pieces = {0: self.pieces[0]}
        for i in range(n_dims):
            pieces[1 << i] = self.pieces[1 + i]
        pieces = {slot: then(p, *after) for slot, p in pieces.items()}
        for slot in range(1, cube.half):
            if slot not in pieces:
                low = slot & -slot
                pieces[slot] = cube.step(pieces[slot ^ low], n_dims - low.bit_length())
        pieces = [pieces[slot] for slot in range(cube.half)]
        return pieces + [cube.sibling(p) for p in pieces]


def flip(array, bit, size):
    return lax.ppermute(array, "col", [(z, z ^ bit) for z in range(size)])


def gather_planes(x, n_col):
    xs = [x]
    for k in range(1, n_col):
        low = k & -k
        xs.append(flip(xs[k ^ low], low, n_col))
    return xs


def sum_planes(parts, n_col, direct, after):
    terms = [wide(p) for p in parts]
    arrived = list(after)
    for k in range(n_col - 1, 0, -1):
        low = k if direct else k & -k
        sent = terms[k].astype(jnp.bfloat16)
        if not direct:
            sent = then(sent, *arrived)
        moved = flip(sent, low, n_col)
        if direct or low != k:
            arrived.append(moved)
        terms[k ^ low] = terms[k ^ low] + wide(moved)
    return terms[0].astype(jnp.bfloat16), arrived


def shards(cube, n_col, inputs, gate_weight, up_weight, gate_pattern, up_pattern, cotangent):
    depth, local_hidden = gate_weight.shape
    share = cotangent.shape[0]
    tile = local_hidden // sum(BACKWARD)
    weights = (gate_weight, up_weight)
    flags = [
        jnp.repeat(p.astype(jnp.bfloat16), BLOCK, axis=1).reshape(
            FEATURE_PARTS, -1, local_hidden
        )
        for p in (gate_pattern, up_pattern)
    ]
    table = places(cube, n_col)
    row, col = lax.axis_index("row"), lax.axis_index("col")
    where = jnp.asarray(table)[row, col]
    slots = jnp.asarray(np.argsort(table, axis=-1).astype(np.int32))[row, col]

    xs = gather_planes(inputs, n_col)
    units = list(zip(np.cumsum((0,) + FORWARD).tolist(), FORWARD))
    sums, after, moved = [], {}, []
    for n, (first, tiles) in enumerate(units):
        keep, send = forward(
            slots, xs, weights, flags, first, tiles, tile, after.pop(n, [])
        )
        sums.append(ReduceScatter(cube, keep, send))
        after.setdefault(n + 1, []).append(keep)
        moved.append([])
        for i in range(len(cube.dims[0])):
            before = []
            if i == 1 and n == 1:
                before = sums[0].terms[-1:]
            elif i == 0 and n == 2:
                before = moved[1][-1:]
            elif i == 0 and n == 3:
                before = [sums[2].first, sums[0].terms[-1], sums[1].terms[-1]]
            elif i == 1 and n == 3:
                before = sums[2].terms[-1:]
            moved[n].append(sums[n].exchange(i, before))
            after.setdefault(n + 2 + i, []).append(moved[n][-1])
    first_moved = [m[0] for m in moved]

    hidden, gathers, owns = [], [], []
    starts = [sum(BACKWARD[:n]) for n in range(len(BACKWARD))]
    for first, tiles in zip(starts, BACKWARD):
        layout, terms = [], []
        for (start, width), unit in zip(units, sums):
            low, high = max(first, start), min(first + tiles, start + width)
            if low < high:
                layout.append(((low - start) * tile, (low - first) * tile, (high - low) * tile))
                terms.append(unit.terms)
        h, own = derivatives(
            layout, terms, cotangent, first * tile, tiles * tile, owns[-1:] or first_moved
        )
        hidden.append(h)
        owns.append(own)
        gathers.append(AllGather(cube, own, moved[-1][0]))
    carry = backward(
        None, where, gathers[0].finish(*[u.terms[-1] for u in sums]), weights, flags, 0, tile, None, 0, owns[1:]
    )
    pieces = gathers[1].finish(*carry)
    input_grad, arrived, parts = [], [], []
    for part in range(FEATURE_PARTS):
        parts = backward(
            carry[0],
            where,
            pieces,
            weights,
            flags,
            starts[1],
            tile,
            part,
            n_col,
            parts[:1],
        )
        total, arrived = sum_planes(parts, n_col, part < FEATURE_PARTS - 1, arrived)
        input_grad.append(total)
    return jnp.concatenate(hidden, axis=1), jnp.concatenate(input_grad, axis=1)


def solution(mesh):
    placed = (
        P("col", "row"),
        P("row", "col"),
        P("row", "col"),
        P("row", "col"),
        P("row", "col"),
        P("row", "col"),
    )
    return jax.shard_map(
        functools.partial(shards, Cube(mesh.shape["row"]), mesh.shape["col"]),
        mesh=mesh,
        in_specs=placed,
        out_specs=(P("row", "col"), P("col", "row")),
        check_vma=False,
    )
```

```python
import functools

import jax
import jax.numpy as jnp
import numpy as np
from jax import lax
from jax.experimental import pallas as pl
from jax.experimental.pallas import tpu as pltpu
from jax.sharding import PartitionSpec as P

BLOCK = 128
FORWARD = (2, 3, 4, 4)
BACKWARD = (5, 8)
FEATURE_PARTS = 2
VMEM_BYTES = 48 * 1024 * 1024
ANY = pl.BlockSpec(memory_space=pl.ANY)
COST = pl.CostEstimate(flops=1, bytes_accessed=1, transcendentals=0)


def masked(w_ref, f_ref):
    rows, columns = w_ref.shape
    flags = f_ref[...].reshape(rows // BLOCK, 1, columns)
    return (w_ref[...].reshape(rows // BLOCK, BLOCK, columns) * flags).reshape(rows, columns)


def then(array, *others):
    return lax.optimization_barrier((array, *others))[0]


class Cube:
    def __init__(self, size):
        self.size = size
        self.half = size // 2
        rising = [1 << b for b in range(1, size.bit_length() - 1)]
        self.dims = (rising, rising[::-1])

    def offset(self, parity, slot):
        dims = self.dims[parity]
        digits = [slot >> (len(dims) - 1 - i) & 1 for i in range(len(dims))]
        return int(np.bitwise_xor.reduce([0] + [d for d, on in zip(dims, digits) if on]))

    def owner(self, me, slot):
        if slot >= self.half:
            me, slot = me ^ 1, slot - self.half
        return me ^ self.offset(me & 1, slot)

    def step(self, array, i):
        perm = [(r, r ^ self.dims[r & 1][i]) for r in range(self.size)]
        return lax.ppermute(array, "row", perm)

    def sibling(self, array):
        return lax.ppermute(array, "row", [(r, r ^ 1) for r in range(self.size)])


def places(cube, n_col):
    ratio = cube.size // n_col
    table = np.zeros((cube.size, n_col, cube.size), np.int32)
    for me in range(cube.size):
        for z in range(n_col):
            for slot in range(cube.size):
                d = cube.owner(me, slot)
                table[me, z, slot] = ratio * ((d // ratio) ^ z) + d % ratio
    return table


def copy_all(copies):
    for copy in copies:
        copy.start()
    for copy in copies:
        copy.wait()


def forward_kernel(n_x, n_after, slots, *refs):
    x_refs, refs = refs[:n_x], refs[n_x:]
    wg_ref, wu_ref, fg_ref, fu_ref = refs[:4]
    keep_ref, send_ref, x_all, sem = refs[4 + n_after :]
    half = keep_ref.shape[1]
    shares = slots.shape[0]
    share = 2 * half // shares
    ratio = shares // n_x

    @pl.when(pl.program_id(0) == 0)
    def _():
        copies = []
        for k in range(n_x):
            for c in range(ratio):
                place = k * ratio + c
                row = pl.multiple_of(slots[place] * share, share)
                copies.append(
                    pltpu.make_async_copy(
                        x_refs[k].at[pl.ds(c * share, share), :],
                        x_all.at[pl.ds(row, share), :],
                        sem.at[place],
                    )
                )
        copy_all(copies)

    for n, (w_ref, f_ref) in enumerate(((wg_ref, fg_ref), (wu_ref, fu_ref))):
        out = jnp.dot(x_all[...], masked(w_ref, f_ref), preferred_element_type=jnp.float32)
        out = out.astype(jnp.bfloat16)
        keep_ref[n] = out[:half]
        send_ref[n] = out[half:]


def forward(slots, xs, weights, flags, first, tiles, tile, after):
    depth = weights[0].shape[0]
    rows = len(xs) * xs[0].shape[0]
    w_spec = pl.BlockSpec((depth, tile), lambda i, s: (0, first + i))
    f_spec = pl.BlockSpec((*flags[0].shape[:2], tile), lambda i, s: (0, 0, first + i))
    o_spec = pl.BlockSpec((2, rows // 2, tile), lambda i, s: (0, 0, i))
    out = jax.ShapeDtypeStruct((2, rows // 2, tiles * tile), jnp.bfloat16)
    return pl.pallas_call(
        functools.partial(forward_kernel, len(xs), len(after)),
        grid_spec=pltpu.PrefetchScalarGridSpec(
            num_scalar_prefetch=1,
            grid=(tiles,),
            in_specs=[ANY] * len(xs) + [w_spec] * 2 + [f_spec] * 2 + [ANY] * len(after),
            out_specs=[o_spec, o_spec],
            scratch_shapes=[
                pltpu.VMEM((rows, depth), jnp.bfloat16),
                pltpu.SemaphoreType.DMA((slots.shape[0],)),
            ],
        ),
        out_shape=[out, out],
        compiler_params=pltpu.CompilerParams(vmem_limit_bytes=VMEM_BYTES),
        cost_estimate=pl.CostEstimate(
            flops=8 * rows * depth * tiles * tile,
            bytes_accessed=4 * depth * tiles * tile,
            transcendentals=0,
        ),
    )(slots, *xs, *weights, *flags, *after)


def derivatives_kernel(first, layout, n_terms, *refs):
    sources, cot_ref = refs[: len(layout) * n_terms], refs[len(layout) * n_terms]
    h_ref, g_ref = refs[-4 - n_terms : -2 - n_terms]
    held = refs[-2 - n_terms : -2]
    cot, sem = refs[-2:]
    share, columns = h_ref.shape
    copies = []
    for m, (source, place, width) in enumerate(layout):
        for n in range(n_terms):
            copies.append(
                pltpu.make_async_copy(
                    sources[m * n_terms + n].at[:, pl.ds(0, share), pl.ds(source, width)],
                    held[n].at[:, :, pl.ds(place, width)],
                    sem.at[m * n_terms + n],
                )
            )
    copies.append(
        pltpu.make_async_copy(
            cot_ref.at[:, pl.ds(first, columns)], cot, sem.at[len(layout) * n_terms]
        )
    )
    copy_all(copies)
    step = 256
    for c in range(0, columns, step):
        at = slice(c, c + step)
        gate_sum = sum(wide(v[0, :, at]) for v in held)
        up_sum = sum(wide(v[1, :, at]) for v in held)
        cotangent = wide(cot[:, at])
        sigmoid_gate = jax.nn.sigmoid(gate_sum)
        activated = gate_sum * sigmoid_gate
        h_ref[:, at] = (activated * up_sum).astype(jnp.bfloat16)
        g_ref[0, :, at] = (
            cotangent * up_sum * sigmoid_gate * (1.0 + gate_sum * (1.0 - sigmoid_gate))
        ).astype(jnp.bfloat16)
        g_ref[1, :, at] = (cotangent * activated).astype(jnp.bfloat16)


def derivatives(layout, terms, cotangent, first, columns, after):
    share = cotangent.shape[0]
    n_terms = len(terms[0])
    return pl.pallas_call(
        functools.partial(derivatives_kernel, first, layout, n_terms),
        in_specs=[ANY] * (len(layout) * n_terms + 1 + len(after)),
        out_specs=[pl.BlockSpec(memory_space=pltpu.VMEM)] * 2,
        out_shape=[
            jax.ShapeDtypeStruct((share, columns), jnp.bfloat16),
            jax.ShapeDtypeStruct((2, share, columns), jnp.bfloat16),
        ],
        scratch_shapes=[pltpu.VMEM((2, share, columns), jnp.bfloat16)] * n_terms
        + [
            pltpu.VMEM((share, columns), jnp.bfloat16),
            pltpu.SemaphoreType.DMA((len(layout) * n_terms + 1,)),
        ],
        compiler_params=pltpu.CompilerParams(vmem_limit_bytes=VMEM_BYTES),
        cost_estimate=COST,
    )(*sum(terms, []), cotangent, *after)


def backward_kernel(n_out, steps, chained, n_after, part, where, *refs):
    n_slots = where.shape[0]
    g_refs, refs = refs[:n_slots], refs[n_slots:]
    (wg_ref, wu_ref, fg_ref, fu_ref), refs = refs[:4], refs[4:]
    if chained:
        carry_ref, refs = refs[0], refs[1:]
    refs = refs[n_after:]
    o_refs = refs[:n_out]
    g_all, acc, both, sem = refs[n_out:]
    i = pl.program_id(0)
    tile = wg_ref.shape[1]
    depth, rows = acc.shape
    share = rows // n_slots

    @pl.when(i == 0)
    def _():
        copies = []
        for slot in range(n_slots):
            row = pl.multiple_of(where[slot] * share, share)
            copies.append(
                pltpu.make_async_copy(
                    g_refs[slot], g_all.at[:, pl.ds(row, share), :], sem.at[slot]
                )
            )
        if chained:
            copies.append(
                pltpu.make_async_copy(
                    carry_ref.at[pl.ds(part * depth, depth), :], acc, sem.at[n_slots]
                )
            )
        else:
            acc[...] = jnp.zeros_like(acc)
        copy_all(copies)

    columns = pl.ds(pl.multiple_of(i * tile, tile), tile)
    both[:, :tile] = masked(wg_ref, fg_ref)
    both[:, tile:] = masked(wu_ref, fu_ref)
    acc[...] += lax.dot_general(
        both[...],
        jnp.concatenate([g_all[0, :, columns], g_all[1, :, columns]], axis=1),
        (((1,), (1,)), ((), ())),
        preferred_element_type=jnp.float32,
    )

    @pl.when(i == steps - 1)
    def _():
        if n_out == 1:
            copy_all([pltpu.make_async_copy(acc, o_refs[0], sem.at[0])])
        else:
            for k in range(n_out):
                size = rows // n_out
                o_refs[k][...] = acc[:, k * size : (k + 1) * size].T.astype(jnp.bfloat16)


def backward(carry, where, pieces, weights, flags, first, tile, part, planes, after):
    n_slots = where.shape[0]
    width = pieces[0].shape[2]
    rows = pieces[0].shape[1] * n_slots
    depth = weights[0].shape[0]
    f_parts = FEATURE_PARTS
    if part is not None:
        depth, f_parts = depth // FEATURE_PARTS, 1
    row = part or 0
    tiles = width // tile
    w_spec = pl.BlockSpec((depth, tile), lambda i, s: (row, first + i))
    f_spec = pl.BlockSpec(
        (f_parts, flags[0].shape[1], tile), lambda i, s: (row, 0, first + i)
    )
    if planes:
        out_specs = [pl.BlockSpec((rows // planes, depth), lambda i, s: (0, 0))] * planes
        out_shape = [jax.ShapeDtypeStruct((rows // planes, depth), jnp.bfloat16)] * planes
    else:
        out_specs = [ANY]
        out_shape = [jax.ShapeDtypeStruct((depth, rows), jnp.float32)]
    chained = carry is not None
    return pl.pallas_call(
        functools.partial(
            backward_kernel, len(out_shape), tiles, chained, len(after), part
        ),
        grid_spec=pltpu.PrefetchScalarGridSpec(
            num_scalar_prefetch=1,
            grid=(tiles,),
            in_specs=[ANY] * n_slots + [w_spec] * 2 + [f_spec] * 2 + [ANY] * (chained + len(after)),
            out_specs=out_specs,
            scratch_shapes=[
                pltpu.VMEM((2, rows, width), jnp.bfloat16),
                pltpu.VMEM((depth, rows), jnp.float32),
                pltpu.VMEM((depth, 2 * tile), jnp.bfloat16),
                pltpu.SemaphoreType.DMA((n_slots + 1,)),
            ],
        ),
        out_shape=out_shape,
        compiler_params=pltpu.CompilerParams(vmem_limit_bytes=VMEM_BYTES),
        cost_estimate=pl.CostEstimate(
            flops=6 * rows * depth * width,
            bytes_accessed=4 * depth * width,
            transcendentals=0,
        ),
    )(where, *pieces, *weights, *flags, *((carry,) if chained else ()), *after)


def wide(array):
    return array.astype(jnp.float32)


class ReduceScatter:
    def __init__(self, cube, keep, send):
        self.cube = cube
        self.terms = [keep, cube.sibling(send)]
        self.rows = keep.shape[1]

    def exchange(self, i, after):
        self.rows //= 2
        self.terms[0] = then(self.terms[0], *after)
        rows = self.rows
        moved = sum(wide(t[:, rows : 2 * rows]) for t in self.terms).astype(jnp.bfloat16)
        self.terms.append(self.cube.step(moved, i))
        if i == 0:
            self.first = self.terms[-1]
        return moved


class AllGather:
    def __init__(self, cube, own, *after):
        self.cube = cube
        n_dims = len(cube.dims[0])
        own = then(own, *after)
        self.pieces = [own] + [cube.step(own, n_dims - 1 - i) for i in range(n_dims)]

    def finish(self, *after, late=()):
        cube = self.cube
        n_dims = len(cube.dims[0])
        pieces = {0: self.pieces[0]}
        for i in range(n_dims):
            pieces[1 << i] = self.pieces[1 + i]
        pieces = {slot: then(p, *after) for slot, p in pieces.items()}
        for slot in range(1, cube.half):
            if slot not in pieces:
                low = slot & -slot
                pieces[slot] = cube.step(pieces[slot ^ low], n_dims - low.bit_length())
        last = cube.half - 1
        pieces[last] = then(pieces[last], *late)
        pieces = [pieces[slot] for slot in range(cube.half)]
        return pieces + [cube.sibling(p) for p in pieces]


def flip(array, bit, size):
    return lax.ppermute(array, "col", [(z, z ^ bit) for z in range(size)])


def gather_planes(x, n_col):
    xs = [x]
    for k in range(1, n_col):
        low = k & -k
        xs.append(flip(xs[k ^ low], low, n_col))
    return xs


def sum_planes(parts, n_col, direct, after):
    terms = [wide(p) for p in parts]
    arrived = list(after)
    for k in range(n_col - 1, 0, -1):
        low = k if direct else k & -k
        sent = terms[k].astype(jnp.bfloat16)
        if not direct:
            sent = then(sent, *arrived)
        moved = flip(sent, low, n_col)
        if direct or low != k:
            arrived.append(moved)
        terms[k ^ low] = terms[k ^ low] + wide(moved)
    return terms[0].astype(jnp.bfloat16), arrived


def shards(cube, n_col, inputs, gate_weight, up_weight, gate_pattern, up_pattern, cotangent):
    depth, local_hidden = gate_weight.shape
    share = cotangent.shape[0]
    tile = local_hidden // sum(BACKWARD)
    weights = (gate_weight, up_weight)
    flags = [
        jnp.repeat(p.astype(jnp.bfloat16), BLOCK, axis=1).reshape(
            FEATURE_PARTS, -1, local_hidden
        )
        for p in (gate_pattern, up_pattern)
    ]
    table = places(cube, n_col)
    row, col = lax.axis_index("row"), lax.axis_index("col")
    where = jnp.asarray(table)[row, col]
    slots = jnp.asarray(np.argsort(table, axis=-1).astype(np.int32))[row, col]

    xs = gather_planes(inputs, n_col)
    units = list(zip(np.cumsum((0,) + FORWARD).tolist(), FORWARD))
    sums, after, moved = [], {}, []
    for n, (first, tiles) in enumerate(units):
        keep, send = forward(
            slots, xs, weights, flags, first, tiles, tile, after.pop(n, [])
        )
        sums.append(ReduceScatter(cube, keep, send))
        after.setdefault(n + 1, []).append(keep)
        moved.append([])
        for i in range(len(cube.dims[0])):
            before = []
            if i == 1 and n == 1:
                before = sums[0].terms[-1:]
            elif i == 0 and n == 2:
                before = moved[1][-1:]
            elif i == 0 and n == 3:
                before = [sums[2].first, sums[0].terms[-1], sums[1].terms[-1]]
            elif i == 1 and n == 3:
                before = sums[2].terms[-1:]
            moved[n].append(sums[n].exchange(i, before))
            after.setdefault(n + 2 + i, []).append(moved[n][-1])
    first_moved = [m[0] for m in moved]

    hidden, gathers, owns = [], [], []
    starts = [sum(BACKWARD[:n]) for n in range(len(BACKWARD))]
    for first, tiles in zip(starts, BACKWARD):
        layout, terms = [], []
        for (start, width), unit in zip(units, sums):
            low, high = max(first, start), min(first + tiles, start + width)
            if low < high:
                layout.append(((low - start) * tile, (low - first) * tile, (high - low) * tile))
                terms.append(unit.terms)
        h, own = derivatives(
            layout, terms, cotangent, first * tile, tiles * tile, gathers[0].pieces if gathers else first_moved
        )
        hidden.append(h)
        owns.append(own)
        gathers.append(AllGather(cube, own, moved[-1][-1]))
    pieces = gathers[0].finish(owns[1])
    arrived = gathers[1].pieces
    carry = backward(None, where, pieces, weights, flags, 0, tile, None, 0, arrived)
    pieces = gathers[1].finish(late=carry)
    input_grad, arrived, parts = [], [], []
    for part in range(FEATURE_PARTS):
        parts = backward(
            carry[0],
            where,
            pieces,
            weights,
            flags,
            starts[1],
            tile,
            part,
            n_col,
            parts[:1],
        )
        total, arrived = sum_planes(parts, n_col, part < FEATURE_PARTS - 1, arrived)
        input_grad.append(total)
    return jnp.concatenate(hidden, axis=1), jnp.concatenate(input_grad, axis=1)


def solution(mesh):
    placed = (
        P("col", "row"),
        P("row", "col"),
        P("row", "col"),
        P("row", "col"),
        P("row", "col"),
        P("row", "col"),
    )
    return jax.shard_map(
        functools.partial(shards, Cube(mesh.shape["row"]), mesh.shape["col"]),
        mesh=mesh,
        in_specs=placed,
        out_specs=(P("row", "col"), P("col", "row")),
        check_vma=False,
    )
```

```python
import functools

import jax
import jax.numpy as jnp
import numpy as np
from jax import lax
from jax.experimental import pallas as pl
from jax.experimental.pallas import tpu as pltpu
from jax.sharding import PartitionSpec as P

BLOCK = 128
FORWARD = (2, 3, 4, 4)
BACKWARD = (5, 8)
FEATURE_PARTS = 2
VMEM_BYTES = 48 * 1024 * 1024
ANY = pl.BlockSpec(memory_space=pl.ANY)
COST = pl.CostEstimate(flops=1, bytes_accessed=1, transcendentals=0)


def masked(w_ref, f_ref):
    rows, columns = w_ref.shape
    flags = f_ref[...].reshape(rows // BLOCK, 1, columns)
    return (w_ref[...].reshape(rows // BLOCK, BLOCK, columns) * flags).reshape(rows, columns)


def then(array, *others):
    return lax.optimization_barrier((array, *others))[0]


class Cube:
    def __init__(self, size):
        self.size = size
        self.half = size // 2
        rising = [1 << b for b in range(1, size.bit_length() - 1)]
        self.dims = (rising, rising[::-1])

    def offset(self, parity, slot):
        dims = self.dims[parity]
        digits = [slot >> (len(dims) - 1 - i) & 1 for i in range(len(dims))]
        return int(np.bitwise_xor.reduce([0] + [d for d, on in zip(dims, digits) if on]))

    def owner(self, me, slot):
        if slot >= self.half:
            me, slot = me ^ 1, slot - self.half
        return me ^ self.offset(me & 1, slot)

    def step(self, array, i):
        perm = [(r, r ^ self.dims[r & 1][i]) for r in range(self.size)]
        return lax.ppermute(array, "row", perm)

    def sibling(self, array):
        return lax.ppermute(array, "row", [(r, r ^ 1) for r in range(self.size)])


def places(cube, n_col):
    ratio = cube.size // n_col
    table = np.zeros((cube.size, n_col, cube.size), np.int32)
    for me in range(cube.size):
        for z in range(n_col):
            for slot in range(cube.size):
                d = cube.owner(me, slot)
                table[me, z, slot] = ratio * ((d // ratio) ^ z) + d % ratio
    return table


def copy_all(copies):
    for copy in copies:
        copy.start()
    for copy in copies:
        copy.wait()


def forward_kernel(n_x, n_after, slots, *refs):
    x_refs, refs = refs[:n_x], refs[n_x:]
    wg_ref, wu_ref, fg_ref, fu_ref = refs[:4]
    keep_ref, send_ref, x_all, sem = refs[4 + n_after :]
    half = keep_ref.shape[1]
    shares = slots.shape[0]
    share = 2 * half // shares
    ratio = shares // n_x

    @pl.when(pl.program_id(0) == 0)
    def _():
        copies = []
        for k in range(n_x):
            for c in range(ratio):
                place = k * ratio + c
                row = pl.multiple_of(slots[place] * share, share)
                copies.append(
                    pltpu.make_async_copy(
                        x_refs[k].at[pl.ds(c * share, share), :],
                        x_all.at[pl.ds(row, share), :],
                        sem.at[place],
                    )
                )
        copy_all(copies)

    for n, (w_ref, f_ref) in enumerate(((wg_ref, fg_ref), (wu_ref, fu_ref))):
        out = jnp.dot(x_all[...], masked(w_ref, f_ref), preferred_element_type=jnp.float32)
        out = out.astype(jnp.bfloat16)
        keep_ref[n] = out[:half]
        send_ref[n] = out[half:]


def forward(slots, xs, weights, flags, first, tiles, tile, after):
    depth = weights[0].shape[0]
    rows = len(xs) * xs[0].shape[0]
    w_spec = pl.BlockSpec((depth, tile), lambda i, s: (0, first + i))
    f_spec = pl.BlockSpec((*flags[0].shape[:2], tile), lambda i, s: (0, 0, first + i))
    o_spec = pl.BlockSpec((2, rows // 2, tile), lambda i, s: (0, 0, i))
    out = jax.ShapeDtypeStruct((2, rows // 2, tiles * tile), jnp.bfloat16)
    return pl.pallas_call(
        functools.partial(forward_kernel, len(xs), len(after)),
        grid_spec=pltpu.PrefetchScalarGridSpec(
            num_scalar_prefetch=1,
            grid=(tiles,),
            in_specs=[ANY] * len(xs) + [w_spec] * 2 + [f_spec] * 2 + [ANY] * len(after),
            out_specs=[o_spec, o_spec],
            scratch_shapes=[
                pltpu.VMEM((rows, depth), jnp.bfloat16),
                pltpu.SemaphoreType.DMA((slots.shape[0],)),
            ],
        ),
        out_shape=[out, out],
        compiler_params=pltpu.CompilerParams(vmem_limit_bytes=VMEM_BYTES),
        cost_estimate=pl.CostEstimate(
            flops=8 * rows * depth * tiles * tile,
            bytes_accessed=4 * depth * tiles * tile,
            transcendentals=0,
        ),
    )(slots, *xs, *weights, *flags, *after)


def derivatives_kernel(first, layout, n_terms, *refs):
    sources, cot_ref = refs[: len(layout) * n_terms], refs[len(layout) * n_terms]
    h_ref, g_ref = refs[-4 - n_terms : -2 - n_terms]
    held = refs[-2 - n_terms : -2]
    cot, sem = refs[-2:]
    share, columns = h_ref.shape
    copies = []
    for m, (source, place, width) in enumerate(layout):
        for n in range(n_terms):
            copies.append(
                pltpu.make_async_copy(
                    sources[m * n_terms + n].at[:, pl.ds(0, share), pl.ds(source, width)],
                    held[n].at[:, :, pl.ds(place, width)],
                    sem.at[m * n_terms + n],
                )
            )
    copies.append(
        pltpu.make_async_copy(
            cot_ref.at[:, pl.ds(first, columns)], cot, sem.at[len(layout) * n_terms]
        )
    )
    copy_all(copies)
    step = 256
    for c in range(0, columns, step):
        at = slice(c, c + step)
        gate_sum = sum(wide(v[0, :, at]) for v in held)
        up_sum = sum(wide(v[1, :, at]) for v in held)
        cotangent = wide(cot[:, at])
        sigmoid_gate = jax.nn.sigmoid(gate_sum)
        activated = gate_sum * sigmoid_gate
        h_ref[:, at] = (activated * up_sum).astype(jnp.bfloat16)
        g_ref[0, :, at] = (
            cotangent * up_sum * sigmoid_gate * (1.0 + gate_sum * (1.0 - sigmoid_gate))
        ).astype(jnp.bfloat16)
        g_ref[1, :, at] = (cotangent * activated).astype(jnp.bfloat16)


def derivatives(layout, terms, cotangent, first, columns, after):
    share = cotangent.shape[0]
    n_terms = len(terms[0])
    return pl.pallas_call(
        functools.partial(derivatives_kernel, first, layout, n_terms),
        in_specs=[ANY] * (len(layout) * n_terms + 1 + len(after)),
        out_specs=[pl.BlockSpec(memory_space=pltpu.VMEM)] * 2,
        out_shape=[
            jax.ShapeDtypeStruct((share, columns), jnp.bfloat16),
            jax.ShapeDtypeStruct((2, share, columns), jnp.bfloat16),
        ],
        scratch_shapes=[pltpu.VMEM((2, share, columns), jnp.bfloat16)] * n_terms
        + [
            pltpu.VMEM((share, columns), jnp.bfloat16),
            pltpu.SemaphoreType.DMA((len(layout) * n_terms + 1,)),
        ],
        compiler_params=pltpu.CompilerParams(vmem_limit_bytes=VMEM_BYTES),
        cost_estimate=COST,
    )(*sum(terms, []), cotangent, *after)


def backward_kernel(n_out, steps, chained, n_after, part, where, *refs):
    n_slots = where.shape[0]
    g_refs, refs = refs[:n_slots], refs[n_slots:]
    (wg_ref, wu_ref, fg_ref, fu_ref), refs = refs[:4], refs[4:]
    if chained:
        carry_ref, refs = refs[0], refs[1:]
    refs = refs[n_after:]
    o_refs = refs[:n_out]
    g_all, acc, both, sem = refs[n_out:]
    i = pl.program_id(0)
    tile = wg_ref.shape[1]
    depth, rows = acc.shape
    share = rows // n_slots

    @pl.when(i == 0)
    def _():
        copies = []
        for slot in range(n_slots):
            row = pl.multiple_of(where[slot] * share, share)
            copies.append(
                pltpu.make_async_copy(
                    g_refs[slot], g_all.at[:, pl.ds(row, share), :], sem.at[slot]
                )
            )
        if chained:
            copies.append(
                pltpu.make_async_copy(
                    carry_ref.at[pl.ds(part * depth, depth), :], acc, sem.at[n_slots]
                )
            )
        else:
            acc[...] = jnp.zeros_like(acc)
        copy_all(copies)

    columns = pl.ds(pl.multiple_of(i * tile, tile), tile)
    both[:, :tile] = masked(wg_ref, fg_ref)
    both[:, tile:] = masked(wu_ref, fu_ref)
    acc[...] += lax.dot_general(
        both[...],
        jnp.concatenate([g_all[0, :, columns], g_all[1, :, columns]], axis=1),
        (((1,), (1,)), ((), ())),
        preferred_element_type=jnp.float32,
    )

    @pl.when(i == steps - 1)
    def _():
        if n_out == 1:
            copy_all([pltpu.make_async_copy(acc, o_refs[0], sem.at[0])])
        else:
            for k in range(n_out):
                size = rows // n_out
                o_refs[k][...] = acc[:, k * size : (k + 1) * size].T.astype(jnp.bfloat16)


def backward(carry, where, pieces, weights, flags, first, tile, part, planes, after):
    n_slots = where.shape[0]
    width = pieces[0].shape[2]
    rows = pieces[0].shape[1] * n_slots
    depth = weights[0].shape[0]
    f_parts = FEATURE_PARTS
    if part is not None:
        depth, f_parts = depth // FEATURE_PARTS, 1
    row = part or 0
    tiles = width // tile
    w_spec = pl.BlockSpec((depth, tile), lambda i, s: (row, first + i))
    f_spec = pl.BlockSpec(
        (f_parts, flags[0].shape[1], tile), lambda i, s: (row, 0, first + i)
    )
    if planes:
        out_specs = [pl.BlockSpec((rows // planes, depth), lambda i, s: (0, 0))] * planes
        out_shape = [jax.ShapeDtypeStruct((rows // planes, depth), jnp.bfloat16)] * planes
    else:
        out_specs = [ANY]
        out_shape = [jax.ShapeDtypeStruct((depth, rows), jnp.float32)]
    chained = carry is not None
    return pl.pallas_call(
        functools.partial(
            backward_kernel, len(out_shape), tiles, chained, len(after), part
        ),
        grid_spec=pltpu.PrefetchScalarGridSpec(
            num_scalar_prefetch=1,
            grid=(tiles,),
            in_specs=[ANY] * n_slots + [w_spec] * 2 + [f_spec] * 2 + [ANY] * (chained + len(after)),
            out_specs=out_specs,
            scratch_shapes=[
                pltpu.VMEM((2, rows, width), jnp.bfloat16),
                pltpu.VMEM((depth, rows), jnp.float32),
                pltpu.VMEM((depth, 2 * tile), jnp.bfloat16),
                pltpu.SemaphoreType.DMA((n_slots + 1,)),
            ],
        ),
        out_shape=out_shape,
        compiler_params=pltpu.CompilerParams(vmem_limit_bytes=VMEM_BYTES),
        cost_estimate=pl.CostEstimate(
            flops=6 * rows * depth * width,
            bytes_accessed=4 * depth * width,
            transcendentals=0,
        ),
    )(where, *pieces, *weights, *flags, *((carry,) if chained else ()), *after)


def wide(array):
    return array.astype(jnp.float32)


class ReduceScatter:
    def __init__(self, cube, keep, send):
        self.cube = cube
        self.terms = [keep, cube.sibling(send)]
        self.rows = keep.shape[1]

    def exchange(self, i, after):
        self.rows //= 2
        self.terms[0] = then(self.terms[0], *after)
        rows = self.rows
        moved = sum(wide(t[:, rows : 2 * rows]) for t in self.terms).astype(jnp.bfloat16)
        self.terms.append(self.cube.step(moved, i))
        if i == 0:
            self.first = self.terms[-1]
        return moved


class AllGather:
    def __init__(self, cube, own, *after):
        self.cube = cube
        n_dims = len(cube.dims[0])
        own = then(own, *after)
        self.pieces = [own] + [cube.step(own, n_dims - 1 - i) for i in range(n_dims)]

    def finish(self, *after):
        cube = self.cube
        n_dims = len(cube.dims[0])
        pieces = {0: self.pieces[0]}
        for i in range(n_dims):
            pieces[1 << i] = self.pieces[1 + i]
        pieces = {slot: then(p, *after) for slot, p in pieces.items()}
        for slot in range(1, cube.half):
            if slot not in pieces:
                low = slot & -slot
                pieces[slot] = cube.step(pieces[slot ^ low], n_dims - low.bit_length())
        pieces = [pieces[slot] for slot in range(cube.half)]
        return pieces + [cube.sibling(p) for p in pieces]


def flip(array, bit, size):
    return lax.ppermute(array, "col", [(z, z ^ bit) for z in range(size)])


def gather_planes(x, n_col):
    xs = [x]
    for k in range(1, n_col):
        low = k & -k
        xs.append(flip(xs[k ^ low], low, n_col))
    return xs


def sum_planes(parts, n_col, direct, after):
    terms = [wide(p) for p in parts]
    arrived = list(after)
    for k in range(n_col - 1, 0, -1):
        low = k if direct else k & -k
        sent = terms[k].astype(jnp.bfloat16)
        if not direct:
            sent = then(sent, *arrived)
        moved = flip(sent, low, n_col)
        if direct or low != k:
            arrived.append(moved)
        terms[k ^ low] = terms[k ^ low] + wide(moved)
    return terms[0].astype(jnp.bfloat16), arrived


def shards(cube, n_col, inputs, gate_weight, up_weight, gate_pattern, up_pattern, cotangent):
    depth, local_hidden = gate_weight.shape
    share = cotangent.shape[0]
    tile = local_hidden // sum(BACKWARD)
    weights = (gate_weight, up_weight)
    flags = [
        jnp.repeat(p.astype(jnp.bfloat16), BLOCK, axis=1).reshape(
            FEATURE_PARTS, -1, local_hidden
        )
        for p in (gate_pattern, up_pattern)
    ]
    table = places(cube, n_col)
    row, col = lax.axis_index("row"), lax.axis_index("col")
    where = jnp.asarray(table)[row, col]
    slots = jnp.asarray(np.argsort(table, axis=-1).astype(np.int32))[row, col]

    xs = gather_planes(inputs, n_col)
    units = list(zip(np.cumsum((0,) + FORWARD).tolist(), FORWARD))
    sums, after, moved = [], {}, []
    for n, (first, tiles) in enumerate(units):
        keep, send = forward(
            slots, xs, weights, flags, first, tiles, tile, after.pop(n, [])
        )
        sums.append(ReduceScatter(cube, keep, send))
        after.setdefault(n + 1, []).append(keep)
        moved.append([])
        for i in range(len(cube.dims[0])):
            before = sums[n - 2].terms[-1:] if i == 0 and n > 2 else []
            moved[n].append(sums[n].exchange(i, before))
            after.setdefault(n + 2 + i, []).append(moved[n][-1])
    first_moved = [m[0] for m in moved]

    hidden, gathers, owns = [], [], []
    starts = [sum(BACKWARD[:n]) for n in range(len(BACKWARD))]
    for first, tiles in zip(starts, BACKWARD):
        layout, terms = [], []
        for (start, width), unit in zip(units, sums):
            low, high = max(first, start), min(first + tiles, start + width)
            if low < high:
                layout.append(((low - start) * tile, (low - first) * tile, (high - low) * tile))
                terms.append(unit.terms)
        h, own = derivatives(
            layout, terms, cotangent, first * tile, tiles * tile, owns[-1:] or first_moved
        )
        hidden.append(h)
        owns.append(own)
        gathers.append(AllGather(cube, own))
    carry = backward(
        None, where, gathers[0].finish(), weights, flags, 0, tile, None, 0, owns[1:]
    )
    pieces = gathers[1].finish(*carry)
    input_grad, arrived, parts = [], [], []
    for part in range(FEATURE_PARTS):
        parts = backward(
            carry[0],
            where,
            pieces,
            weights,
            flags,
            starts[1],
            tile,
            part,
            n_col,
            parts[:1],
        )
        total, arrived = sum_planes(parts, n_col, part < FEATURE_PARTS - 1, arrived)
        input_grad.append(total)
    return jnp.concatenate(hidden, axis=1), jnp.concatenate(input_grad, axis=1)


def solution(mesh):
    placed = (
        P("col", "row"),
        P("row", "col"),
        P("row", "col"),
        P("row", "col"),
        P("row", "col"),
        P("row", "col"),
    )
    return jax.shard_map(
        functools.partial(shards, Cube(mesh.shape["row"]), mesh.shape["col"]),
        mesh=mesh,
        in_specs=placed,
        out_specs=(P("row", "col"), P("col", "row")),
        check_vma=False,
    )
```

```python
import functools

import jax
import jax.numpy as jnp
import numpy as np
from jax import lax
from jax.experimental import pallas as pl
from jax.experimental.pallas import tpu as pltpu
from jax.sharding import PartitionSpec as P

BLOCK = 128
FORWARD = (3, 3, 3, 4)
BACKWARD = (6, 7)
FEATURE_PARTS = 2
VMEM_BYTES = 48 * 1024 * 1024
ANY = pl.BlockSpec(memory_space=pl.ANY)
COST = pl.CostEstimate(flops=1, bytes_accessed=1, transcendentals=0)


def masked(w_ref, f_ref):
    rows, columns = w_ref.shape
    flags = f_ref[...].reshape(rows // BLOCK, 1, columns)
    return (w_ref[...].reshape(rows // BLOCK, BLOCK, columns) * flags).reshape(rows, columns)


def then(array, *others):
    return lax.optimization_barrier((array, *others))[0]


class Cube:
    def __init__(self, size):
        self.size = size
        self.half = size // 2
        rising = [1 << b for b in range(1, size.bit_length() - 1)]
        self.dims = (rising, rising[::-1])

    def offset(self, parity, slot):
        dims = self.dims[parity]
        digits = [slot >> (len(dims) - 1 - i) & 1 for i in range(len(dims))]
        return int(np.bitwise_xor.reduce([0] + [d for d, on in zip(dims, digits) if on]))

    def owner(self, me, slot):
        if slot >= self.half:
            me, slot = me ^ 1, slot - self.half
        return me ^ self.offset(me & 1, slot)

    def step(self, array, i):
        perm = [(r, r ^ self.dims[r & 1][i]) for r in range(self.size)]
        return lax.ppermute(array, "row", perm)

    def sibling(self, array):
        return lax.ppermute(array, "row", [(r, r ^ 1) for r in range(self.size)])


def places(cube, n_col):
    ratio = cube.size // n_col
    table = np.zeros((cube.size, n_col, cube.size), np.int32)
    for me in range(cube.size):
        for z in range(n_col):
            for slot in range(cube.size):
                d = cube.owner(me, slot)
                table[me, z, slot] = ratio * ((d // ratio) ^ z) + d % ratio
    return table


def copy_all(copies):
    for copy in copies:
        copy.start()
    for copy in copies:
        copy.wait()


def forward_kernel(n_x, n_after, slots, *refs):
    x_refs, refs = refs[:n_x], refs[n_x:]
    wg_ref, wu_ref, fg_ref, fu_ref = refs[:4]
    keep_ref, send_ref, x_all, sem = refs[4 + n_after :]
    half = keep_ref.shape[1]
    shares = slots.shape[0]
    share = 2 * half // shares
    ratio = shares // n_x

    @pl.when(pl.program_id(0) == 0)
    def _():
        copies = []
        for k in range(n_x):
            for c in range(ratio):
                place = k * ratio + c
                row = pl.multiple_of(slots[place] * share, share)
                copies.append(
                    pltpu.make_async_copy(
                        x_refs[k].at[pl.ds(c * share, share), :],
                        x_all.at[pl.ds(row, share), :],
                        sem.at[place],
                    )
                )
        copy_all(copies)

    for n, (w_ref, f_ref) in enumerate(((wg_ref, fg_ref), (wu_ref, fu_ref))):
        out = jnp.dot(x_all[...], masked(w_ref, f_ref), preferred_element_type=jnp.float32)
        out = out.astype(jnp.bfloat16)
        keep_ref[n] = out[:half]
        send_ref[n] = out[half:]


def forward(slots, xs, weights, flags, first, tiles, tile, after):
    depth = weights[0].shape[0]
    rows = len(xs) * xs[0].shape[0]
    w_spec = pl.BlockSpec((depth, tile), lambda i, s: (0, first + i))
    f_spec = pl.BlockSpec((*flags[0].shape[:2], tile), lambda i, s: (0, 0, first + i))
    o_spec = pl.BlockSpec((2, rows // 2, tile), lambda i, s: (0, 0, i))
    out = jax.ShapeDtypeStruct((2, rows // 2, tiles * tile), jnp.bfloat16)
    return pl.pallas_call(
        functools.partial(forward_kernel, len(xs), len(after)),
        grid_spec=pltpu.PrefetchScalarGridSpec(
            num_scalar_prefetch=1,
            grid=(tiles,),
            in_specs=[ANY] * len(xs) + [w_spec] * 2 + [f_spec] * 2 + [ANY] * len(after),
            out_specs=[o_spec, o_spec],
            scratch_shapes=[
                pltpu.VMEM((rows, depth), jnp.bfloat16),
                pltpu.SemaphoreType.DMA((slots.shape[0],)),
            ],
        ),
        out_shape=[out, out],
        compiler_params=pltpu.CompilerParams(vmem_limit_bytes=VMEM_BYTES),
        cost_estimate=pl.CostEstimate(
            flops=8 * rows * depth * tiles * tile,
            bytes_accessed=4 * depth * tiles * tile,
            transcendentals=0,
        ),
    )(slots, *xs, *weights, *flags, *after)


def derivatives_kernel(first, layout, n_terms, *refs):
    sources, cot_ref = refs[: len(layout) * n_terms], refs[len(layout) * n_terms]
    h_ref, g_ref = refs[-4 - n_terms : -2 - n_terms]
    held = refs[-2 - n_terms : -2]
    cot, sem = refs[-2:]
    share, columns = h_ref.shape
    copies = []
    for m, (source, place, width) in enumerate(layout):
        for n in range(n_terms):
            copies.append(
                pltpu.make_async_copy(
                    sources[m * n_terms + n].at[:, pl.ds(0, share), pl.ds(source, width)],
                    held[n].at[:, :, pl.ds(place, width)],
                    sem.at[m * n_terms + n],
                )
            )
    copies.append(
        pltpu.make_async_copy(
            cot_ref.at[:, pl.ds(first, columns)], cot, sem.at[len(layout) * n_terms]
        )
    )
    copy_all(copies)
    step = 256
    for c in range(0, columns, step):
        at = slice(c, c + step)
        gate_sum = sum(wide(v[0, :, at]) for v in held)
        up_sum = sum(wide(v[1, :, at]) for v in held)
        cotangent = wide(cot[:, at])
        sigmoid_gate = jax.nn.sigmoid(gate_sum)
        activated = gate_sum * sigmoid_gate
        h_ref[:, at] = (activated * up_sum).astype(jnp.bfloat16)
        g_ref[0, :, at] = (
            cotangent * up_sum * sigmoid_gate * (1.0 + gate_sum * (1.0 - sigmoid_gate))
        ).astype(jnp.bfloat16)
        g_ref[1, :, at] = (cotangent * activated).astype(jnp.bfloat16)


def derivatives(layout, terms, cotangent, first, columns, after):
    share = cotangent.shape[0]
    n_terms = len(terms[0])
    return pl.pallas_call(
        functools.partial(derivatives_kernel, first, layout, n_terms),
        in_specs=[ANY] * (len(layout) * n_terms + 1 + len(after)),
        out_specs=[pl.BlockSpec(memory_space=pltpu.VMEM)] * 2,
        out_shape=[
            jax.ShapeDtypeStruct((share, columns), jnp.bfloat16),
            jax.ShapeDtypeStruct((2, share, columns), jnp.bfloat16),
        ],
        scratch_shapes=[pltpu.VMEM((2, share, columns), jnp.bfloat16)] * n_terms
        + [
            pltpu.VMEM((share, columns), jnp.bfloat16),
            pltpu.SemaphoreType.DMA((len(layout) * n_terms + 1,)),
        ],
        compiler_params=pltpu.CompilerParams(vmem_limit_bytes=VMEM_BYTES),
        cost_estimate=COST,
    )(*sum(terms, []), cotangent, *after)


def backward_kernel(n_out, steps, chained, n_after, part, where, *refs):
    n_slots = where.shape[0]
    g_refs, refs = refs[:n_slots], refs[n_slots:]
    (wg_ref, wu_ref, fg_ref, fu_ref), refs = refs[:4], refs[4:]
    if chained:
        carry_ref, refs = refs[0], refs[1:]
    refs = refs[n_after:]
    o_refs = refs[:n_out]
    g_all, acc, both, sem = refs[n_out:]
    i = pl.program_id(0)
    tile = wg_ref.shape[1]
    depth, rows = acc.shape
    share = rows // n_slots

    @pl.when(i == 0)
    def _():
        copies = []
        for slot in range(n_slots):
            row = pl.multiple_of(where[slot] * share, share)
            copies.append(
                pltpu.make_async_copy(
                    g_refs[slot], g_all.at[:, pl.ds(row, share), :], sem.at[slot]
                )
            )
        if chained:
            copies.append(
                pltpu.make_async_copy(
                    carry_ref.at[pl.ds(part * depth, depth), :], acc, sem.at[n_slots]
                )
            )
        else:
            acc[...] = jnp.zeros_like(acc)
        copy_all(copies)

    columns = pl.ds(pl.multiple_of(i * tile, tile), tile)
    both[:, :tile] = masked(wg_ref, fg_ref)
    both[:, tile:] = masked(wu_ref, fu_ref)
    acc[...] += lax.dot_general(
        both[...],
        jnp.concatenate([g_all[0, :, columns], g_all[1, :, columns]], axis=1),
        (((1,), (1,)), ((), ())),
        preferred_element_type=jnp.float32,
    )

    @pl.when(i == steps - 1)
    def _():
        if n_out == 1:
            copy_all([pltpu.make_async_copy(acc, o_refs[0], sem.at[0])])
        else:
            for k in range(n_out):
                size = rows // n_out
                o_refs[k][...] = acc[:, k * size : (k + 1) * size].T.astype(jnp.bfloat16)


def backward(carry, where, pieces, weights, flags, first, tile, part, planes, after):
    n_slots = where.shape[0]
    width = pieces[0].shape[2]
    rows = pieces[0].shape[1] * n_slots
    depth = weights[0].shape[0]
    f_parts = FEATURE_PARTS
    if part is not None:
        depth, f_parts = depth // FEATURE_PARTS, 1
    row = part or 0
    tiles = width // tile
    w_spec = pl.BlockSpec((depth, tile), lambda i, s: (row, first + i))
    f_spec = pl.BlockSpec(
        (f_parts, flags[0].shape[1], tile), lambda i, s: (row, 0, first + i)
    )
    if planes:
        out_specs = [pl.BlockSpec((rows // planes, depth), lambda i, s: (0, 0))] * planes
        out_shape = [jax.ShapeDtypeStruct((rows // planes, depth), jnp.bfloat16)] * planes
    else:
        out_specs = [ANY]
        out_shape = [jax.ShapeDtypeStruct((depth, rows), jnp.float32)]
    chained = carry is not None
    return pl.pallas_call(
        functools.partial(
            backward_kernel, len(out_shape), tiles, chained, len(after), part
        ),
        grid_spec=pltpu.PrefetchScalarGridSpec(
            num_scalar_prefetch=1,
            grid=(tiles,),
            in_specs=[ANY] * n_slots + [w_spec] * 2 + [f_spec] * 2 + [ANY] * (chained + len(after)),
            out_specs=out_specs,
            scratch_shapes=[
                pltpu.VMEM((2, rows, width), jnp.bfloat16),
                pltpu.VMEM((depth, rows), jnp.float32),
                pltpu.VMEM((depth, 2 * tile), jnp.bfloat16),
                pltpu.SemaphoreType.DMA((n_slots + 1,)),
            ],
        ),
        out_shape=out_shape,
        compiler_params=pltpu.CompilerParams(vmem_limit_bytes=VMEM_BYTES),
        cost_estimate=pl.CostEstimate(
            flops=6 * rows * depth * width,
            bytes_accessed=4 * depth * width,
            transcendentals=0,
        ),
    )(where, *pieces, *weights, *flags, *((carry,) if chained else ()), *after)


def wide(array):
    return array.astype(jnp.float32)


class ReduceScatter:
    def __init__(self, cube, keep, send):
        self.cube = cube
        self.terms = [keep, cube.sibling(send)]
        self.rows = keep.shape[1]

    def exchange(self, i, after):
        self.rows //= 2
        self.terms[0] = then(self.terms[0], *after)
        rows = self.rows
        moved = sum(wide(t[:, rows : 2 * rows]) for t in self.terms).astype(jnp.bfloat16)
        self.terms.append(self.cube.step(moved, i))
        if i == 0:
            self.first = self.terms[-1]
        return moved


class AllGather:
    def __init__(self, cube, own, *after):
        self.cube = cube
        n_dims = len(cube.dims[0])
        own = then(own, *after)
        self.pieces = [own] + [cube.step(own, n_dims - 1 - i) for i in range(n_dims)]

    def finish(self, *after):
        cube = self.cube
        n_dims = len(cube.dims[0])
        pieces = {0: self.pieces[0]}
        for i in range(n_dims):
            pieces[1 << i] = self.pieces[1 + i]
        pieces = {slot: then(p, *after) for slot, p in pieces.items()}
        for slot in range(1, cube.half):
            if slot not in pieces:
                low = slot & -slot
                pieces[slot] = cube.step(pieces[slot ^ low], n_dims - low.bit_length())
        pieces = [pieces[slot] for slot in range(cube.half)]
        return pieces + [cube.sibling(p) for p in pieces]


def flip(array, bit, size):
    return lax.ppermute(array, "col", [(z, z ^ bit) for z in range(size)])


def gather_planes(x, n_col):
    xs = [x]
    for k in range(1, n_col):
        low = k & -k
        xs.append(flip(xs[k ^ low], low, n_col))
    return xs


def sum_planes(parts, n_col, direct, after):
    terms = [wide(p) for p in parts]
    arrived = list(after)
    for k in range(n_col - 1, 0, -1):
        low = k if direct else k & -k
        sent = terms[k].astype(jnp.bfloat16)
        if not direct:
            sent = then(sent, *arrived)
        moved = flip(sent, low, n_col)
        if direct or low != k:
            arrived.append(moved)
        terms[k ^ low] = terms[k ^ low] + wide(moved)
    return terms[0].astype(jnp.bfloat16), arrived


def shards(cube, n_col, inputs, gate_weight, up_weight, gate_pattern, up_pattern, cotangent):
    depth, local_hidden = gate_weight.shape
    share = cotangent.shape[0]
    tile = local_hidden // sum(BACKWARD)
    weights = (gate_weight, up_weight)
    flags = [
        jnp.repeat(p.astype(jnp.bfloat16), BLOCK, axis=1).reshape(
            FEATURE_PARTS, -1, local_hidden
        )
        for p in (gate_pattern, up_pattern)
    ]
    table = places(cube, n_col)
    row, col = lax.axis_index("row"), lax.axis_index("col")
    where = jnp.asarray(table)[row, col]
    slots = jnp.asarray(np.argsort(table, axis=-1).astype(np.int32))[row, col]

    xs = gather_planes(inputs, n_col)
    units = list(zip(np.cumsum((0,) + FORWARD).tolist(), FORWARD))
    sums, after, moved = [], {}, []
    for n, (first, tiles) in enumerate(units):
        keep, send = forward(
            slots, xs, weights, flags, first, tiles, tile, after.pop(n, [])
        )
        sums.append(ReduceScatter(cube, keep, send))
        after.setdefault(n + 1, []).append(keep)
        moved.append([])
        for i in range(len(cube.dims[0])):
            before = sums[n - 2].terms[-1:] if i == 0 and n > 2 else []
            moved[n].append(sums[n].exchange(i, before))
            after.setdefault(n + 2 + i, []).append(moved[n][-1])
    first_moved = [m[0] for m in moved]

    hidden, gathers, owns = [], [], []
    starts = [sum(BACKWARD[:n]) for n in range(len(BACKWARD))]
    for first, tiles in zip(starts, BACKWARD):
        layout, terms = [], []
        for (start, width), unit in zip(units, sums):
            low, high = max(first, start), min(first + tiles, start + width)
            if low < high:
                layout.append(((low - start) * tile, (low - first) * tile, (high - low) * tile))
                terms.append(unit.terms)
        h, own = derivatives(
            layout, terms, cotangent, first * tile, tiles * tile, owns[-1:] or first_moved
        )
        hidden.append(h)
        owns.append(own)
        gathers.append(AllGather(cube, own))
    carry = backward(
        None, where, gathers[0].finish(), weights, flags, 0, tile, None, 0, owns[1:]
    )
    pieces = gathers[1].finish(*carry)
    input_grad, arrived, parts = [], [], []
    for part in range(FEATURE_PARTS):
        parts = backward(
            carry[0],
            where,
            pieces,
            weights,
            flags,
            starts[1],
            tile,
            part,
            n_col,
            parts[:1],
        )
        total, arrived = sum_planes(parts, n_col, part < FEATURE_PARTS - 1, arrived)
        input_grad.append(total)
    return jnp.concatenate(hidden, axis=1), jnp.concatenate(input_grad, axis=1)


def solution(mesh):
    placed = (
        P("col", "row"),
        P("row", "col"),
        P("row", "col"),
        P("row", "col"),
        P("row", "col"),
        P("row", "col"),
    )
    return jax.shard_map(
        functools.partial(shards, Cube(mesh.shape["row"]), mesh.shape["col"]),
        mesh=mesh,
        in_specs=placed,
        out_specs=(P("row", "col"), P("col", "row")),
        check_vma=False,
    )
```

```python
import functools

import jax
import jax.numpy as jnp
import numpy as np
from jax import lax
from jax.experimental import pallas as pl
from jax.experimental.pallas import tpu as pltpu
from jax.sharding import PartitionSpec as P

BLOCK = 128
FORWARD = (2, 3, 4, 4)
BACKWARD = (5, 8)
FEATURE_PARTS = 2
VMEM_BYTES = 36 * 1024 * 1024
ANY = pl.BlockSpec(memory_space=pl.ANY)
COST = pl.CostEstimate(flops=1, bytes_accessed=1, transcendentals=0)


def masked(w_ref, f_ref):
    rows, columns = w_ref.shape
    flags = f_ref[...].reshape(rows // BLOCK, 1, columns)
    return (w_ref[...].reshape(rows // BLOCK, BLOCK, columns) * flags).reshape(rows, columns)


def then(array, *others):
    return lax.optimization_barrier((array, *others))[0]


class Cube:
    def __init__(self, size):
        self.size = size
        self.half = size // 2
        rising = [1 << b for b in range(1, size.bit_length() - 1)]
        self.dims = (rising, rising[::-1])

    def offset(self, parity, slot):
        dims = self.dims[parity]
        digits = [slot >> (len(dims) - 1 - i) & 1 for i in range(len(dims))]
        return int(np.bitwise_xor.reduce([0] + [d for d, on in zip(dims, digits) if on]))

    def owner(self, me, slot):
        if slot >= self.half:
            me, slot = me ^ 1, slot - self.half
        return me ^ self.offset(me & 1, slot)

    def step(self, array, i):
        perm = [(r, r ^ self.dims[r & 1][i]) for r in range(self.size)]
        return lax.ppermute(array, "row", perm)

    def sibling(self, array):
        return lax.ppermute(array, "row", [(r, r ^ 1) for r in range(self.size)])


def places(cube, n_col):
    ratio = cube.size // n_col
    table = np.zeros((cube.size, n_col, cube.size), np.int32)
    for me in range(cube.size):
        for z in range(n_col):
            for slot in range(cube.size):
                d = cube.owner(me, slot)
                table[me, z, slot] = ratio * ((d // ratio) ^ z) + d % ratio
    return table


def copy_all(copies):
    for copy in copies:
        copy.start()
    for copy in copies:
        copy.wait()


def forward_kernel(n_x, n_after, slots, *refs):
    x_refs, refs = refs[:n_x], refs[n_x:]
    wg_ref, wu_ref, fg_ref, fu_ref = refs[:4]
    keep_ref, send_ref, x_all, sem = refs[4 + n_after :]
    half = keep_ref.shape[1]
    shares = slots.shape[0]
    share = 2 * half // shares
    ratio = shares // n_x

    @pl.when(pl.program_id(0) == 0)
    def _():
        copies = []
        for k in range(n_x):
            for c in range(ratio):
                place = k * ratio + c
                row = pl.multiple_of(slots[place] * share, share)
                copies.append(
                    pltpu.make_async_copy(
                        x_refs[k].at[pl.ds(c * share, share), :],
                        x_all.at[pl.ds(row, share), :],
                        sem.at[place],
                    )
                )
        copy_all(copies)

    for n, (w_ref, f_ref) in enumerate(((wg_ref, fg_ref), (wu_ref, fu_ref))):
        out = jnp.dot(x_all[...], masked(w_ref, f_ref), preferred_element_type=jnp.float32)
        out = out.astype(jnp.bfloat16)
        keep_ref[n] = out[:half]
        send_ref[n] = out[half:]


def forward(slots, xs, weights, flags, first, tiles, tile, after):
    depth = weights[0].shape[0]
    rows = len(xs) * xs[0].shape[0]
    w_spec = pl.BlockSpec((depth, tile), lambda i, s: (0, first + i))
    f_spec = pl.BlockSpec((*flags[0].shape[:2], tile), lambda i, s: (0, 0, first + i))
    o_spec = pl.BlockSpec((2, rows // 2, tile), lambda i, s: (0, 0, i))
    out = jax.ShapeDtypeStruct((2, rows // 2, tiles * tile), jnp.bfloat16)
    return pl.pallas_call(
        functools.partial(forward_kernel, len(xs), len(after)),
        grid_spec=pltpu.PrefetchScalarGridSpec(
            num_scalar_prefetch=1,
            grid=(tiles,),
            in_specs=[ANY] * len(xs) + [w_spec] * 2 + [f_spec] * 2 + [ANY] * len(after),
            out_specs=[o_spec, o_spec],
            scratch_shapes=[
                pltpu.VMEM((rows, depth), jnp.bfloat16),
                pltpu.SemaphoreType.DMA((slots.shape[0],)),
            ],
        ),
        out_shape=[out, out],
        compiler_params=pltpu.CompilerParams(vmem_limit_bytes=VMEM_BYTES),
        cost_estimate=pl.CostEstimate(
            flops=8 * rows * depth * tiles * tile,
            bytes_accessed=4 * depth * tiles * tile,
            transcendentals=0,
        ),
    )(slots, *xs, *weights, *flags, *after)


def derivatives_kernel(first, layout, n_terms, *refs):
    sources, cot_ref = refs[: len(layout) * n_terms], refs[len(layout) * n_terms]
    h_ref, g_ref = refs[-4 - n_terms : -2 - n_terms]
    held = refs[-2 - n_terms : -2]
    cot, sem = refs[-2:]
    share, columns = h_ref.shape
    copies = []
    for m, (source, place, width) in enumerate(layout):
        for n in range(n_terms):
            copies.append(
                pltpu.make_async_copy(
                    sources[m * n_terms + n].at[:, pl.ds(0, share), pl.ds(source, width)],
                    held[n].at[:, :, pl.ds(place, width)],
                    sem.at[m * n_terms + n],
                )
            )
    copies.append(
        pltpu.make_async_copy(
            cot_ref.at[:, pl.ds(first, columns)], cot, sem.at[len(layout) * n_terms]
        )
    )
    copy_all(copies)
    step = 256
    for c in range(0, columns, step):
        at = slice(c, c + step)
        gate_sum = sum(wide(v[0, :, at]) for v in held)
        up_sum = sum(wide(v[1, :, at]) for v in held)
        cotangent = wide(cot[:, at])
        sigmoid_gate = jax.nn.sigmoid(gate_sum)
        activated = gate_sum * sigmoid_gate
        h_ref[:, at] = (activated * up_sum).astype(jnp.bfloat16)
        g_ref[0, :, at] = (
            cotangent * up_sum * sigmoid_gate * (1.0 + gate_sum * (1.0 - sigmoid_gate))
        ).astype(jnp.bfloat16)
        g_ref[1, :, at] = (cotangent * activated).astype(jnp.bfloat16)


def derivatives(layout, terms, cotangent, first, columns, after):
    share = cotangent.shape[0]
    n_terms = len(terms[0])
    return pl.pallas_call(
        functools.partial(derivatives_kernel, first, layout, n_terms),
        in_specs=[ANY] * (len(layout) * n_terms + 1 + len(after)),
        out_specs=[pl.BlockSpec(memory_space=pltpu.VMEM)] * 2,
        out_shape=[
            jax.ShapeDtypeStruct((share, columns), jnp.bfloat16),
            jax.ShapeDtypeStruct((2, share, columns), jnp.bfloat16),
        ],
        scratch_shapes=[pltpu.VMEM((2, share, columns), jnp.bfloat16)] * n_terms
        + [
            pltpu.VMEM((share, columns), jnp.bfloat16),
            pltpu.SemaphoreType.DMA((len(layout) * n_terms + 1,)),
        ],
        compiler_params=pltpu.CompilerParams(vmem_limit_bytes=VMEM_BYTES),
        cost_estimate=COST,
    )(*sum(terms, []), cotangent, *after)


def backward_kernel(n_out, steps, chained, n_after, part, where, *refs):
    n_slots = where.shape[0]
    g_refs, refs = refs[:n_slots], refs[n_slots:]
    (wg_ref, wu_ref, fg_ref, fu_ref), refs = refs[:4], refs[4:]
    if chained:
        carry_ref, refs = refs[0], refs[1:]
    refs = refs[n_after:]
    o_refs = refs[:n_out]
    g_all, acc, both, sem = refs[n_out:]
    i = pl.program_id(0)
    tile = wg_ref.shape[1]
    depth, rows = acc.shape
    share = rows // n_slots

    @pl.when(i == 0)
    def _():
        copies = []
        for slot in range(n_slots):
            row = pl.multiple_of(where[slot] * share, share)
            copies.append(
                pltpu.make_async_copy(
                    g_refs[slot], g_all.at[:, pl.ds(row, share), :], sem.at[slot]
                )
            )
        if chained:
            copies.append(
                pltpu.make_async_copy(
                    carry_ref.at[pl.ds(part * depth, depth), :], acc, sem.at[n_slots]
                )
            )
        else:
            acc[...] = jnp.zeros_like(acc)
        copy_all(copies)

    columns = pl.ds(pl.multiple_of(i * tile, tile), tile)
    both[:, :tile] = masked(wg_ref, fg_ref)
    both[:, tile:] = masked(wu_ref, fu_ref)
    acc[...] += lax.dot_general(
        both[...],
        jnp.concatenate([g_all[0, :, columns], g_all[1, :, columns]], axis=1),
        (((1,), (1,)), ((), ())),
        preferred_element_type=jnp.float32,
    )

    @pl.when(i == steps - 1)
    def _():
        if n_out == 1:
            copy_all([pltpu.make_async_copy(acc, o_refs[0], sem.at[0])])
        else:
            for k in range(n_out):
                size = rows // n_out
                o_refs[k][...] = acc[:, k * size : (k + 1) * size].T.astype(jnp.bfloat16)


def backward(carry, where, pieces, weights, flags, first, tile, part, planes, after):
    n_slots = where.shape[0]
    width = pieces[0].shape[2]
    rows = pieces[0].shape[1] * n_slots
    depth = weights[0].shape[0]
    f_parts = FEATURE_PARTS
    if part is not None:
        depth, f_parts = depth // FEATURE_PARTS, 1
    row = part or 0
    tiles = width // tile
    w_spec = pl.BlockSpec((depth, tile), lambda i, s: (row, first + i))
    f_spec = pl.BlockSpec(
        (f_parts, flags[0].shape[1], tile), lambda i, s: (row, 0, first + i)
    )
    if planes:
        out_specs = [pl.BlockSpec((rows // planes, depth), lambda i, s: (0, 0))] * planes
        out_shape = [jax.ShapeDtypeStruct((rows // planes, depth), jnp.bfloat16)] * planes
    else:
        out_specs = [ANY]
        out_shape = [jax.ShapeDtypeStruct((depth, rows), jnp.float32)]
    chained = carry is not None
    return pl.pallas_call(
        functools.partial(
            backward_kernel, len(out_shape), tiles, chained, len(after), part
        ),
        grid_spec=pltpu.PrefetchScalarGridSpec(
            num_scalar_prefetch=1,
            grid=(tiles,),
            in_specs=[ANY] * n_slots + [w_spec] * 2 + [f_spec] * 2 + [ANY] * (chained + len(after)),
            out_specs=out_specs,
            scratch_shapes=[
                pltpu.VMEM((2, rows, width), jnp.bfloat16),
                pltpu.VMEM((depth, rows), jnp.float32),
                pltpu.VMEM((depth, 2 * tile), jnp.bfloat16),
                pltpu.SemaphoreType.DMA((n_slots + 1,)),
            ],
        ),
        out_shape=out_shape,
        compiler_params=pltpu.CompilerParams(vmem_limit_bytes=VMEM_BYTES),
        cost_estimate=pl.CostEstimate(
            flops=6 * rows * depth * width,
            bytes_accessed=4 * depth * width,
            transcendentals=0,
        ),
    )(where, *pieces, *weights, *flags, *((carry,) if chained else ()), *after)


def wide(array):
    return array.astype(jnp.float32)


class ReduceScatter:
    def __init__(self, cube, keep, send):
        self.cube = cube
        self.terms = [keep, cube.sibling(send)]
        self.rows = keep.shape[1]

    def exchange(self, i, after):
        self.rows //= 2
        self.terms[0] = then(self.terms[0], *after)
        rows = self.rows
        moved = sum(wide(t[:, rows : 2 * rows]) for t in self.terms).astype(jnp.bfloat16)
        self.terms.append(self.cube.step(moved, i))
        if i == 0:
            self.first = self.terms[-1]
        return moved


class AllGather:
    def __init__(self, cube, own, *after):
        self.cube = cube
        n_dims = len(cube.dims[0])
        own = then(own, *after)
        self.pieces = [own] + [cube.step(own, n_dims - 1 - i) for i in range(n_dims)]

    def finish(self, *after):
        cube = self.cube
        n_dims = len(cube.dims[0])
        pieces = {0: self.pieces[0]}
        for i in range(n_dims):
            pieces[1 << i] = self.pieces[1 + i]
        pieces = {slot: then(p, *after) for slot, p in pieces.items()}
        for slot in range(1, cube.half):
            if slot not in pieces:
                low = slot & -slot
                pieces[slot] = cube.step(pieces[slot ^ low], n_dims - low.bit_length())
        pieces = [pieces[slot] for slot in range(cube.half)]
        return pieces + [cube.sibling(p) for p in pieces]


def flip(array, bit, size):
    return lax.ppermute(array, "col", [(z, z ^ bit) for z in range(size)])


def gather_planes(x, n_col):
    xs = [x]
    for k in range(1, n_col):
        low = k & -k
        xs.append(flip(xs[k ^ low], low, n_col))
    return xs


def sum_planes(parts, n_col, direct, after):
    terms = [wide(p) for p in parts]
    arrived = list(after)
    for k in range(n_col - 1, 0, -1):
        low = k if direct else k & -k
        sent = terms[k].astype(jnp.bfloat16)
        if not direct:
            sent = then(sent, *arrived)
        moved = flip(sent, low, n_col)
        if direct or low != k:
            arrived.append(moved)
        terms[k ^ low] = terms[k ^ low] + wide(moved)
    return terms[0].astype(jnp.bfloat16), arrived


def shards(cube, n_col, inputs, gate_weight, up_weight, gate_pattern, up_pattern, cotangent):
    depth, local_hidden = gate_weight.shape
    share = cotangent.shape[0]
    tile = local_hidden // sum(BACKWARD)
    weights = (gate_weight, up_weight)
    flags = [
        jnp.repeat(p.astype(jnp.bfloat16), BLOCK, axis=1).reshape(
            FEATURE_PARTS, -1, local_hidden
        )
        for p in (gate_pattern, up_pattern)
    ]
    table = places(cube, n_col)
    row, col = lax.axis_index("row"), lax.axis_index("col")
    where = jnp.asarray(table)[row, col]
    slots = jnp.asarray(np.argsort(table, axis=-1).astype(np.int32))[row, col]

    xs = gather_planes(inputs, n_col)
    units = list(zip(np.cumsum((0,) + FORWARD).tolist(), FORWARD))
    sums, after, moved = [], {}, []
    for n, (first, tiles) in enumerate(units):
        keep, send = forward(
            slots, xs, weights, flags, first, tiles, tile, after.pop(n, [])
        )
        sums.append(ReduceScatter(cube, keep, send))
        after.setdefault(n + 1, []).append(keep)
        moved.append([])
        for i in range(len(cube.dims[0])):
            before = sums[n - 2].terms[-1:] if i == 0 and n > 2 else []
            moved[n].append(sums[n].exchange(i, before))
            after.setdefault(n + 2 + i, []).append(moved[n][-1])
    first_moved = [m[0] for m in moved]

    hidden, gathers, owns = [], [], []
    starts = [sum(BACKWARD[:n]) for n in range(len(BACKWARD))]
    for first, tiles in zip(starts, BACKWARD):
        layout, terms = [], []
        for (start, width), unit in zip(units, sums):
            low, high = max(first, start), min(first + tiles, start + width)
            if low < high:
                layout.append(((low - start) * tile, (low - first) * tile, (high - low) * tile))
                terms.append(unit.terms)
        h, own = derivatives(
            layout, terms, cotangent, first * tile, tiles * tile, owns[-1:] or first_moved
        )
        hidden.append(h)
        owns.append(own)
        gathers.append(AllGather(cube, own))
    carry = backward(
        None, where, gathers[0].finish(), weights, flags, 0, tile, None, 0, owns[1:]
    )
    pieces = gathers[1].finish(*carry)
    input_grad, arrived, parts = [], [], []
    for part in range(FEATURE_PARTS):
        parts = backward(
            carry[0],
            where,
            pieces,
            weights,
            flags,
            starts[1],
            tile,
            part,
            n_col,
            parts[:1],
        )
        total, arrived = sum_planes(parts, n_col, part < FEATURE_PARTS - 1, arrived)
        input_grad.append(total)
    return jnp.concatenate(hidden, axis=1), jnp.concatenate(input_grad, axis=1)


def solution(mesh):
    placed = (
        P("col", "row"),
        P("row", "col"),
        P("row", "col"),
        P("row", "col"),
        P("row", "col"),
        P("row", "col"),
    )
    return jax.shard_map(
        functools.partial(shards, Cube(mesh.shape["row"]), mesh.shape["col"]),
        mesh=mesh,
        in_specs=placed,
        out_specs=(P("row", "col"), P("col", "row")),
        check_vma=False,
    )
```
